256 devices in a mesh: row: 8 (over z), col: 32 (over y, x, core).
Axes of the slice: x: 4, y: 4, z: 8, core: 2. Of those that a mesh axis runs over, the one named last changes fastest.
Arguments:
- positions: float32 [3, 6291456], P(None, ('row', 'col')), may hold values from -10 to 10
- moments: float32 [3, 6291456], P(None, ('row', 'col')), may hold values from -6 to 6
- near_list: int32 [49152, 2], P(('row', 'col')), may hold values from 0 to 575
- far_list: int32 [49152, 16], P(('row', 'col')), may hold values from 0 to 1023
- let_rows: int32 [256, 8, 128], P(('row', 'col')), may hold values from 0 to 191
Outputs:
- near_field: float32 [3, 6291456], P(None, ('row', 'col'))
- let_field: float32 [3, 6291456], P(None, ('row', 'col'))
- top_field: float32 [3, 6291456], P(None, ('row', 'col'))
The draws below stay inside these ranges and needn't reach their ends.
All inputs are finite; a program needn't handle non-finite values.
Results may differ from the reference program's by a relative error of at most 0.0003.
Values sent between devices are 32-bit elements; how exact they have to be, the bound alone decides.
A program may use at most 64 MiB of HBM per device.

```python
import math
import jax
import jax.numpy as jnp
from jax import lax

CELL = 128
CELLS_DEV = 192
R = 128
NEAR_K = 2
FAR_K = 16
TOP_DEV = 2
NCELLS = 49152
N = 6291456
BITS = 8
N_COL = 32
DEVICES = 256


def draw_positions(key, part):
    key = jax.random.fold_in(key, 11)
    cell_key, jitter_key = jax.random.split(key)
    devices = jnp.arange(DEVICES, dtype=jnp.int32)
    centres = jnp.zeros((3, DEVICES), jnp.float32)
    for level in range(12):
        bit_value = (devices // 2 ** level % 2).astype(jnp.float32)
        heading = jnp.array([0.7 * math.cos(2.4 * level), 0.7 * math.sin(2.4 * level), 0.5 * math.cos(1.7 * level)], jnp.float32)
        centres = centres + heading[:, None] * bit_value[None, :]
    cell_centres = jnp.repeat(centres, CELLS_DEV, axis=1) + jax.random.uniform(cell_key, (3, NCELLS), jnp.float32, -0.5, 0.5)
    return jnp.repeat(cell_centres, CELL, axis=1) + jax.random.uniform(jitter_key, (3, N), jnp.float32, -0.6, 0.6)


def set_ends(values, stream_key, least, top_value):
    shape = values.shape
    spot = [jax.random.randint(jax.random.fold_in(stream_key, axis), (), 0, shape[axis]) for axis in range(len(shape))]
    values = values.at[tuple(spot)].set(least)
    longest = shape.index(max(shape))
    spot[longest] = (spot[longest] + 1) % shape[longest]
    return values.at[tuple(spot)].set(top_value)


def shard_levels(rng, shape, shards, least, largest):
    factor_of = 1.0
    for position, shards_of in shards:
        draws = jax.random.uniform(jax.random.fold_in(jax.random.fold_in(rng, 6), position), (shards_of,), jnp.float32, least / len(shards), largest / len(shards))
        factor_of = factor_of * jnp.repeat(jnp.exp(draws), shape[position] // shards_of).reshape((-1,) + (1,) * (len(shape) - 1 - position))
    return factor_of


def noise(own_key, extent, width, most, cuts=(), kind=jnp.bfloat16):
    level = shard_levels(own_key, extent, cuts, -0.22, 0.18) if cuts else 1.0
    values = jax.random.normal(own_key, extent, jnp.float32) * width * level
    return jnp.minimum(jnp.maximum(values, -most), most).astype(kind)


def setup_inputs(seed: int = 0) -> dict:
    arg_keys = jax.random.split(jax.random.key(seed), 6)
    return {
        "positions": draw_positions(jax.random.fold_in(arg_keys[5], 71), 0),
        "moments": noise(arg_keys[1], (3, N), 1.0, 6.0, ((1, 256),), jnp.float32),
        "near_list": set_ends(jax.random.randint(arg_keys[2], (NCELLS, NEAR_K), 0, 3 * CELLS_DEV), jax.random.fold_in(arg_keys[2], 1), 0, (3 * CELLS_DEV) - 1).astype(jnp.int32),
        "far_list": set_ends(jax.random.randint(arg_keys[3], (NCELLS, FAR_K), 0, BITS * R), jax.random.fold_in(arg_keys[3], 1), 0, (BITS * R) - 1).astype(jnp.int32),
        "let_rows": set_ends(jax.random.randint(arg_keys[4], (DEVICES, BITS, R), 0, CELLS_DEV), jax.random.fold_in(arg_keys[4], 1), 0, CELLS_DEV - 1).astype(jnp.int32),
    }


SOFTEN = 0.09
COUPLING = 0.004

def powers(offset):
    square = offset[0] * offset[0] + offset[1] * offset[1] + offset[2] * offset[2] + SOFTEN
    inverse_two = 1.0 / square
    inverse_three = inverse_two * jnp.sqrt(inverse_two)
    inverse_five = inverse_three * inverse_two
    return (inverse_two, inverse_three, inverse_five)

def dipole(offset, moment):
    inverse_two, inverse_three, inverse_five = powers(offset)
    projected = offset[0] * moment[0] + offset[1] * moment[1] + offset[2] * moment[2]
    return [3.0 * offset[component] * projected * inverse_five - moment[component] * inverse_three for component in range(3)]

def first_moment(table, first_axis, second_axis):
    return table[6 + 3 * first_axis + second_axis]

def expansion(offset, table):
    inverse_two, inverse_three, inverse_five = powers(offset)
    inverse_seven = inverse_five * inverse_two
    totals = [table[3 + component] for component in range(3)]
    projected = offset[0] * totals[0] + offset[1] * totals[1] + offset[2] * totals[2]
    left_product = [sum((first_moment(table, first_axis, second_axis) * offset[second_axis] for second_axis in range(3))) for first_axis in range(3)]
    right_product = [sum((first_moment(table, first_axis, second_axis) * offset[first_axis] for first_axis in range(3))) for second_axis in range(3)]
    trace_sum = first_moment(table, 0, 0) + first_moment(table, 1, 1) + first_moment(table, 2, 2)
    curvature = left_product[0] * offset[0] + left_product[1] * offset[1] + left_product[2] * offset[2]
    return [3.0 * offset[component] * projected * inverse_five - totals[component] * inverse_three - 3.0 * inverse_five * (left_product[component] + trace_sum * offset[component] + right_product[component]) + 15.0 * curvature * offset[component] * inverse_seven for component in range(3)]

def moments_of(place, moment):
    centre = lax.optimization_barrier(jnp.sum(place, axis=2)) / place.shape[2]
    spread = place - centre[:, :, None]
    totals = lax.optimization_barrier(jnp.sum(moment, axis=2))
    firsts = [lax.optimization_barrier(jnp.sum(spread[first_axis] * moment[second_axis], axis=1)) for first_axis in range(3) for second_axis in range(3)]
    return jnp.concatenate([centre, totals, jnp.stack(firsts)], axis=0)

def near_cell(target, listed, owner, source_place, source_moment):
    place = jnp.take(source_place, listed, axis=1)
    moment = jnp.take(source_moment, listed, axis=1)
    offset = [target[component][None, :, None] - place[component][:, None, :] for component in range(3)]
    fields = dipole(offset, [moment[component][:, None, :] for component in range(3)])
    slot_ids = jnp.arange(target.shape[1], dtype=jnp.int32)
    self_pair = (listed[:, None, None] == owner) & (slot_ids[:, None] == slot_ids[None, :])[None, :, :]
    return jnp.stack([lax.optimization_barrier(jnp.sum(jnp.where(self_pair, 0.0, component_field), axis=(0, 2))) for component_field in fields])

def near_all(target_place, source_place, source_moment, near_rows):
    cell_count = target_place.shape[1]
    cell_width = target_place.shape[2]
    group_size = math.gcd(cell_count, 16)
    owners = (cell_count + jnp.arange(cell_count, dtype=jnp.int32)).reshape(cell_count // group_size, group_size)
    targets = jnp.moveaxis(target_place, 1, 0).reshape(cell_count // group_size, group_size, 3, cell_width)
    listed = near_rows.reshape(cell_count // group_size, group_size, near_rows.shape[1])

    def one_group(packed):
        return jax.vmap(near_cell, in_axes=(0, 0, 0, None, None))(packed[0], packed[1], packed[2], source_place, source_moment)
    fields = lax.map(one_group, (targets, listed, owners))
    return jnp.moveaxis(fields.reshape(cell_count, 3, cell_width), 1, 0).reshape(3, cell_count * cell_width)

def let_field_of(target_place, listed):
    offset = [target_place[component][:, None, :] - listed[component][:, :, None] for component in range(3)]
    fields = expansion(offset, [listed[entry][:, :, None] for entry in range(15)])
    return jnp.stack([lax.optimization_barrier(jnp.sum(component_field, axis=1)) for component_field in fields]).reshape(3, -1)

def top_field_of(place, top_cells, keep_mask):
    offset = [place[component][None, :] - top_cells[component][:, None] for component in range(3)]
    fields = expansion(offset, [top_cells[entry][:, None] for entry in range(15)])
    return jnp.stack([lax.optimization_barrier(jnp.sum(component_field * keep_mask[:, None], axis=0)) for component_field in fields])

def reference(positions, moments, near_list, far_list, let_rows):
    per_device = CELL * CELLS_DEV
    leaf_table = moments_of(positions.reshape(3, NCELLS, CELL), moments.reshape(3, NCELLS, CELL))
    top_table = moments_of(positions.reshape(3, DEVICES * TOP_DEV, per_device // TOP_DEV), moments.reshape(3, DEVICES * TOP_DEV, per_device // TOP_DEV))
    padded_place = jnp.pad(positions, ((0, 0), (per_device, per_device)))
    padded_moment = jnp.pad(moments, ((0, 0), (per_device, per_device)))

    def device_fields(device):
        first_index = device * per_device
        own_place = lax.dynamic_slice_in_dim(positions, first_index, per_device, 1)
        source_place = lax.dynamic_slice_in_dim(padded_place, first_index, 3 * per_device, 1).reshape(3, 3 * CELLS_DEV, CELL)
        source_moment = lax.dynamic_slice_in_dim(padded_moment, first_index, 3 * per_device, 1).reshape(3, 3 * CELLS_DEV, CELL)
        near_rows = lax.dynamic_slice_in_dim(near_list, device * CELLS_DEV, CELLS_DEV, 0)
        near_part = near_all(own_place.reshape(3, CELLS_DEV, CELL), source_place, source_moment, near_rows)
        pieces = []
        for section_bit in range(BITS):
            bit_value = device // 2 ** section_bit % 2
            partner = (device + 2 ** section_bit * (1 - 2 * bit_value)).astype(jnp.int32)
            chosen = lax.dynamic_index_in_dim(let_rows, partner, 0, keepdims=False)[section_bit]
            pieces.append(jnp.take(leaf_table, partner * CELLS_DEV + chosen, axis=1))
        let_table = jnp.concatenate(pieces, axis=1)
        far_rows = lax.dynamic_slice_in_dim(far_list, device * CELLS_DEV, CELLS_DEV, 0)
        listed = jnp.take(let_table, far_rows, axis=1)
        remote = let_field_of(own_place.reshape(3, CELLS_DEV, CELL), listed)
        group_first = (device // N_COL * N_COL * TOP_DEV).astype(jnp.int32)
        top_cells = lax.dynamic_slice_in_dim(top_table, group_first, N_COL * TOP_DEV, 1)
        keep_mask = (jnp.arange(N_COL * TOP_DEV, dtype=jnp.int32) // TOP_DEV != device % N_COL).astype(jnp.float32)
        coarse = top_field_of(own_place, top_cells, keep_mask)
        return (COUPLING * near_part, COUPLING * remote, COUPLING * coarse)
    near_part, remote, coarse = lax.map(device_fields, jnp.arange(DEVICES, dtype=jnp.int32))

    def assemble(stacked):
        return jnp.moveaxis(stacked, 1, 0).reshape(3, N)
    return (assemble(near_part), assemble(remote), assemble(coarse))
```

```python
import functools

import jax
import jax.numpy as jnp
from jax import lax
from jax.experimental import pallas as pl
from jax.experimental.pallas import tpu as pltpu
from jax.sharding import PartitionSpec as P

CELL = 128
SOFTEN = 0.09
COUPLING = 0.004
F32 = jnp.float32
BF16 = jnp.bfloat16
MESH = pl.DeviceIdType.MESH
HIGHEST = lax.Precision.HIGHEST
VMEM_LIMIT = 58 * 1024 * 1024
SIX = ((0, 0), (0, 1), (0, 2), (1, 1), (1, 2), (2, 2))
NEAR_K = 48
FAR_K = 64
OUT_K = 16
NEAR_S = 56
FAR_S = 72
COEF_S = 56
TOP_UNROLL = 24
NEAR_UNROLL = 16


def split3(value):
    high = value.astype(BF16).astype(F32)
    rest = value - high
    middle = rest.astype(BF16).astype(F32)
    return high, middle, rest - middle


def split2(value):
    high = value.astype(BF16)
    return high, (value - high.astype(F32)).astype(BF16)


def source_pairing(parts):
    return [parts[0], parts[1], parts[2], parts[0], parts[1], parts[0]]


def target_pairing(parts):
    return [parts[0], parts[0], parts[0], parts[1], parts[1], parts[2]]


def expansion_coefficients(table):
    c = table[0:3]
    m = [COUPLING * entry for entry in table[3:6]]
    q = [[COUPLING * table[6 + 3 * j + i] for i in range(3)] for j in range(3)]
    g = [[q[j][i] + q[i][j] for i in range(3)] for j in range(3)]
    t = q[0][0] + q[1][1] + q[2][2]
    gc = [g[i][0] * c[0] + g[i][1] * c[1] + g[i][2] * c[2] for i in range(3)]
    zero = jnp.zeros_like(c[0])
    one = jnp.ones_like(c[0])
    square = (
        c[0] * c[0] + c[1] * c[1] + c[2] * c[2] + SOFTEN,
        [-2.0 * c[i] for i in range(3)],
        [one if i == j else zero for i, j in SIX],
    )
    first = (
        -3.0 * (c[0] * m[0] + c[1] * m[1] + c[2] * m[2] + t),
        [3.0 * m[i] for i in range(3)],
        None,
    )
    second = (
        7.5 * (c[0] * gc[0] + c[1] * gc[1] + c[2] * gc[2]),
        [-15.0 * gc[i] for i in range(3)],
        [(7.5 if i == j else 15.0) * g[i][j] for i, j in SIX],
    )
    outputs = [one] + list(c) + m + [3.0 * g[i][j] for i, j in SIX] + [3.0 * gc[i] for i in range(3)]
    return square, first, second, outputs


def source_rows(form, zero):
    const, linear, quadratic = form
    rows = list(split3(const))
    for entry in linear:
        rows += source_pairing(split3(entry))
    if quadratic is None:
        rows += [zero] * 36
    else:
        for entry in quadratic:
            rows += source_pairing(split3(entry))
    return rows + [zero] * (FAR_K - len(rows))


def target_rows(x):
    one = jnp.ones_like(x[0])
    rows = [one, one, one]
    for entry in x:
        rows += target_pairing(split3(entry))
    for i, j in SIX:
        rows += target_pairing(split3(x[i] * x[j]))
    return rows + [jnp.zeros_like(one)] * (FAR_K - len(rows))


def weights_of(square, first, second):
    inverse = lax.rsqrt(square)
    two = inverse * inverse
    three = two * inverse
    five = three * two
    return five * (first + second * two), three, five


def expansion_fields(x, sums):
    g = {}
    for place, (i, j) in enumerate(SIX):
        g[i, j] = g[j, i] = sums[7 + place]
    return [
        x[i] * sums[0]
        - sums[1 + i]
        - sums[4 + i]
        - (g[i, 0] * x[0] + g[i, 1] * x[1] + g[i, 2] * x[2])
        + sums[13 + i]
        for i in range(3)
    ]


def pitch_of(cells):
    return cells + 8 * (1 - cells // 8 % 2)


def rows8(start):
    return pl.ds(pl.multiple_of(start, 8), 8)


def lanes(block):
    return pl.ds(pl.multiple_of(block * CELL, CELL), CELL)


def store_rows(ref, rows, first, stride):
    for place, value in enumerate(rows):
        ref[pl.ds(first * stride + place, 8, stride=stride), :] = value


def own_offsets(planes_ref, centre_ref, cells, start):
    return [
        planes_ref[rows8(i * pitch_of(cells) + start), :] - centre_ref[i : i + 1, :] for i in range(3)
    ]


def planes_to_output(planes_ref, out_ref, cells):
    def step(b, carry):
        out_ref[:, lanes(b)] = planes_ref[pl.ds(b, 3, stride=pitch_of(cells)), :]
        return carry

    lax.fori_loop(0, cells, step, 0, unroll=8)


def leaf_sections(cells, place, moment, let_rows_ref, let_ref):
    ones = jnp.ones((CELL, CELL), F32)
    eight = jnp.ones((8, CELL), F32)
    padding = jnp.zeros((256 - cells, CELL), F32)

    def lane_sums(plane):
        return lax.dot_general(
            eight,
            jnp.concatenate([plane, padding], axis=0),
            (((1,), (1,)), ((), ())),
            precision=HIGHEST,
            preferred_element_type=F32,
        )

    spread = [
        entry - jnp.dot(entry, ones, precision=HIGHEST, preferred_element_type=F32) * (1.0 / CELL)
        for entry in place
    ]
    leaf = [lane_sums(entry) * (1.0 / CELL) for entry in place]
    leaf += [lane_sums(entry) for entry in moment]
    leaf += [lane_sums(spread[j] * moment[i]) for j in range(3) for i in range(3)]
    chosen = let_rows_ref[0]
    low = jnp.bitwise_and(chosen, CELL - 1)
    upper = chosen >= CELL
    for entry in range(15):
        let_ref[:, entry, :] = jnp.where(
            upper,
            jnp.take_along_axis(leaf[entry][:, CELL:], low, axis=1),
            jnp.take_along_axis(leaf[entry][:, :CELL], low, axis=1),
        )
    let_ref[:, 15, :] = jnp.zeros((8, CELL), F32)


def top_tables(cells, place, moment, top_ref, centre_ref):
    half = cells // 2
    sublane = lax.broadcasted_iota(jnp.int32, (8, CELL), 0)
    lane = lax.broadcasted_iota(jnp.int32, (8, CELL), 1)
    tile = jnp.zeros((8, CELL), F32)
    centres = []

    def total(plane):
        column = jnp.sum(plane, axis=0, keepdims=True)
        return jnp.sum(column, axis=1, keepdims=True)

    for top in range(2):
        part = slice(top * half, (top + 1) * half)
        centre = [total(place[i][part]) * (1.0 / (half * CELL)) for i in range(3)]
        entries = list(centre) + [total(moment[i][part]) for i in range(3)]
        for j in range(3):
            offset = place[j][part] - centre[j]
            entries += [total(offset * moment[i][part]) for i in range(3)]
        for entry in range(15):
            tile = jnp.where((sublane == top) & (lane == entry), entries[entry], tile)
        centres.append(centre)
    top_ref[...] = tile
    middle = jnp.zeros((8, CELL), F32)
    for i in range(3):
        middle = jnp.where(sublane == i, 0.5 * (centres[0][i] + centres[1][i]), middle)
    centre_ref[...] = middle


def first_kernel(
    cells,
    n_row,
    n_col,
    pos_ref,
    mom_ref,
    let_rows_ref,
    planes_ref,
    before_ref,
    after_ref,
    let_in,
    centre_ref,
    out_ref,
    let_ref,
    top_ref,
    top_in,
    feats,
    forms_rows,
    forms,
    coeffs,
    sums,
    field,
    side_send,
    side_recv,
    let_send,
    let_recv,
    top_send,
    top_recv,
):
    row = lax.axis_index("row")
    col = lax.axis_index("col")
    device = row * n_col + col
    devices = n_row * n_col
    col_bits = n_col.bit_length() - 1
    row_bits = n_row.bit_length() - 1
    sources = 2 * n_col
    pitch = pitch_of(cells)

    def flip(value, bit):
        return value + (1 << bit) * (1 - 2 * lax.rem(value // (1 << bit), 2))

    def place_of(index):
        return (index // n_col, lax.rem(index, n_col))

    following = place_of(lax.rem(device + 1, devices))
    preceding = place_of(lax.rem(device + devices - 1, devices))

    barrier = pltpu.get_barrier_semaphore()

    def greet(step, carry):
        other = lax.rem(col + step, n_col)
        pl.semaphore_signal(barrier, inc=1, device_id=(row, other), device_id_type=MESH)
        return carry

    lax.fori_loop(1, n_col, greet, 0)
    for bit in range(row_bits):
        pl.semaphore_signal(barrier, inc=1, device_id=(flip(row, bit), col), device_id_type=MESH)

    @pl.when(col == 0)
    def _():
        pl.semaphore_signal(barrier, inc=1, device_id=preceding, device_id_type=MESH)

    @pl.when(col == n_col - 1)
    def _():
        pl.semaphore_signal(barrier, inc=1, device_id=following, device_id_type=MESH)

    def to_planes(b, carry):
        planes_ref[pl.ds(b, 3, stride=pitch), :] = pos_ref[:, lanes(b)]
        planes_ref[pl.ds(3 * pitch + b, 3, stride=pitch), :] = mom_ref[:, lanes(b)]
        return carry

    lax.fori_loop(0, cells, to_planes, 0, unroll=8)
    top_in[col] = jnp.zeros(top_ref.shape, F32)

    edge = jnp.where(col == 0, 1, 0) + jnp.where(col == n_col - 1, 1, 0)
    pl.semaphore_wait(barrier, n_col - 1 + row_bits + edge)

    def side_copy(side, target, to):
        return pltpu.make_async_remote_copy(
            src_ref=planes_ref,
            dst_ref=target,
            send_sem=side_send.at[side],
            recv_sem=side_recv.at[side],
            device_id=to,
            device_id_type=MESH,
        )

    sides = [side_copy(0, before_ref, following), side_copy(1, after_ref, preceding)]
    for copy in sides:
        copy.start()

    place = [planes_ref[i * pitch : i * pitch + cells, :] for i in range(3)]
    moment = [planes_ref[(3 + i) * pitch : (3 + i) * pitch + cells, :] for i in range(3)]
    top_tables(cells, place, moment, top_ref, centre_ref)

    def top_copy(step):
        return pltpu.make_async_remote_copy(
            src_ref=top_ref,
            dst_ref=top_in.at[col],
            send_sem=top_send.at[step],
            recv_sem=top_recv.at[step],
            device_id=(row, lax.rem(col + step, n_col)),
            device_id_type=MESH,
        )

    def start(step, carry):
        top_copy(step).start()
        return carry

    def finish(step, carry):
        top_copy(step).wait()
        return carry

    lax.fori_loop(1, n_col, start, 0)

    leaf_sections(cells, place, moment, let_rows_ref, let_ref)
    sections = []
    for section in range(col_bits + row_bits):
        if section < col_bits:
            partner = (row, flip(col, section))
        else:
            partner = (flip(row, section - col_bits), col)
        sections.append(
            pltpu.make_async_remote_copy(
                src_ref=let_ref.at[section],
                dst_ref=let_in.at[section],
                send_sem=let_send.at[section],
                recv_sem=let_recv.at[section],
                device_id=partner,
                device_id_type=MESH,
            )
        )
    for copy in sections:
        copy.start()

    def build(group, carry):
        x = own_offsets(planes_ref, centre_ref, cells, group * 8)
        store_rows(feats, target_rows(x), group * 8, FAR_S)
        return carry

    lax.fori_loop(0, cells // 8, build, 0)
    lax.fori_loop(1, n_col, finish, 0)

    table = jnp.concatenate(
        [top_in[:, top, :] for top in range(2)] + [jnp.zeros((CELL - sources, CELL), F32)], axis=0
    )
    table = table.T
    entries = [table[k : k + 1, :] for k in range(15)]
    entries = [entries[i] - centre_ref[i : i + 1, :] for i in range(3)] + entries[3:]
    square, first, second, outputs = expansion_coefficients(entries)
    zero = jnp.zeros_like(entries[0])
    for position, form in enumerate((square, first, second)):
        for k, value in enumerate(source_rows(form, zero)):
            forms_rows[position * FAR_K + k : position * FAR_K + k + 1, :] = value
    for position in range(3):
        forms[position * sources : (position + 1) * sources, :] = (
            forms_rows[position * FAR_K : (position + 1) * FAR_K, :].T[:sources, :].astype(BF16)
        )
    for k, value in enumerate(outputs):
        for part, piece in enumerate(split3(value)):
            forms_rows[part * OUT_K + k : part * OUT_K + k + 1, :] = piece
    stacked = forms_rows[0 : 3 * OUT_K, 0:sources]
    kind = lax.rem(lax.broadcasted_iota(jnp.int32, stacked.shape, 0), OUT_K)
    pieces = []
    for low, high in ((0, 4), (4, 7), (7, OUT_K)):
        piece = jnp.where((kind >= low) & (kind < high), stacked, 0.0)
        pieces += [piece, piece]
    coeffs[...] = jnp.concatenate(pieces, axis=1).astype(BF16)

    def step(pair, carry):
        for sub in range(TOP_UNROLL):
            cell = 2 * (TOP_UNROLL * pair + sub)
            features = jnp.concatenate(
                [
                    feats[pl.ds(pl.multiple_of((cell + k) * FAR_S, FAR_S), FAR_K), :]
                    for k in range(2)
                ],
                axis=1,
            ).astype(BF16)
            values = jnp.dot(forms[...], features, preferred_element_type=F32)
            parts = weights_of(
                values[:sources], values[sources : 2 * sources], values[2 * sources :]
            )
            weights = jnp.concatenate([half for part in parts for half in split2(part)], axis=0)
            result = jnp.dot(coeffs[...], weights, preferred_element_type=F32)
            result = result[:OUT_K] + result[OUT_K : 2 * OUT_K] + result[2 * OUT_K :]
            for k in range(2):
                sums[pl.ds(cell + k, OUT_K, stride=pitch), :] = result[:, k * CELL : (k + 1) * CELL]
        return carry

    lax.fori_loop(0, cells // (2 * TOP_UNROLL), step, 0)

    def finish_top(group, carry):
        x = own_offsets(planes_ref, centre_ref, cells, group * 8)
        totals = [sums[rows8(k * pitch + group * 8), :] for k in range(OUT_K)]
        for i, value in enumerate(expansion_fields(x, totals)):
            field[rows8(i * pitch + group * 8), :] = value
        return carry

    lax.fori_loop(0, cells // 8, finish_top, 0)
    planes_to_output(field, out_ref, cells)

    for copy in sections:
        copy.wait()
    for copy in sides:
        copy.wait()


def near_source_rows(y, moment):
    zero = jnp.zeros_like(y[0])
    one = jnp.ones_like(y[0])
    back = [split3(-2.0 * entry) for entry in y]
    square = split3(y[0] * y[0] + y[1] * y[1] + y[2] * y[2] + SOFTEN)
    scaled = [(3.0 * COUPLING) * entry for entry in moment]
    const = split3(-(y[0] * scaled[0] + y[1] * scaled[1] + y[2] * scaled[2]))
    scaled = [split3(entry) for entry in scaled]
    rows = []
    for part in range(3):
        rows += [one] + [b[part] for b in back] + [s[part] for s in scaled] + [const[part]]
    for part, source in ((0, 0), (1, 1), (2, 0)):
        rows += [square[part]] + [b[source] for b in back] + [s[source] for s in scaled] + [zero]
    return rows


def near_target_rows(x):
    one = jnp.ones_like(x[0])
    zero = jnp.zeros_like(x[0])
    norm = split3(x[0] * x[0] + x[1] * x[1] + x[2] * x[2])
    pieces = [split3(entry) for entry in x]
    rows = []
    for part in range(3):
        high = [p[0] for p in pieces]
        rows += [norm[part]] + high + high + [one]
    for target in (1, 1, 2):
        chosen = [p[target] for p in pieces]
        rows += [one] + chosen + chosen + [zero]
    return rows


def near_kernel(
    cells,
    devices,
    n_col,
    near_ref,
    own_ref,
    prev_ref,
    next_ref,
    centre_ref,
    far_ref,
    let_ref,
    near_out,
    let_out,
    near_sources,
    near_targets,
    far_sources,
    far_coeffs,
    far_targets,
    masks,
    near_sums,
    far_sums,
    field,
):
    sublane = lax.broadcasted_iota(jnp.int32, (8, CELL), 0)
    lane = lax.broadcasted_iota(jnp.int32, (8, CELL), 1)
    diagonal = lax.broadcasted_iota(jnp.int32, (CELL, CELL), 0) == lax.broadcasted_iota(
        jnp.int32, (CELL, CELL), 1
    )
    masks[0:CELL, :] = jnp.zeros((CELL, CELL), F32)
    masks[CELL : 2 * CELL, :] = jnp.where(diagonal, 1e30, 0.0)

    def build_sources(ref, first, keep):
        def build(group, carry):
            y = own_offsets(ref, centre_ref, cells, group * 8)
            moment = [ref[rows8((3 + i) * pitch_of(cells) + group * 8), :] for i in range(3)]
            if keep is not None:
                moment = [jnp.where(keep, entry, 0.0) for entry in moment]
            store_rows(near_sources, near_source_rows(y, moment), first + group * 8, NEAR_S)
            return carry

        lax.fori_loop(0, cells // 8, build, 0)

    device = lax.axis_index("row") * n_col + lax.axis_index("col")
    ordinal = jnp.full((8, CELL), device, jnp.int32)
    build_sources(prev_ref, 0, ordinal > 0)
    build_sources(own_ref, cells, None)
    build_sources(next_ref, 2 * cells, ordinal < devices - 1)

    def build_targets(group, carry):
        x = own_offsets(own_ref, centre_ref, cells, group * 8)
        store_rows(near_targets, near_target_rows(x), group * 8, NEAR_S)
        store_rows(far_targets, target_rows(x), group * 8, FAR_S)
        return carry

    lax.fori_loop(0, cells // 8, build_targets, 0)

    groups = cells // 8
    lists = far_ref[...].astype(F32)
    lists = jnp.concatenate([lists, jnp.zeros((lists.shape[0], 256 - cells), F32)], axis=1)
    lists = jnp.concatenate([lists, jnp.zeros((CELL - lists.shape[0], 256), F32)], axis=0)
    far_sums[0:256, :] = lists.T
    repeated = jnp.bitwise_and(lax.broadcasted_iota(jnp.int32, (groups, CELL), 1), 15)
    slot = jnp.right_shift(lax.broadcasted_iota(jnp.int32, (groups, CELL), 1), 4)
    listed = jnp.zeros((groups, CELL), F32)
    for k in range(8):
        rows = far_sums[pl.ds(k, groups, stride=8), :]
        listed = jnp.where(slot == k, jnp.take_along_axis(rows, repeated, axis=1), listed)
    listed = listed.astype(jnp.int32)
    low = jnp.bitwise_and(listed, CELL - 1)
    section = jnp.right_shift(listed, 7)
    dense = []
    for entry in range(15):
        table = let_ref[pl.ds(entry, 8, stride=16), :]
        value = jnp.zeros(listed.shape, F32)
        for k in range(8):
            source = jnp.broadcast_to(table[k : k + 1, :], listed.shape)
            value = jnp.where(section == k, jnp.take_along_axis(source, low, axis=1), value)
        dense.append(value)
    repeat = sublane * 16 + jnp.bitwise_and(lane, 15)
    for entry in range(15):
        far_sums[entry * groups : (entry + 1) * groups, :] = dense[entry]

    def build_far(group, carry):
        table = [
            jnp.take_along_axis(
                jnp.broadcast_to(far_sums[pl.ds(entry * groups + group, 1), :], (8, CELL)),
                repeat,
                axis=1,
            )
            for entry in range(15)
        ]
        table = [table[i] - centre_ref[i : i + 1, :] for i in range(3)] + table[3:]
        square, first, second, outputs = expansion_coefficients(table)
        zero = jnp.zeros((8, CELL), F32)
        forms = [source_rows(form, zero) for form in (square, first, second)]
        rows = [
            jnp.where(lane < 16, a, jnp.where(lane < 32, b, c)) for a, b, c in zip(*forms)
        ]
        store_rows(far_sources, rows, group * 8, FAR_S)
        pieces = [split3(value) for value in outputs]
        rows = []
        for part in range(3):
            for k in range(OUT_K):
                kind = 0 if k < 4 else 1 if k < 7 else 2
                inside = (lane >= 32 * kind) & (lane < 32 * kind + 32)
                rows.append(jnp.where(inside, pieces[k][part], 0.0))
        store_rows(far_coeffs, rows, group * 8, COEF_S)
        return carry

    lax.fori_loop(0, groups, build_far, 0)

    upper_rows = lax.rem(lax.broadcasted_iota(jnp.int32, (NEAR_K, CELL), 0), 8) < 4

    def near_part(cell):
        targets = near_targets[pl.ds(pl.multiple_of(cell * NEAR_S, NEAR_S), NEAR_K), :]
        features = jnp.concatenate(
            [jnp.where(upper_rows, targets, 0.0), jnp.where(upper_rows, 0.0, targets)], axis=1
        ).astype(BF16)
        total = None
        for e in range(2):
            block = near_ref[e, cell]
            source = near_sources[pl.ds(pl.multiple_of(block * NEAR_S, NEAR_S), NEAR_K), :]
            values = jnp.dot(source.astype(BF16).T, features, preferred_element_type=F32)
            own = (block == cells + cell).astype(jnp.int32)
            mask = masks[pl.ds(pl.multiple_of(own * CELL, CELL), CELL), :]
            inverse = lax.rsqrt(values[:, :CELL] + mask)
            two = inverse * inverse
            three = two * inverse
            projected = values[:, CELL:] * two * three
            p_high, p_low = split2(projected)
            t_high, t_low = split2(three)
            weights = jnp.concatenate(
                [
                    jnp.concatenate([p_high, t_high], axis=1),
                    jnp.concatenate([p_low, t_low], axis=1),
                ],
                axis=0,
            )
            coeffs = source[:32].astype(BF16)
            result = jnp.dot(
                jnp.concatenate([coeffs, coeffs], axis=1), weights, preferred_element_type=F32
            )
            result = result[0:8] + result[8:16] + result[16:24]
            total = result if total is None else total + result
        near_sums[pl.ds(cell, 8, stride=pitch_of(cells)), :] = jnp.where(
            sublane < 4, total[:, :CELL], total[:, CELL:]
        )

    def far_part(cell):
        source = far_sources[pl.ds(pl.multiple_of(cell * FAR_S, FAR_S), FAR_K), :]
        features = far_targets[pl.ds(pl.multiple_of(cell * FAR_S, FAR_S), FAR_K), :].astype(BF16)
        values = jnp.dot(source.astype(BF16).T[:48], features, preferred_element_type=F32)
        parts = weights_of(values[:16], values[16:32], values[32:48])
        weights = jnp.concatenate([half for part in parts for half in split2(part)], axis=0)
        coeffs = far_coeffs[pl.ds(pl.multiple_of(cell * COEF_S, COEF_S), 48), :][:, :96].astype(BF16)
        result = jnp.dot(coeffs, weights, preferred_element_type=F32)
        result = result[:OUT_K] + result[OUT_K : 2 * OUT_K] + result[2 * OUT_K :]
        far_sums[pl.ds(cell, OUT_K, stride=pitch_of(cells)), :] = result

    def step(pair, carry):
        for sub in range(NEAR_UNROLL):
            near_part(NEAR_UNROLL * pair + sub)
            far_part(NEAR_UNROLL * pair + sub)
        return carry

    lax.fori_loop(0, cells // NEAR_UNROLL, step, 0)

    def finish_near(group, carry):
        x = own_offsets(own_ref, centre_ref, cells, group * 8)
        totals = [near_sums[rows8(k * pitch_of(cells) + group * 8), :] for k in range(7)]
        for i in range(3):
            field[rows8(i * pitch_of(cells) + group * 8), :] = (
                (x[i] * totals[0] - totals[4 + i]) * (1.0 / 3.0) + 0.5 * totals[1 + i]
            )
        return carry

    lax.fori_loop(0, cells // 8, finish_near, 0)
    planes_to_output(field, near_out, cells)

    def finish_far(group, carry):
        x = own_offsets(own_ref, centre_ref, cells, group * 8)
        totals = [far_sums[rows8(k * pitch_of(cells) + group * 8), :] for k in range(OUT_K)]
        for i, value in enumerate(expansion_fields(x, totals)):
            field[rows8(i * pitch_of(cells) + group * 8), :] = value
        return carry

    lax.fori_loop(0, cells // 8, finish_far, 0)
    planes_to_output(field, let_out, cells)


def vmem(count):
    return [pl.BlockSpec(memory_space=pltpu.VMEM)] * count


def make_first(cells, n_row, n_col, n):
    bits = n_row.bit_length() + n_col.bit_length() - 2
    sources = 2 * n_col
    planes = jax.ShapeDtypeStruct((6 * pitch_of(cells), CELL), F32)
    return pl.pallas_call(
        functools.partial(first_kernel, cells, n_row, n_col),
        out_shape=(
            planes,
            planes,
            planes,
            jax.ShapeDtypeStruct((bits, 16, CELL), F32),
            jax.ShapeDtypeStruct((8, CELL), F32),
            jax.ShapeDtypeStruct((3, n), F32),
        ),
        in_specs=vmem(3),
        out_specs=tuple(
            vmem(1) + [pl.BlockSpec(memory_space=pl.ANY)] * 2 + vmem(3)
        ),
        scratch_shapes=[
            pltpu.VMEM((bits, 16, CELL), F32),
            pltpu.VMEM((8, CELL), F32),
            pltpu.VMEM((n_col, 8, CELL), F32),
            pltpu.VMEM((cells * FAR_S, CELL), F32),
            pltpu.VMEM((3 * FAR_K, CELL), F32),
            pltpu.VMEM((3 * sources, FAR_K), BF16),
            pltpu.VMEM((3 * OUT_K, 6 * sources), BF16),
            pltpu.VMEM((OUT_K * pitch_of(cells), CELL), F32),
            pltpu.VMEM((3 * pitch_of(cells), CELL), F32),
            pltpu.SemaphoreType.DMA((2,)),
            pltpu.SemaphoreType.DMA((2,)),
            pltpu.SemaphoreType.DMA((bits,)),
            pltpu.SemaphoreType.DMA((bits,)),
            pltpu.SemaphoreType.DMA((n_col,)),
            pltpu.SemaphoreType.DMA((n_col,)),
        ],
        compiler_params=pltpu.CompilerParams(
            collective_id=0, has_side_effects=True, vmem_limit_bytes=VMEM_LIMIT
        ),
        cost_estimate=pl.CostEstimate(
            flops=8_000_000_000, bytes_accessed=4_000_000, transcendentals=1_600_000
        ),
        name="tables_exchange_top",
    )


def make_near(cells, devices, n_col, n):
    return pl.pallas_call(
        functools.partial(near_kernel, cells, devices, n_col),
        out_shape=(jax.ShapeDtypeStruct((3, n), F32), jax.ShapeDtypeStruct((3, n), F32)),
        in_specs=[pl.BlockSpec(memory_space=pltpu.SMEM)] + vmem(6),
        out_specs=tuple(vmem(2)),
        scratch_shapes=[
            pltpu.VMEM((3 * cells * NEAR_S, CELL), F32),
            pltpu.VMEM((cells * NEAR_S, CELL), F32),
            pltpu.VMEM((cells * FAR_S, CELL), F32),
            pltpu.VMEM((cells * COEF_S, CELL), F32),
            pltpu.VMEM((cells * FAR_S, CELL), F32),
            pltpu.VMEM((2 * CELL, CELL), F32),
            pltpu.VMEM((8 * pitch_of(cells), CELL), F32),
            pltpu.VMEM((OUT_K * pitch_of(cells), CELL), F32),
            pltpu.VMEM((3 * pitch_of(cells), CELL), F32),
        ],
        compiler_params=pltpu.CompilerParams(vmem_limit_bytes=VMEM_LIMIT),
        cost_estimate=pl.CostEstimate(
            flops=30_000_000_000, bytes_accessed=4_000_000, transcendentals=6_600_000
        ),
        name="near_and_let_field",
    )


def body(positions, moments, near_list, far_list, let_rows):
    n = positions.shape[1]
    cells = n // CELL
    n_row, n_col = lax.axis_size("row"), lax.axis_size("col")
    bits = let_rows.shape[1]
    planes, before, after, let_in, centre, top = make_first(cells, n_row, n_col, n)(
        positions, moments, let_rows
    )
    near, remote = make_near(cells, n_row * n_col, n_col, n)(
        near_list.T,
        planes,
        before,
        after,
        centre,
        far_list.T,
        let_in.reshape(bits * 16, CELL),
    )
    return near, remote, top


def solution(mesh):
    return jax.shard_map(
        body,
        mesh=mesh,
        in_specs=(
            P(None, ("row", "col")),
            P(None, ("row", "col")),
            P(("row", "col"), None),
            P(("row", "col"), None),
            P(("row", "col"), None, None),
        ),
        out_specs=(P(None, ("row", "col")), P(None, ("row", "col")), P(None, ("row", "col"))),
        check_vma=False,
    )
```

```python
import functools

import jax
import jax.numpy as jnp
from jax import lax
from jax.experimental import pallas as pl
from jax.experimental.pallas import tpu as pltpu
from jax.sharding import PartitionSpec as P

CELL = 128
SOFTEN = 0.09
COUPLING = 0.004
F32 = jnp.float32
BF16 = jnp.bfloat16
MESH = pl.DeviceIdType.MESH
VMEM_LIMIT = 58 * 1024 * 1024
SIX = ((0, 0), (0, 1), (0, 2), (1, 1), (1, 2), (2, 2))
NEAR_K = 48
FAR_K = 64
OUT_K = 16
NEAR_S = 56
FAR_S = 72
COEF_S = 56
FORMS = 6
GROUP = 4
TOP_UNROLL = 24
NEAR_UNROLL = 16


def split3(value):
    high = value.astype(BF16).astype(F32)
    rest = value - high
    middle = rest.astype(BF16).astype(F32)
    return high, middle, rest - middle


def split2(value):
    high = value.astype(BF16)
    return high, (value - high.astype(F32)).astype(BF16)


def source_pairing(parts):
    return [parts[0], parts[1], parts[2], parts[0], parts[1], parts[0]]


def target_pairing(parts):
    return [parts[0], parts[0], parts[0], parts[1], parts[1], parts[2]]


def expansion_coefficients(table):
    c = table[0:3]
    m = [COUPLING * entry for entry in table[3:6]]
    q = [[COUPLING * table[6 + 3 * j + i] for i in range(3)] for j in range(3)]
    g = [[q[j][i] + q[i][j] for i in range(3)] for j in range(3)]
    t = q[0][0] + q[1][1] + q[2][2]
    gc = [g[i][0] * c[0] + g[i][1] * c[1] + g[i][2] * c[2] for i in range(3)]
    zero = jnp.zeros_like(c[0])
    one = jnp.ones_like(c[0])
    square = (
        c[0] * c[0] + c[1] * c[1] + c[2] * c[2] + SOFTEN,
        [-2.0 * c[i] for i in range(3)],
        [one if i == j else zero for i, j in SIX],
    )
    first = (
        -3.0 * (c[0] * m[0] + c[1] * m[1] + c[2] * m[2] + t),
        [3.0 * m[i] for i in range(3)],
        None,
    )
    second = (
        7.5 * (c[0] * gc[0] + c[1] * gc[1] + c[2] * gc[2]),
        [-15.0 * gc[i] for i in range(3)],
        [(7.5 if i == j else 15.0) * g[i][j] for i, j in SIX],
    )
    outputs = [one] + list(c) + m + [3.0 * g[i][j] for i, j in SIX] + [3.0 * gc[i] for i in range(3)]
    return square, first, second, outputs


def source_rows(form, zero):
    const, linear, quadratic = form
    rows = list(split3(const))
    for entry in linear:
        rows += source_pairing(split3(entry))
    if quadratic is None:
        rows += [zero] * 36
    else:
        for entry in quadratic:
            rows += source_pairing(split3(entry))
    return rows + [zero] * (FAR_K - len(rows))


def target_rows(x):
    one = jnp.ones_like(x[0])
    rows = [one, one, one]
    for entry in x:
        rows += target_pairing(split3(entry))
    for i, j in SIX:
        rows += target_pairing(split3(x[i] * x[j]))
    return rows + [jnp.zeros_like(one)] * (FAR_K - len(rows))


def weights_of(square, first, second):
    inverse = lax.rsqrt(square)
    two = inverse * inverse
    three = two * inverse
    five = three * two
    return five * (first + second * two), three, five


def expansion_fields(x, sums):
    g = {}
    for place, (i, j) in enumerate(SIX):
        g[i, j] = g[j, i] = sums[7 + place]
    return [
        x[i] * sums[0]
        - sums[1 + i]
        - sums[4 + i]
        - (g[i, 0] * x[0] + g[i, 1] * x[1] + g[i, 2] * x[2])
        + sums[13 + i]
        for i in range(3)
    ]


def pitch_of(cells):
    return cells + 8 * (1 - cells // 8 % 2)


def rows8(start):
    return pl.ds(pl.multiple_of(start, 8), 8)


def lanes(block):
    return pl.ds(pl.multiple_of(block * CELL, CELL), CELL)


def store_rows(ref, rows, first, stride):
    for place, value in enumerate(rows):
        ref[pl.ds(first * stride + place, 8, stride=stride), :] = value


def own_offsets(planes_ref, centre_ref, cells, start):
    return [
        planes_ref[rows8(i * pitch_of(cells) + start), :] - centre_ref[i : i + 1, :] for i in range(3)
    ]


def planes_to_output(planes_ref, out_ref, cells):
    def step(b, carry):
        out_ref[:, lanes(b)] = planes_ref[pl.ds(b, 3, stride=pitch_of(cells)), :]
        return carry

    lax.fori_loop(0, cells, step, 0, unroll=8)


def lane_iota(shape):
    return lax.broadcasted_iota(jnp.int32, shape, len(shape) - 1)


def spread_sums(planes, targets):
    total = None
    for plane, target in zip(planes, targets):
        parts = jnp.concatenate([part.astype(BF16) for part in split3(plane)], axis=1)
        marked = target(lane_iota((3 * CELL, CELL))).astype(F32).astype(BF16)
        value = jnp.dot(parts, marked, preferred_element_type=F32)
        total = value if total is None else total + value
    return total


def leaf_tables(place, moment):
    mean = 1.0 / CELL
    centres = [spread_sums([entry], [lambda l: l >= 0]) * mean for entry in place]
    spread = [entry - centre for entry, centre in zip(place, centres)]
    lane = lane_iota(centres[0].shape)
    table = spread_sums(
        moment + [spread[j] * moment[i] for j in range(3) for i in range(3)],
        [lambda l, k=k: l == 3 + k for k in range(12)],
    )
    inner = (lane >= 6) & (lane < 15)
    by_centre = jnp.zeros_like(table)
    for j in range(3):
        table = jnp.where(lane == j, centres[j], table)
        by_centre = jnp.where(inner & (lane // 3 == 2 + j), centres[j], by_centre)
    by_moment = spread_sums(
        moment,
        [lambda l, i=i: (l >= 6) & (l < 15) & (lax.rem(l, 3) == i) for i in range(3)],
    )
    return table, by_centre, by_moment


def leaf_sections(table, let_rows_ref, let_ref):
    cells = table.shape[0]
    rows = jnp.concatenate([table, jnp.zeros((256 - cells, CELL), F32)], axis=0).T
    chosen = let_rows_ref[0]
    low = jnp.bitwise_and(chosen, CELL - 1)
    upper = chosen >= CELL
    for entry in range(15):
        row = jnp.broadcast_to(rows[entry : entry + 1, :], (8, 256))
        let_ref[:, entry, :] = jnp.where(
            upper,
            jnp.take_along_axis(row[:, CELL:], low, axis=1),
            jnp.take_along_axis(row[:, :CELL], low, axis=1),
        )
    let_ref[:, 15, :] = jnp.zeros((8, CELL), F32)


def top_tables(table, by_centre, by_moment, top_ref, centre_ref):
    half = table.shape[0] // 2
    sublane = lax.broadcasted_iota(jnp.int32, (8, CELL), 0)
    lane = lane_iota((1, CELL))
    tile = jnp.zeros((8, CELL), F32)
    middle = jnp.zeros((1, CELL), F32)
    for top in range(2):
        part = slice(top * half, (top + 1) * half)
        total = jnp.sum(table[part], axis=0, keepdims=True)
        centre = jnp.sum(by_centre[part], axis=0, keepdims=True) * (1.0 / half)
        moved = jnp.sum((by_centre[part] - centre) * by_moment[part], axis=0, keepdims=True)
        row = jnp.where(lane < 3, total * (1.0 / half), total + moved)
        tile = jnp.where(sublane == top, row, tile)
        middle = middle + 0.5 * row
    top_ref[...] = tile
    for i in range(3):
        centre_ref[i : i + 1, :] = jnp.broadcast_to(middle[:, i : i + 1], (1, CELL))
    centre_ref[3:8, :] = jnp.zeros((5, CELL), F32)


def first_kernel(
    cells,
    n_row,
    n_col,
    pos_ref,
    mom_ref,
    let_rows_ref,
    planes_ref,
    before_ref,
    after_ref,
    let_in,
    centre_ref,
    out_ref,
    let_ref,
    top_ref,
    top_in,
    feats,
    forms_rows,
    forms_stage,
    forms,
    coeffs,
    sums,
    side_send,
    side_recv,
    let_send,
    let_recv,
    top_send,
    top_recv,
):
    row = lax.axis_index("row")
    col = lax.axis_index("col")
    device = row * n_col + col
    devices = n_row * n_col
    col_bits = n_col.bit_length() - 1
    row_bits = n_row.bit_length() - 1
    sources = 2 * n_col
    pitch = pitch_of(cells)

    def flip(value, bit):
        return value + (1 << bit) * (1 - 2 * lax.rem(value // (1 << bit), 2))

    def flip_by(value, mask):
        for bit in range(mask.bit_length()):
            if mask >> bit & 1:
                value = flip(value, bit)
        return value

    def place_of(index):
        return (index // n_col, lax.rem(index, n_col))

    following = place_of(lax.rem(device + 1, devices))
    preceding = place_of(lax.rem(device + devices - 1, devices))

    four = [flip_by(col, k) for k in range(1, GROUP)]
    groups = [flip_by(col, k * GROUP) for k in range(1, n_col // GROUP)]
    barrier = pltpu.get_barrier_semaphore()
    partners = [(row, other) for other in four + groups]
    partners += [(flip(row, bit), col) for bit in range(row_bits)] + [following, preceding]
    for partner in partners:
        pl.semaphore_signal(barrier, inc=1, device_id=partner, device_id_type=MESH)

    def to_planes(b, carry):
        planes_ref[pl.ds(b, 3, stride=pitch), :] = pos_ref[:, lanes(b)]
        planes_ref[pl.ds(3 * pitch + b, 3, stride=pitch), :] = mom_ref[:, lanes(b)]
        return carry

    lax.fori_loop(0, cells, to_planes, 0, unroll=8)

    def side_copy(side, target, to):
        return pltpu.make_async_remote_copy(
            src_ref=planes_ref,
            dst_ref=target,
            send_sem=side_send.at[side],
            recv_sem=side_recv.at[side],
            device_id=to,
            device_id_type=MESH,
        )

    place = [planes_ref[i * pitch : i * pitch + cells, :] for i in range(3)]
    moment = [planes_ref[(3 + i) * pitch : (3 + i) * pitch + cells, :] for i in range(3)]
    leaf, by_centre, by_moment = leaf_tables(place, moment)
    top_tables(leaf, by_centre, by_moment, top_ref, centre_ref)
    top_in[col] = top_ref[...]
    pl.semaphore_wait(barrier, len(partners))

    first_copies = [
        pltpu.make_async_remote_copy(
            src_ref=top_ref,
            dst_ref=top_in.at[col],
            send_sem=top_send.at[k],
            recv_sem=top_recv.at[k],
            device_id=(row, other),
            device_id_type=MESH,
        )
        for k, other in enumerate(four)
    ]
    for copy in first_copies:
        copy.start()
    sides = [side_copy(0, before_ref, following), side_copy(1, after_ref, preceding)]
    for copy in sides:
        copy.start()

    leaf_sections(leaf, let_rows_ref, let_ref)
    sections = []
    for section in range(col_bits + row_bits):
        if section < col_bits:
            partner = (row, flip(col, section))
        else:
            partner = (flip(row, section - col_bits), col)
        sections.append(
            pltpu.make_async_remote_copy(
                src_ref=let_ref.at[section],
                dst_ref=let_in.at[section],
                send_sem=let_send.at[section],
                recv_sem=let_recv.at[section],
                device_id=partner,
                device_id_type=MESH,
            )
        )
    for copy in sections:
        copy.start()

    for copy in first_copies:
        copy.wait()
    mine = pl.ds(col // GROUP * GROUP, GROUP)
    second_copies = [
        pltpu.make_async_remote_copy(
            src_ref=top_in.at[mine],
            dst_ref=top_in.at[mine],
            send_sem=top_send.at[len(four) + k],
            recv_sem=top_recv.at[len(four) + k],
            device_id=(row, other),
            device_id_type=MESH,
        )
        for k, other in enumerate(groups)
    ]
    for copy in second_copies:
        copy.start()

    def build(group, carry):
        x = own_offsets(planes_ref, centre_ref, cells, group * 8)
        store_rows(feats, target_rows(x), group * 8, FAR_S)
        return carry

    lax.fori_loop(0, cells // 8, build, 0, unroll=2)
    for copy in second_copies:
        copy.wait()
    top_in[col] = jnp.zeros(top_ref.shape, F32)

    table = jnp.concatenate(
        [top_in[:, top, :] for top in range(2)] + [jnp.zeros((CELL - sources, CELL), F32)], axis=0
    )
    table = table.T
    entries = [table[k : k + 1, :] for k in range(15)]
    entries = [entries[i] - centre_ref[i : i + 1, :] for i in range(3)] + entries[3:]
    square, first, second, outputs = expansion_coefficients(entries)
    zero = jnp.zeros_like(entries[0])
    g = [[outputs[7 + SIX.index((min(i, j), max(i, j)))] for j in range(3)] for i in range(3)]
    bent = [(-outputs[13 + i], g[i], None) for i in range(3)]
    for position, form in enumerate([square, first, second] + bent):
        base = position * FAR_K
        for k, value in enumerate(source_rows(form, zero)):
            forms_rows[base + k : base + k + 1, :] = value
    for position in range(FORMS):
        value = forms_rows[position * FAR_K : (position + 1) * FAR_K, :].T
        for tile in range(sources // 8):
            start = (tile * FORMS + position) * 8
            forms_stage[start : start + 8, :] = value[tile * 8 : (tile + 1) * 8, :]
    forms[...] = forms_stage[...].astype(BF16)
    for k, value in enumerate(entries[:3] + outputs[4:7]):
        forms_rows[k : k + 1, :] = value
    columns = forms_rows[0:CELL, :].T
    for k in range(6):
        coeffs[k * sources : (k + 1) * sources, :] = jnp.broadcast_to(
            columns[:sources, k : k + 1], (sources, CELL)
        )

    def step(pair, carry):
        for sub in range(TOP_UNROLL):
            cell = 2 * (TOP_UNROLL * pair + sub)
            features = jnp.concatenate(
                [
                    feats[pl.ds(pl.multiple_of((cell + k) * FAR_S, FAR_S), FAR_K), :]
                    for k in range(2)
                ],
                axis=1,
            ).astype(BF16)
            values = jnp.dot(forms[...], features, preferred_element_type=F32)
            for k in range(2):
                totals = None
                for tile in range(sources // 8):
                    form = [
                        values[
                            (tile * FORMS + f) * 8 : (tile * FORMS + f + 1) * 8,
                            k * CELL : (k + 1) * CELL,
                        ]
                        for f in range(FORMS)
                    ]
                    const = [
                        coeffs[f * sources + tile * 8 : f * sources + (tile + 1) * 8, :]
                        for f in range(6)
                    ]
                    weight, three, five = weights_of(*form[:3])
                    terms = [weight] + [
                        const[i] * weight + const[3 + i] * three + form[3 + i] * five
                        for i in range(3)
                    ]
                    totals = terms if totals is None else [t + u for t, u in zip(totals, terms)]
                for place_, value in enumerate(totals):
                    sums[rows8((place_ * cells + cell + k) * 8), :] = value
        return carry

    lax.fori_loop(0, cells // (2 * TOP_UNROLL), step, 0)

    def finish_top(group, carry):
        x = own_offsets(planes_ref, centre_ref, cells, group * 8)
        totals = []
        for place_ in range(4):
            base = (place_ * cells + group * 8) * 8
            parts = [sums[pl.ds(base + k, 8, stride=8), :] for k in range(8)]
            while len(parts) > 1:
                parts = [parts[k] + parts[k + 1] for k in range(0, len(parts), 2)]
            totals.append(parts[0])
        for i in range(3):
            out_ref[rows8(i * pitch + group * 8), :] = x[i] * totals[0] - totals[1 + i]
        return carry

    lax.fori_loop(0, cells // 8, finish_top, 0, unroll=2)

    for copy in sections:
        copy.wait()
    for copy in sides:
        copy.wait()


def near_source_rows(y, moment):
    zero = jnp.zeros_like(y[0])
    one = jnp.ones_like(y[0])
    back = [split3(-2.0 * entry) for entry in y]
    square = split3(y[0] * y[0] + y[1] * y[1] + y[2] * y[2] + SOFTEN)
    scaled = [(3.0 * COUPLING) * entry for entry in moment]
    const = split3(-(y[0] * scaled[0] + y[1] * scaled[1] + y[2] * scaled[2]))
    scaled = [split3(entry) for entry in scaled]
    rows = []
    for part in range(3):
        rows += [one] + [b[part] for b in back] + [s[part] for s in scaled] + [const[part]]
    for part, source in ((0, 0), (1, 1), (2, 0)):
        rows += [square[part]] + [b[source] for b in back] + [s[source] for s in scaled] + [zero]
    return rows


def near_target_rows(x):
    one = jnp.ones_like(x[0])
    zero = jnp.zeros_like(x[0])
    norm = split3(x[0] * x[0] + x[1] * x[1] + x[2] * x[2])
    pieces = [split3(entry) for entry in x]
    rows = []
    for part in range(3):
        high = [p[0] for p in pieces]
        rows += [norm[part]] + high + high + [one]
    for target in (1, 1, 2):
        chosen = [p[target] for p in pieces]
        rows += [one] + chosen + chosen + [zero]
    return rows


def near_kernel(
    cells,
    devices,
    n_col,
    near_ref,
    own_ref,
    prev_ref,
    next_ref,
    centre_ref,
    far_ref,
    let_ref,
    top_ref,
    near_out,
    let_out,
    top_out,
    near_sources,
    near_targets,
    far_sources,
    far_coeffs,
    far_targets,
    masks,
    near_sums,
    far_sums,
    field,
):
    sublane = lax.broadcasted_iota(jnp.int32, (8, CELL), 0)
    lane = lax.broadcasted_iota(jnp.int32, (8, CELL), 1)
    diagonal = lax.broadcasted_iota(jnp.int32, (CELL, CELL), 0) == lax.broadcasted_iota(
        jnp.int32, (CELL, CELL), 1
    )
    masks[0:CELL, :] = jnp.zeros((CELL, CELL), F32)
    masks[CELL : 2 * CELL, :] = jnp.where(diagonal, 1e30, 0.0)

    def build_sources(ref, first, keep):
        def build(group, carry):
            y = own_offsets(ref, centre_ref, cells, group * 8)
            moment = [ref[rows8((3 + i) * pitch_of(cells) + group * 8), :] for i in range(3)]
            if keep is not None:
                moment = [jnp.where(keep, entry, 0.0) for entry in moment]
            store_rows(near_sources, near_source_rows(y, moment), first + group * 8, NEAR_S)
            return carry

        lax.fori_loop(0, cells // 8, build, 0, unroll=2)

    device = lax.axis_index("row") * n_col + lax.axis_index("col")
    ordinal = jnp.full((8, CELL), device, jnp.int32)
    build_sources(prev_ref, 0, ordinal > 0)
    build_sources(own_ref, cells, None)
    build_sources(next_ref, 2 * cells, ordinal < devices - 1)

    def build_targets(group, carry):
        x = own_offsets(own_ref, centre_ref, cells, group * 8)
        store_rows(near_targets, near_target_rows(x), group * 8, NEAR_S)
        store_rows(far_targets, target_rows(x), group * 8, FAR_S)
        return carry

    lax.fori_loop(0, cells // 8, build_targets, 0, unroll=2)

    groups = cells // 8
    lists = far_ref[...].astype(F32)
    lists = jnp.concatenate([lists, jnp.zeros((lists.shape[0], 256 - cells), F32)], axis=1)
    lists = jnp.concatenate([lists, jnp.zeros((CELL - lists.shape[0], 256), F32)], axis=0)
    far_sums[0:256, :] = lists.T
    repeated = jnp.bitwise_and(lax.broadcasted_iota(jnp.int32, (groups, CELL), 1), 15)
    slot = jnp.right_shift(lax.broadcasted_iota(jnp.int32, (groups, CELL), 1), 4)
    listed = jnp.zeros((groups, CELL), F32)
    for k in range(8):
        rows = far_sums[pl.ds(k, groups, stride=8), :]
        listed = jnp.where(slot == k, jnp.take_along_axis(rows, repeated, axis=1), listed)
    listed = listed.astype(jnp.int32)
    low = jnp.bitwise_and(listed, CELL - 1)
    section = jnp.right_shift(listed, 7)
    dense = []
    for entry in range(15):
        table = let_ref[pl.ds(entry, 8, stride=16), :]
        value = jnp.zeros(listed.shape, F32)
        for k in range(8):
            source = jnp.broadcast_to(table[k : k + 1, :], listed.shape)
            value = jnp.where(section == k, jnp.take_along_axis(source, low, axis=1), value)
        dense.append(value)
    repeat = sublane * 16 + jnp.bitwise_and(lane, 15)
    for entry in range(15):
        far_sums[entry * groups : (entry + 1) * groups, :] = dense[entry]

    def build_far(group, carry):
        table = [
            jnp.take_along_axis(
                jnp.broadcast_to(far_sums[pl.ds(entry * groups + group, 1), :], (8, CELL)),
                repeat,
                axis=1,
            )
            for entry in range(15)
        ]
        table = [table[i] - centre_ref[i : i + 1, :] for i in range(3)] + table[3:]
        square, first, second, outputs = expansion_coefficients(table)
        zero = jnp.zeros((8, CELL), F32)
        forms = [source_rows(form, zero) for form in (square, first, second)]
        rows = [
            jnp.where(lane < 16, a, jnp.where(lane < 32, b, c)) for a, b, c in zip(*forms)
        ]
        store_rows(far_sources, rows, group * 8, FAR_S)
        pieces = [split3(value) for value in outputs]
        rows = []
        for part in range(3):
            for k in range(OUT_K):
                kind = 0 if k < 4 else 1 if k < 7 else 2
                inside = (lane >= 32 * kind) & (lane < 32 * kind + 32)
                rows.append(jnp.where(inside, pieces[k][part], 0.0))
        store_rows(far_coeffs, rows, group * 8, COEF_S)
        return carry

    lax.fori_loop(0, groups, build_far, 0, unroll=2)

    upper_rows = lax.rem(lax.broadcasted_iota(jnp.int32, (NEAR_K, CELL), 0), 8) < 4

    def near_part(cell):
        targets = near_targets[pl.ds(pl.multiple_of(cell * NEAR_S, NEAR_S), NEAR_K), :]
        features = jnp.concatenate(
            [jnp.where(upper_rows, targets, 0.0), jnp.where(upper_rows, 0.0, targets)], axis=1
        ).astype(BF16)
        total = None
        for e in range(2):
            block = near_ref[e, cell]
            source = near_sources[pl.ds(pl.multiple_of(block * NEAR_S, NEAR_S), NEAR_K), :]
            values = jnp.dot(source.astype(BF16).T, features, preferred_element_type=F32)
            own = (block == cells + cell).astype(jnp.int32)
            mask = masks[pl.ds(pl.multiple_of(own * CELL, CELL), CELL), :]
            inverse = lax.rsqrt(values[:, :CELL] + mask)
            two = inverse * inverse
            three = two * inverse
            projected = values[:, CELL:] * two * three
            p_high, p_low = split2(projected)
            t_high, t_low = split2(three)
            weights = jnp.concatenate(
                [
                    jnp.concatenate([p_high, t_high], axis=1),
                    jnp.concatenate([p_low, t_low], axis=1),
                ],
                axis=0,
            )
            coeffs = source[:32].astype(BF16)
            result = jnp.dot(
                jnp.concatenate([coeffs, coeffs], axis=1), weights, preferred_element_type=F32
            )
            result = result[0:8] + result[8:16] + result[16:24]
            total = result if total is None else total + result
        near_sums[pl.ds(cell, 8, stride=pitch_of(cells)), :] = jnp.where(
            sublane < 4, total[:, :CELL], total[:, CELL:]
        )

    def far_part(cell):
        source = far_sources[pl.ds(pl.multiple_of(cell * FAR_S, FAR_S), FAR_K), :]
        features = far_targets[pl.ds(pl.multiple_of(cell * FAR_S, FAR_S), FAR_K), :].astype(BF16)
        values = jnp.dot(source.astype(BF16).T[:48], features, preferred_element_type=F32)
        parts = weights_of(values[:16], values[16:32], values[32:48])
        weights = jnp.concatenate([half for part in parts for half in split2(part)], axis=0)
        coeffs = far_coeffs[pl.ds(pl.multiple_of(cell * COEF_S, COEF_S), 48), :][:, :96].astype(BF16)
        result = jnp.dot(coeffs, weights, preferred_element_type=F32)
        result = result[:OUT_K] + result[OUT_K : 2 * OUT_K] + result[2 * OUT_K :]
        far_sums[pl.ds(cell, OUT_K, stride=pitch_of(cells)), :] = result

    def step(pair, carry):
        for sub in range(NEAR_UNROLL):
            near_part(NEAR_UNROLL * pair + sub)
            far_part(NEAR_UNROLL * pair + sub)
        return carry

    lax.fori_loop(0, cells // NEAR_UNROLL, step, 0)

    def finish_near(group, carry):
        x = own_offsets(own_ref, centre_ref, cells, group * 8)
        totals = [near_sums[rows8(k * pitch_of(cells) + group * 8), :] for k in range(7)]
        for i in range(3):
            field[rows8(i * pitch_of(cells) + group * 8), :] = (
                (x[i] * totals[0] - totals[4 + i]) * (1.0 / 3.0) + 0.5 * totals[1 + i]
            )
        return carry

    lax.fori_loop(0, cells // 8, finish_near, 0, unroll=2)
    planes_to_output(field, near_out, cells)

    def finish_far(group, carry):
        x = own_offsets(own_ref, centre_ref, cells, group * 8)
        totals = [far_sums[rows8(k * pitch_of(cells) + group * 8), :] for k in range(OUT_K)]
        for i, value in enumerate(expansion_fields(x, totals)):
            field[rows8(i * pitch_of(cells) + group * 8), :] = value
        return carry

    lax.fori_loop(0, cells // 8, finish_far, 0, unroll=2)
    planes_to_output(field, let_out, cells)
    planes_to_output(top_ref, top_out, cells)


def vmem(count):
    return [pl.BlockSpec(memory_space=pltpu.VMEM)] * count


def make_first(cells, n_row, n_col):
    bits = n_row.bit_length() + n_col.bit_length() - 2
    sources = 2 * n_col
    planes = jax.ShapeDtypeStruct((6 * pitch_of(cells), CELL), F32)
    return pl.pallas_call(
        functools.partial(first_kernel, cells, n_row, n_col),
        out_shape=(
            planes,
            planes,
            planes,
            jax.ShapeDtypeStruct((bits, 16, CELL), F32),
            jax.ShapeDtypeStruct((8, CELL), F32),
            jax.ShapeDtypeStruct((3 * pitch_of(cells), CELL), F32),
        ),
        in_specs=vmem(3),
        out_specs=tuple(
            vmem(1) + [pl.BlockSpec(memory_space=pl.ANY)] * 2 + vmem(3)
        ),
        scratch_shapes=[
            pltpu.VMEM((bits, 16, CELL), F32),
            pltpu.VMEM((8, CELL), F32),
            pltpu.VMEM((n_col, 8, CELL), F32),
            pltpu.VMEM((cells * FAR_S, CELL), F32),
            pltpu.VMEM((FORMS * FAR_K, CELL), F32),
            pltpu.VMEM((FORMS * sources, FAR_K), F32),
            pltpu.VMEM((FORMS * sources, FAR_K), BF16),
            pltpu.VMEM((6 * sources, CELL), F32),
            pltpu.VMEM((4 * cells * 8, CELL), F32),
            pltpu.SemaphoreType.DMA((2,)),
            pltpu.SemaphoreType.DMA((2,)),
            pltpu.SemaphoreType.DMA((bits,)),
            pltpu.SemaphoreType.DMA((bits,)),
            pltpu.SemaphoreType.DMA((n_col,)),
            pltpu.SemaphoreType.DMA((n_col,)),
        ],
        compiler_params=pltpu.CompilerParams(
            collective_id=0, has_side_effects=True, vmem_limit_bytes=VMEM_LIMIT
        ),
        cost_estimate=pl.CostEstimate(
            flops=8_000_000_000, bytes_accessed=4_000_000, transcendentals=1_600_000
        ),
        name="tables_exchange_top",
    )


def make_near(cells, devices, n_col, n):
    return pl.pallas_call(
        functools.partial(near_kernel, cells, devices, n_col),
        out_shape=(jax.ShapeDtypeStruct((3, n), F32),) * 3,
        in_specs=[pl.BlockSpec(memory_space=pltpu.SMEM)] + vmem(7),
        out_specs=tuple(vmem(3)),
        scratch_shapes=[
            pltpu.VMEM((3 * cells * NEAR_S, CELL), F32),
            pltpu.VMEM((cells * NEAR_S, CELL), F32),
            pltpu.VMEM((cells * FAR_S, CELL), F32),
            pltpu.VMEM((cells * COEF_S, CELL), F32),
            pltpu.VMEM((cells * FAR_S, CELL), F32),
            pltpu.VMEM((2 * CELL, CELL), F32),
            pltpu.VMEM((8 * pitch_of(cells), CELL), F32),
            pltpu.VMEM((OUT_K * pitch_of(cells), CELL), F32),
            pltpu.VMEM((3 * pitch_of(cells), CELL), F32),
        ],
        compiler_params=pltpu.CompilerParams(vmem_limit_bytes=VMEM_LIMIT),
        cost_estimate=pl.CostEstimate(
            flops=30_000_000_000, bytes_accessed=4_000_000, transcendentals=6_600_000
        ),
        name="near_and_let_field",
    )


def body(positions, moments, near_list, far_list, let_rows):
    n = positions.shape[1]
    cells = n // CELL
    n_row, n_col = lax.axis_size("row"), lax.axis_size("col")
    bits = let_rows.shape[1]
    planes, before, after, let_in, centre, top = make_first(cells, n_row, n_col)(
        positions, moments, let_rows
    )
    return make_near(cells, n_row * n_col, n_col, n)(
        near_list.T,
        planes,
        before,
        after,
        centre,
        far_list.T,
        let_in.reshape(bits * 16, CELL),
        top,
    )


def solution(mesh):
    return jax.shard_map(
        body,
        mesh=mesh,
        in_specs=(
            P(None, ("row", "col")),
            P(None, ("row", "col")),
            P(("row", "col"), None),
            P(("row", "col"), None),
            P(("row", "col"), None, None),
        ),
        out_specs=(P(None, ("row", "col")), P(None, ("row", "col")), P(None, ("row", "col"))),
        check_vma=False,
    )
```

```python
import functools

import jax
import jax.numpy as jnp
from jax import lax
from jax.experimental import pallas as pl
from jax.experimental.pallas import tpu as pltpu
from jax.sharding import PartitionSpec as P

CELL = 128
SOFTEN = 0.09
COUPLING = 0.004
F32 = jnp.float32
BF16 = jnp.bfloat16
MESH = pl.DeviceIdType.MESH
VMEM_LIMIT = 58 * 1024 * 1024
SIX = ((0, 0), (0, 1), (0, 2), (1, 1), (1, 2), (2, 2))
NEAR_K = 48
FAR_K = 64
OUT_K = 16
NEAR_S = 56
FAR_S = 72
COEF_S = 56
FORMS = 6
GROUP = 4
TOP_UNROLL = 24
NEAR_UNROLL = 32


def split3(value):
    high = value.astype(BF16).astype(F32)
    rest = value - high
    middle = rest.astype(BF16).astype(F32)
    return high, middle, rest - middle


def split2(value):
    high = value.astype(BF16)
    return high, (value - high.astype(F32)).astype(BF16)


def source_pairing(parts):
    return [parts[0], parts[1], parts[2], parts[0], parts[1], parts[0]]


def target_pairing(parts):
    return [parts[0], parts[0], parts[0], parts[1], parts[1], parts[2]]


def expansion_coefficients(table):
    c = table[0:3]
    m = [COUPLING * entry for entry in table[3:6]]
    q = [[COUPLING * table[6 + 3 * j + i] for i in range(3)] for j in range(3)]
    g = [[q[j][i] + q[i][j] for i in range(3)] for j in range(3)]
    t = q[0][0] + q[1][1] + q[2][2]
    gc = [g[i][0] * c[0] + g[i][1] * c[1] + g[i][2] * c[2] for i in range(3)]
    zero = jnp.zeros_like(c[0])
    one = jnp.ones_like(c[0])
    square = (
        c[0] * c[0] + c[1] * c[1] + c[2] * c[2] + SOFTEN,
        [-2.0 * c[i] for i in range(3)],
        [one if i == j else zero for i, j in SIX],
    )
    first = (
        -3.0 * (c[0] * m[0] + c[1] * m[1] + c[2] * m[2] + t),
        [3.0 * m[i] for i in range(3)],
        None,
    )
    second = (
        7.5 * (c[0] * gc[0] + c[1] * gc[1] + c[2] * gc[2]),
        [-15.0 * gc[i] for i in range(3)],
        [(7.5 if i == j else 15.0) * g[i][j] for i, j in SIX],
    )
    outputs = [one] + list(c) + m + [3.0 * g[i][j] for i, j in SIX] + [3.0 * gc[i] for i in range(3)]
    return square, first, second, outputs


def source_rows(form, zero):
    const, linear, quadratic = form
    rows = list(split3(const))
    for entry in linear:
        rows += source_pairing(split3(entry))
    if quadratic is None:
        rows += [zero] * 36
    else:
        for entry in quadratic:
            rows += source_pairing(split3(entry))
    return rows + [zero] * (FAR_K - len(rows))


def target_rows(x):
    one = jnp.ones_like(x[0])
    rows = [one, one, one]
    for entry in x:
        rows += target_pairing(split3(entry))
    for i, j in SIX:
        rows += target_pairing(split3(x[i] * x[j]))
    return rows + [jnp.zeros_like(one)] * (FAR_K - len(rows))


def weights_of(square, first, second):
    inverse = lax.rsqrt(square)
    two = inverse * inverse
    three = two * inverse
    five = three * two
    return five * (first + second * two), three, five


def expansion_fields(x, sums):
    g = {}
    for place, (i, j) in enumerate(SIX):
        g[i, j] = g[j, i] = sums[7 + place]
    return [
        x[i] * sums[0]
        - sums[1 + i]
        - sums[4 + i]
        - (g[i, 0] * x[0] + g[i, 1] * x[1] + g[i, 2] * x[2])
        + sums[13 + i]
        for i in range(3)
    ]


def pitch_of(cells):
    return cells + 8 * (1 - cells // 8 % 2)


def rows8(start):
    return pl.ds(pl.multiple_of(start, 8), 8)


def lanes(block):
    return pl.ds(pl.multiple_of(block * CELL, CELL), CELL)


def store_rows(ref, rows, first, stride):
    for place, value in enumerate(rows):
        ref[pl.ds(first * stride + place, 8, stride=stride), :] = value


def own_offsets(planes_ref, centre_ref, cells, start):
    return [
        planes_ref[rows8(i * pitch_of(cells) + start), :] - centre_ref[i : i + 1, :] for i in range(3)
    ]


def planes_to_output(planes_ref, out_ref, cells):
    def step(b, carry):
        out_ref[:, lanes(b)] = planes_ref[pl.ds(b, 3, stride=pitch_of(cells)), :]
        return carry

    lax.fori_loop(0, cells, step, 0, unroll=8)


def lane_iota(shape):
    return lax.broadcasted_iota(jnp.int32, shape, len(shape) - 1)


def spread_sums(planes, targets):
    total = None
    for plane, target in zip(planes, targets):
        parts = jnp.concatenate([part.astype(BF16) for part in split3(plane)], axis=1)
        marked = target(lane_iota((3 * CELL, CELL))).astype(F32).astype(BF16)
        value = jnp.dot(parts, marked, preferred_element_type=F32)
        total = value if total is None else total + value
    return total


def leaf_tables(place, moment):
    mean = 1.0 / CELL
    centres = [spread_sums([entry], [lambda l: l >= 0]) * mean for entry in place]
    spread = [entry - centre for entry, centre in zip(place, centres)]
    lane = lane_iota(centres[0].shape)
    table = spread_sums(
        moment + [spread[j] * moment[i] for j in range(3) for i in range(3)],
        [lambda l, k=k: l == 3 + k for k in range(12)],
    )
    inner = (lane >= 6) & (lane < 15)
    by_centre = jnp.zeros_like(table)
    for j in range(3):
        table = jnp.where(lane == j, centres[j], table)
        by_centre = jnp.where(inner & (lane // 3 == 2 + j), centres[j], by_centre)
    by_moment = spread_sums(
        moment,
        [lambda l, i=i: (l >= 6) & (l < 15) & (lax.rem(l, 3) == i) for i in range(3)],
    )
    return table, by_centre, by_moment


def leaf_sections(table, let_rows_ref, let_ref):
    cells = table.shape[0]
    rows = jnp.concatenate([table, jnp.zeros((256 - cells, CELL), F32)], axis=0).T
    chosen = let_rows_ref[0]
    low = jnp.bitwise_and(chosen, CELL - 1)
    upper = chosen >= CELL
    for entry in range(15):
        row = jnp.broadcast_to(rows[entry : entry + 1, :], (8, 256))
        let_ref[:, entry, :] = jnp.where(
            upper,
            jnp.take_along_axis(row[:, CELL:], low, axis=1),
            jnp.take_along_axis(row[:, :CELL], low, axis=1),
        )
    let_ref[:, 15, :] = jnp.zeros((8, CELL), F32)


def top_tables(table, by_centre, by_moment, top_ref, centre_ref):
    half = table.shape[0] // 2
    sublane = lax.broadcasted_iota(jnp.int32, (8, CELL), 0)
    lane = lane_iota((1, CELL))
    tile = jnp.zeros((8, CELL), F32)
    middle = jnp.zeros((1, CELL), F32)
    for top in range(2):
        part = slice(top * half, (top + 1) * half)
        total = jnp.sum(table[part], axis=0, keepdims=True)
        centre = jnp.sum(by_centre[part], axis=0, keepdims=True) * (1.0 / half)
        moved = jnp.sum((by_centre[part] - centre) * by_moment[part], axis=0, keepdims=True)
        row = jnp.where(lane < 3, total * (1.0 / half), total + moved)
        tile = jnp.where(sublane == top, row, tile)
        middle = middle + 0.5 * row
    top_ref[...] = tile
    for i in range(3):
        centre_ref[i : i + 1, :] = jnp.broadcast_to(middle[:, i : i + 1], (1, CELL))
    centre_ref[3:8, :] = jnp.zeros((5, CELL), F32)


def first_kernel(
    cells,
    n_row,
    n_col,
    pos_ref,
    mom_ref,
    let_rows_ref,
    planes_ref,
    before_ref,
    after_ref,
    let_in,
    centre_ref,
    out_ref,
    let_ref,
    top_ref,
    top_in,
    feats,
    forms_rows,
    forms_stage,
    forms,
    coeffs,
    sums,
    side_send,
    side_recv,
    let_send,
    let_recv,
    top_send,
    top_recv,
):
    row = lax.axis_index("row")
    col = lax.axis_index("col")
    device = row * n_col + col
    devices = n_row * n_col
    col_bits = n_col.bit_length() - 1
    row_bits = n_row.bit_length() - 1
    sources = 2 * n_col
    pitch = pitch_of(cells)

    def flip(value, bit):
        return value + (1 << bit) * (1 - 2 * lax.rem(value // (1 << bit), 2))

    def flip_by(value, mask):
        for bit in range(mask.bit_length()):
            if mask >> bit & 1:
                value = flip(value, bit)
        return value

    def place_of(index):
        return (index // n_col, lax.rem(index, n_col))

    following = place_of(lax.rem(device + 1, devices))
    preceding = place_of(lax.rem(device + devices - 1, devices))

    four = [flip_by(col, k) for k in range(1, GROUP)]
    groups = [flip_by(col, k * GROUP) for k in range(1, n_col // GROUP)]
    barrier = pltpu.get_barrier_semaphore()
    partners = [(row, other) for other in four + groups]
    partners += [(flip(row, bit), col) for bit in range(row_bits)] + [following, preceding]
    for partner in partners:
        pl.semaphore_signal(barrier, inc=1, device_id=partner, device_id_type=MESH)

    def to_planes(b, carry):
        planes_ref[pl.ds(b, 3, stride=pitch), :] = pos_ref[:, lanes(b)]
        planes_ref[pl.ds(3 * pitch + b, 3, stride=pitch), :] = mom_ref[:, lanes(b)]
        return carry

    lax.fori_loop(0, cells, to_planes, 0, unroll=8)

    def side_copy(side, part, target, to):
        rows = slice(part * pitch, (part + 1) * pitch)
        return pltpu.make_async_remote_copy(
            src_ref=planes_ref.at[rows],
            dst_ref=target.at[rows],
            send_sem=side_send.at[6 * side + part],
            recv_sem=side_recv.at[6 * side + part],
            device_id=to,
            device_id_type=MESH,
        )

    place = [planes_ref[i * pitch : i * pitch + cells, :] for i in range(3)]
    moment = [planes_ref[(3 + i) * pitch : (3 + i) * pitch + cells, :] for i in range(3)]
    leaf, by_centre, by_moment = leaf_tables(place, moment)
    top_tables(leaf, by_centre, by_moment, top_ref, centre_ref)
    top_in[col] = top_ref[...]
    pl.semaphore_wait(barrier, len(partners))

    first_copies = [
        pltpu.make_async_remote_copy(
            src_ref=top_ref,
            dst_ref=top_in.at[col],
            send_sem=top_send.at[k],
            recv_sem=top_recv.at[k],
            device_id=(row, other),
            device_id_type=MESH,
        )
        for k, other in enumerate(four)
    ]
    for copy in first_copies:
        copy.start()
    sides = []
    for part in range(6):
        sides.append(side_copy(0, part, before_ref, following))
        sides.append(side_copy(1, part, after_ref, preceding))
    for copy in sides:
        copy.start()

    leaf_sections(leaf, let_rows_ref, let_ref)
    sections = []
    for section in range(col_bits + row_bits):
        if section < col_bits:
            partner = (row, flip(col, section))
        else:
            partner = (flip(row, section - col_bits), col)
        sections.append(
            pltpu.make_async_remote_copy(
                src_ref=let_ref.at[section],
                dst_ref=let_in.at[section],
                send_sem=let_send.at[section],
                recv_sem=let_recv.at[section],
                device_id=partner,
                device_id_type=MESH,
            )
        )
    for copy in sections:
        copy.start()

    for copy in first_copies:
        copy.wait()
    mine = pl.ds(col // GROUP * GROUP, GROUP)
    second_copies = [
        pltpu.make_async_remote_copy(
            src_ref=top_in.at[mine],
            dst_ref=top_in.at[mine],
            send_sem=top_send.at[len(four) + k],
            recv_sem=top_recv.at[len(four) + k],
            device_id=(row, other),
            device_id_type=MESH,
        )
        for k, other in enumerate(groups)
    ]
    for copy in second_copies:
        copy.start()

    def build(group, carry):
        x = own_offsets(planes_ref, centre_ref, cells, group * 8)
        store_rows(feats, target_rows(x), group * 8, FAR_S)
        return carry

    lax.fori_loop(0, cells // 8, build, 0, unroll=2)
    for copy in second_copies:
        copy.wait()
    top_in[col] = jnp.zeros(top_ref.shape, F32)

    table = jnp.concatenate(
        [top_in[:, top, :] for top in range(2)] + [jnp.zeros((CELL - sources, CELL), F32)], axis=0
    )
    table = table.T
    entries = [table[k : k + 1, :] for k in range(15)]
    entries = [entries[i] - centre_ref[i : i + 1, :] for i in range(3)] + entries[3:]
    square, first, second, outputs = expansion_coefficients(entries)
    zero = jnp.zeros_like(entries[0])
    g = [[outputs[7 + SIX.index((min(i, j), max(i, j)))] for j in range(3)] for i in range(3)]
    bent = [(-outputs[13 + i], g[i], None) for i in range(3)]
    for position, form in enumerate([square, first, second] + bent):
        base = position * FAR_K
        for k, value in enumerate(source_rows(form, zero)):
            forms_rows[base + k : base + k + 1, :] = value
    for position in range(FORMS):
        value = forms_rows[position * FAR_K : (position + 1) * FAR_K, :].T
        for tile in range(sources // 8):
            start = (tile * FORMS + position) * 8
            forms_stage[start : start + 8, :] = value[tile * 8 : (tile + 1) * 8, :]
    forms[...] = forms_stage[...].astype(BF16)
    for k, value in enumerate(entries[:3] + outputs[4:7]):
        forms_rows[k : k + 1, :] = value
    columns = forms_rows[0:CELL, :].T
    for k in range(6):
        coeffs[k * sources : (k + 1) * sources, :] = jnp.broadcast_to(
            columns[:sources, k : k + 1], (sources, CELL)
        )

    def step(pair, carry):
        for sub in range(TOP_UNROLL):
            cell = 2 * (TOP_UNROLL * pair + sub)
            features = jnp.concatenate(
                [
                    feats[pl.ds(pl.multiple_of((cell + k) * FAR_S, FAR_S), FAR_K), :]
                    for k in range(2)
                ],
                axis=1,
            ).astype(BF16)
            values = jnp.dot(forms[...], features, preferred_element_type=F32)
            for k in range(2):
                totals = None
                for tile in range(sources // 8):
                    form = [
                        values[
                            (tile * FORMS + f) * 8 : (tile * FORMS + f + 1) * 8,
                            k * CELL : (k + 1) * CELL,
                        ]
                        for f in range(FORMS)
                    ]
                    const = [
                        coeffs[f * sources + tile * 8 : f * sources + (tile + 1) * 8, :]
                        for f in range(6)
                    ]
                    weight, three, five = weights_of(*form[:3])
                    terms = [weight] + [
                        const[i] * weight + const[3 + i] * three + form[3 + i] * five
                        for i in range(3)
                    ]
                    totals = terms if totals is None else [t + u for t, u in zip(totals, terms)]
                for place_, value in enumerate(totals):
                    sums[rows8((place_ * cells + cell + k) * 8), :] = value
        return carry

    lax.fori_loop(0, cells // (2 * TOP_UNROLL), step, 0)

    def finish_top(group, carry):
        x = own_offsets(planes_ref, centre_ref, cells, group * 8)
        totals = []
        for place_ in range(4):
            base = (place_ * cells + group * 8) * 8
            parts = [sums[pl.ds(base + k, 8, stride=8), :] for k in range(8)]
            while len(parts) > 1:
                parts = [parts[k] + parts[k + 1] for k in range(0, len(parts), 2)]
            totals.append(parts[0])
        for i in range(3):
            out_ref[rows8(i * pitch + group * 8), :] = x[i] * totals[0] - totals[1 + i]
        return carry

    lax.fori_loop(0, cells // 8, finish_top, 0, unroll=2)

    for copy in sections:
        copy.wait()
    for copy in sides:
        copy.wait()


def near_source_rows(y, moment):
    zero = jnp.zeros_like(y[0])
    one = jnp.ones_like(y[0])
    back = [split3(-2.0 * entry) for entry in y]
    square = split3(y[0] * y[0] + y[1] * y[1] + y[2] * y[2] + SOFTEN)
    scaled = [(3.0 * COUPLING) * entry for entry in moment]
    const = split3(-(y[0] * scaled[0] + y[1] * scaled[1] + y[2] * scaled[2]))
    scaled = [split3(entry) for entry in scaled]
    rows = []
    for part in range(3):
        rows += [one] + [b[part] for b in back] + [s[part] for s in scaled] + [const[part]]
    for part, source in ((0, 0), (1, 1), (2, 0)):
        rows += [square[part]] + [b[source] for b in back] + [s[source] for s in scaled] + [zero]
    return rows


def near_target_rows(x):
    one = jnp.ones_like(x[0])
    zero = jnp.zeros_like(x[0])
    norm = split3(x[0] * x[0] + x[1] * x[1] + x[2] * x[2])
    pieces = [split3(entry) for entry in x]
    rows = []
    for part in range(3):
        high = [p[0] for p in pieces]
        rows += [norm[part]] + high + high + [one]
    for target in (1, 1, 2):
        chosen = [p[target] for p in pieces]
        rows += [one] + chosen + chosen + [zero]
    return rows


def near_kernel(
    cells,
    devices,
    n_col,
    near_ref,
    own_ref,
    prev_ref,
    next_ref,
    centre_ref,
    far_ref,
    let_ref,
    top_ref,
    near_out,
    let_out,
    top_out,
    near_sources,
    near_targets,
    far_sources,
    far_coeffs,
    far_targets,
    masks,
    near_sums,
    far_sums,
    field,
):
    sublane = lax.broadcasted_iota(jnp.int32, (8, CELL), 0)
    lane = lax.broadcasted_iota(jnp.int32, (8, CELL), 1)
    diagonal = lax.broadcasted_iota(jnp.int32, (CELL, CELL), 0) == lax.broadcasted_iota(
        jnp.int32, (CELL, CELL), 1
    )
    masks[0:CELL, :] = jnp.zeros((CELL, CELL), F32)
    masks[CELL : 2 * CELL, :] = jnp.where(diagonal, 1e30, 0.0)

    def build_sources(ref, first, keep):
        def build(group, carry):
            y = own_offsets(ref, centre_ref, cells, group * 8)
            moment = [ref[rows8((3 + i) * pitch_of(cells) + group * 8), :] for i in range(3)]
            if keep is not None:
                moment = [jnp.where(keep, entry, 0.0) for entry in moment]
            store_rows(near_sources, near_source_rows(y, moment), first + group * 8, NEAR_S)
            return carry

        lax.fori_loop(0, cells // 8, build, 0, unroll=2)

    device = lax.axis_index("row") * n_col + lax.axis_index("col")
    ordinal = jnp.full((8, CELL), device, jnp.int32)
    build_sources(prev_ref, 0, ordinal > 0)
    build_sources(own_ref, cells, None)
    build_sources(next_ref, 2 * cells, ordinal < devices - 1)

    def build_targets(group, carry):
        x = own_offsets(own_ref, centre_ref, cells, group * 8)
        store_rows(near_targets, near_target_rows(x), group * 8, NEAR_S)
        store_rows(far_targets, target_rows(x), group * 8, FAR_S)
        return carry

    lax.fori_loop(0, cells // 8, build_targets, 0, unroll=2)

    groups = cells // 8
    lists = far_ref[...].astype(F32)
    lists = jnp.concatenate([lists, jnp.zeros((lists.shape[0], 256 - cells), F32)], axis=1)
    lists = jnp.concatenate([lists, jnp.zeros((CELL - lists.shape[0], 256), F32)], axis=0)
    far_sums[0:256, :] = lists.T
    repeated = jnp.bitwise_and(lax.broadcasted_iota(jnp.int32, (groups, CELL), 1), 15)
    slot = jnp.right_shift(lax.broadcasted_iota(jnp.int32, (groups, CELL), 1), 4)
    listed = jnp.zeros((groups, CELL), F32)
    for k in range(8):
        rows = far_sums[pl.ds(k, groups, stride=8), :]
        listed = jnp.where(slot == k, jnp.take_along_axis(rows, repeated, axis=1), listed)
    listed = listed.astype(jnp.int32)
    low = jnp.bitwise_and(listed, CELL - 1)
    section = jnp.right_shift(listed, 7)
    dense = []
    for entry in range(15):
        table = let_ref[pl.ds(entry, 8, stride=16), :]
        value = jnp.zeros(listed.shape, F32)
        for k in range(8):
            source = jnp.broadcast_to(table[k : k + 1, :], listed.shape)
            value = jnp.where(section == k, jnp.take_along_axis(source, low, axis=1), value)
        dense.append(value)
    repeat = sublane * 16 + jnp.bitwise_and(lane, 15)
    for entry in range(15):
        far_sums[entry * groups : (entry + 1) * groups, :] = dense[entry]

    def build_far(group, carry):
        table = [
            jnp.take_along_axis(
                jnp.broadcast_to(far_sums[pl.ds(entry * groups + group, 1), :], (8, CELL)),
                repeat,
                axis=1,
            )
            for entry in range(15)
        ]
        table = [table[i] - centre_ref[i : i + 1, :] for i in range(3)] + table[3:]
        square, first, second, outputs = expansion_coefficients(table)
        zero = jnp.zeros((8, CELL), F32)
        forms = [source_rows(form, zero) for form in (square, first, second)]
        rows = [
            jnp.where(lane < 16, a, jnp.where(lane < 32, b, c)) for a, b, c in zip(*forms)
        ]
        store_rows(far_sources, rows, group * 8, FAR_S)
        pieces = [split3(value) for value in outputs]
        rows = []
        for part in range(3):
            for k in range(OUT_K):
                kind = 0 if k < 4 else 1 if k < 7 else 2
                inside = (lane >= 32 * kind) & (lane < 32 * kind + 32)
                rows.append(jnp.where(inside, pieces[k][part], 0.0))
        store_rows(far_coeffs, rows, group * 8, COEF_S)
        return carry

    lax.fori_loop(0, groups, build_far, 0, unroll=2)

    upper_rows = lax.rem(lax.broadcasted_iota(jnp.int32, (NEAR_K, CELL), 0), 8) < 4

    def near_part(cell):
        targets = near_targets[pl.ds(pl.multiple_of(cell * NEAR_S, NEAR_S), NEAR_K), :]
        features = jnp.concatenate(
            [jnp.where(upper_rows, targets, 0.0), jnp.where(upper_rows, 0.0, targets)], axis=1
        ).astype(BF16)
        total = None
        for e in range(2):
            block = near_ref[e, cell]
            source = near_sources[pl.ds(pl.multiple_of(block * NEAR_S, NEAR_S), NEAR_K), :]
            values = jnp.dot(source.astype(BF16).T, features, preferred_element_type=F32)
            own = (block == cells + cell).astype(jnp.int32)
            mask = masks[pl.ds(pl.multiple_of(own * CELL, CELL), CELL), :]
            inverse = lax.rsqrt(values[:, :CELL] + mask)
            two = inverse * inverse
            three = two * inverse
            projected = values[:, CELL:] * two * three
            p_high, p_low = split2(projected)
            t_high, t_low = split2(three)
            weights = jnp.concatenate(
                [
                    jnp.concatenate([p_high, t_high], axis=1),
                    jnp.concatenate([p_low, t_low], axis=1),
                ],
                axis=0,
            )
            coeffs = source[:32].astype(BF16)
            result = jnp.dot(
                jnp.concatenate([coeffs, coeffs], axis=1), weights, preferred_element_type=F32
            )
            result = result[0:8] + result[8:16] + result[16:24]
            total = result if total is None else total + result
        near_sums[pl.ds(cell, 8, stride=pitch_of(cells)), :] = jnp.where(
            sublane < 4, total[:, :CELL], total[:, CELL:]
        )

    def far_part(cell):
        source = far_sources[pl.ds(pl.multiple_of(cell * FAR_S, FAR_S), FAR_K), :]
        features = far_targets[pl.ds(pl.multiple_of(cell * FAR_S, FAR_S), FAR_K), :].astype(BF16)
        values = jnp.dot(source.astype(BF16).T[:48], features, preferred_element_type=F32)
        parts = weights_of(values[:16], values[16:32], values[32:48])
        weights = jnp.concatenate([half for part in parts for half in split2(part)], axis=0)
        coeffs = far_coeffs[pl.ds(pl.multiple_of(cell * COEF_S, COEF_S), 48), :][:, :96].astype(BF16)
        result = jnp.dot(coeffs, weights, preferred_element_type=F32)
        result = result[:OUT_K] + result[OUT_K : 2 * OUT_K] + result[2 * OUT_K :]
        far_sums[pl.ds(cell, OUT_K, stride=pitch_of(cells)), :] = result

    def step(pair, carry):
        for sub in range(NEAR_UNROLL):
            near_part(NEAR_UNROLL * pair + sub)
            far_part(NEAR_UNROLL * pair + sub)
        return carry

    lax.fori_loop(0, cells // NEAR_UNROLL, step, 0)

    def finish_near(group, carry):
        x = own_offsets(own_ref, centre_ref, cells, group * 8)
        totals = [near_sums[rows8(k * pitch_of(cells) + group * 8), :] for k in range(7)]
        for i in range(3):
            field[rows8(i * pitch_of(cells) + group * 8), :] = (
                (x[i] * totals[0] - totals[4 + i]) * (1.0 / 3.0) + 0.5 * totals[1 + i]
            )
        return carry

    lax.fori_loop(0, cells // 8, finish_near, 0, unroll=2)
    planes_to_output(field, near_out, cells)

    def finish_far(group, carry):
        x = own_offsets(own_ref, centre_ref, cells, group * 8)
        totals = [far_sums[rows8(k * pitch_of(cells) + group * 8), :] for k in range(OUT_K)]
        for i, value in enumerate(expansion_fields(x, totals)):
            field[rows8(i * pitch_of(cells) + group * 8), :] = value
        return carry

    lax.fori_loop(0, cells // 8, finish_far, 0, unroll=2)
    planes_to_output(field, let_out, cells)
    planes_to_output(top_ref, top_out, cells)


def vmem(count):
    return [pl.BlockSpec(memory_space=pltpu.VMEM)] * count


def make_first(cells, n_row, n_col):
    bits = n_row.bit_length() + n_col.bit_length() - 2
    sources = 2 * n_col
    planes = jax.ShapeDtypeStruct((6 * pitch_of(cells), CELL), F32)
    return pl.pallas_call(
        functools.partial(first_kernel, cells, n_row, n_col),
        out_shape=(
            planes,
            planes,
            planes,
            jax.ShapeDtypeStruct((bits, 16, CELL), F32),
            jax.ShapeDtypeStruct((8, CELL), F32),
            jax.ShapeDtypeStruct((3 * pitch_of(cells), CELL), F32),
        ),
        in_specs=vmem(3),
        out_specs=tuple(
            vmem(1) + [pl.BlockSpec(memory_space=pl.ANY)] * 2 + vmem(3)
        ),
        scratch_shapes=[
            pltpu.VMEM((bits, 16, CELL), F32),
            pltpu.VMEM((8, CELL), F32),
            pltpu.VMEM((n_col, 8, CELL), F32),
            pltpu.VMEM((cells * FAR_S, CELL), F32),
            pltpu.VMEM((FORMS * FAR_K, CELL), F32),
            pltpu.VMEM((FORMS * sources, FAR_K), F32),
            pltpu.VMEM((FORMS * sources, FAR_K), BF16),
            pltpu.VMEM((6 * sources, CELL), F32),
            pltpu.VMEM((4 * cells * 8, CELL), F32),
            pltpu.SemaphoreType.DMA((12,)),
            pltpu.SemaphoreType.DMA((12,)),
            pltpu.SemaphoreType.DMA((bits,)),
            pltpu.SemaphoreType.DMA((bits,)),
            pltpu.SemaphoreType.DMA((n_col,)),
            pltpu.SemaphoreType.DMA((n_col,)),
        ],
        compiler_params=pltpu.CompilerParams(
            collective_id=0, has_side_effects=True, vmem_limit_bytes=VMEM_LIMIT
        ),
        cost_estimate=pl.CostEstimate(
            flops=8_000_000_000, bytes_accessed=4_000_000, transcendentals=1_600_000
        ),
        name="tables_exchange_top",
    )


def make_near(cells, devices, n_col, n):
    return pl.pallas_call(
        functools.partial(near_kernel, cells, devices, n_col),
        out_shape=(jax.ShapeDtypeStruct((3, n), F32),) * 3,
        in_specs=[pl.BlockSpec(memory_space=pltpu.SMEM)] + vmem(7),
        out_specs=tuple(vmem(3)),
        scratch_shapes=[
            pltpu.VMEM((3 * cells * NEAR_S, CELL), F32),
            pltpu.VMEM((cells * NEAR_S, CELL), F32),
            pltpu.VMEM((cells * FAR_S, CELL), F32),
            pltpu.VMEM((cells * COEF_S, CELL), F32),
            pltpu.VMEM((cells * FAR_S, CELL), F32),
            pltpu.VMEM((2 * CELL, CELL), F32),
            pltpu.VMEM((8 * pitch_of(cells), CELL), F32),
            pltpu.VMEM((OUT_K * pitch_of(cells), CELL), F32),
            pltpu.VMEM((3 * pitch_of(cells), CELL), F32),
        ],
        compiler_params=pltpu.CompilerParams(vmem_limit_bytes=VMEM_LIMIT),
        cost_estimate=pl.CostEstimate(
            flops=30_000_000_000, bytes_accessed=4_000_000, transcendentals=6_600_000
        ),
        name="near_and_let_field",
    )


def body(positions, moments, near_list, far_list, let_rows):
    n = positions.shape[1]
    cells = n // CELL
    n_row, n_col = lax.axis_size("row"), lax.axis_size("col")
    bits = let_rows.shape[1]
    planes, before, after, let_in, centre, top = make_first(cells, n_row, n_col)(
        positions, moments, let_rows
    )
    return make_near(cells, n_row * n_col, n_col, n)(
        near_list.T,
        planes,
        before,
        after,
        centre,
        far_list.T,
        let_in.reshape(bits * 16, CELL),
        top,
    )


def solution(mesh):
    return jax.shard_map(
        body,
        mesh=mesh,
        in_specs=(
            P(None, ("row", "col")),
            P(None, ("row", "col")),
            P(("row", "col"), None),
            P(("row", "col"), None),
            P(("row", "col"), None, None),
        ),
        out_specs=(P(None, ("row", "col")), P(None, ("row", "col")), P(None, ("row", "col"))),
        check_vma=False,
    )
```

```python
import functools

import jax
import jax.numpy as jnp
from jax import lax
from jax.experimental import pallas as pl
from jax.experimental.pallas import tpu as pltpu
from jax.sharding import PartitionSpec as P

CELL = 128
SOFTEN = 0.09
COUPLING = 0.004
F32 = jnp.float32
BF16 = jnp.bfloat16
MESH = pl.DeviceIdType.MESH
VMEM_LIMIT = 58 * 1024 * 1024
SIX = ((0, 0), (0, 1), (0, 2), (1, 1), (1, 2), (2, 2))
NEAR_K = 48
FAR_K = 64
OUT_K = 16
NEAR_S = 56
FAR_S = 72
COEF_S = 56
FORMS = 6
GROUP = 4
TOP_UNROLL = 24
NEAR_UNROLL = 48


def split3(value):
    high = value.astype(BF16).astype(F32)
    rest = value - high
    middle = rest.astype(BF16).astype(F32)
    return high, middle, rest - middle


def split2(value):
    high = value.astype(BF16)
    return high, (value - high.astype(F32)).astype(BF16)


def source_pairing(parts):
    return [parts[0], parts[1], parts[2], parts[0], parts[1], parts[0]]


def target_pairing(parts):
    return [parts[0], parts[0], parts[0], parts[1], parts[1], parts[2]]


def expansion_coefficients(table):
    c = table[0:3]
    m = [COUPLING * entry for entry in table[3:6]]
    q = [[COUPLING * table[6 + 3 * j + i] for i in range(3)] for j in range(3)]
    g = [[q[j][i] + q[i][j] for i in range(3)] for j in range(3)]
    t = q[0][0] + q[1][1] + q[2][2]
    gc = [g[i][0] * c[0] + g[i][1] * c[1] + g[i][2] * c[2] for i in range(3)]
    zero = jnp.zeros_like(c[0])
    one = jnp.ones_like(c[0])
    square = (
        c[0] * c[0] + c[1] * c[1] + c[2] * c[2] + SOFTEN,
        [-2.0 * c[i] for i in range(3)],
        [one if i == j else zero for i, j in SIX],
    )
    first = (
        -3.0 * (c[0] * m[0] + c[1] * m[1] + c[2] * m[2] + t),
        [3.0 * m[i] for i in range(3)],
        None,
    )
    second = (
        7.5 * (c[0] * gc[0] + c[1] * gc[1] + c[2] * gc[2]),
        [-15.0 * gc[i] for i in range(3)],
        [(7.5 if i == j else 15.0) * g[i][j] for i, j in SIX],
    )
    outputs = [one] + list(c) + m + [3.0 * g[i][j] for i, j in SIX] + [3.0 * gc[i] for i in range(3)]
    return square, first, second, outputs


def source_rows(form, zero):
    const, linear, quadratic = form
    rows = list(split3(const))
    for entry in linear:
        rows += source_pairing(split3(entry))
    if quadratic is None:
        rows += [zero] * 36
    else:
        for entry in quadratic:
            rows += source_pairing(split3(entry))
    return rows + [zero] * (FAR_K - len(rows))


def target_rows(x):
    one = jnp.ones_like(x[0])
    rows = [one, one, one]
    for entry in x:
        rows += target_pairing(split3(entry))
    for i, j in SIX:
        rows += target_pairing(split3(x[i] * x[j]))
    return rows + [jnp.zeros_like(one)] * (FAR_K - len(rows))


def weights_of(square, first, second):
    inverse = lax.rsqrt(square)
    two = inverse * inverse
    three = two * inverse
    five = three * two
    return five * (first + second * two), three, five


def expansion_fields(x, sums):
    g = {}
    for place, (i, j) in enumerate(SIX):
        g[i, j] = g[j, i] = sums[7 + place]
    return [
        x[i] * sums[0]
        - sums[1 + i]
        - sums[4 + i]
        - (g[i, 0] * x[0] + g[i, 1] * x[1] + g[i, 2] * x[2])
        + sums[13 + i]
        for i in range(3)
    ]


def pitch_of(cells):
    return cells + 8 * (1 - cells // 8 % 2)


def rows8(start):
    return pl.ds(pl.multiple_of(start, 8), 8)


def lanes(block):
    return pl.ds(pl.multiple_of(block * CELL, CELL), CELL)


def store_rows(ref, rows, first, stride):
    for place, value in enumerate(rows):
        ref[pl.ds(first * stride + place, 8, stride=stride), :] = value


def own_offsets(planes_ref, centre_ref, cells, start):
    return [
        planes_ref[rows8(i * pitch_of(cells) + start), :] - centre_ref[i : i + 1, :] for i in range(3)
    ]


def planes_to_output(planes_ref, out_ref, cells):
    def step(b, carry):
        out_ref[:, lanes(b)] = planes_ref[pl.ds(b, 3, stride=pitch_of(cells)), :]
        return carry

    lax.fori_loop(0, cells, step, 0, unroll=8)


def lane_iota(shape):
    return lax.broadcasted_iota(jnp.int32, shape, len(shape) - 1)


def spread_sums(planes, targets):
    total = None
    for plane, target in zip(planes, targets):
        parts = jnp.concatenate([part.astype(BF16) for part in split3(plane)], axis=1)
        marked = target(lane_iota((3 * CELL, CELL))).astype(F32).astype(BF16)
        value = jnp.dot(parts, marked, preferred_element_type=F32)
        total = value if total is None else total + value
    return total


def leaf_tables(place, moment):
    mean = 1.0 / CELL
    centres = [spread_sums([entry], [lambda l: l >= 0]) * mean for entry in place]
    spread = [entry - centre for entry, centre in zip(place, centres)]
    lane = lane_iota(centres[0].shape)
    table = spread_sums(
        moment + [spread[j] * moment[i] for j in range(3) for i in range(3)],
        [lambda l, k=k: l == 3 + k for k in range(12)],
    )
    inner = (lane >= 6) & (lane < 15)
    by_centre = jnp.zeros_like(table)
    for j in range(3):
        table = jnp.where(lane == j, centres[j], table)
        by_centre = jnp.where(inner & (lane // 3 == 2 + j), centres[j], by_centre)
    by_moment = spread_sums(
        moment,
        [lambda l, i=i: (l >= 6) & (l < 15) & (lax.rem(l, 3) == i) for i in range(3)],
    )
    return table, by_centre, by_moment


def leaf_sections(table, let_rows_ref, let_ref):
    cells = table.shape[0]
    rows = jnp.concatenate([table, jnp.zeros((256 - cells, CELL), F32)], axis=0).T
    chosen = let_rows_ref[0]
    low = jnp.bitwise_and(chosen, CELL - 1)
    upper = chosen >= CELL
    for entry in range(15):
        row = jnp.broadcast_to(rows[entry : entry + 1, :], (8, 256))
        let_ref[:, entry, :] = jnp.where(
            upper,
            jnp.take_along_axis(row[:, CELL:], low, axis=1),
            jnp.take_along_axis(row[:, :CELL], low, axis=1),
        )
    let_ref[:, 15, :] = jnp.zeros((8, CELL), F32)


def top_tables(table, by_centre, by_moment, top_ref, centre_ref):
    half = table.shape[0] // 2
    sublane = lax.broadcasted_iota(jnp.int32, (8, CELL), 0)
    lane = lane_iota((1, CELL))
    tile = jnp.zeros((8, CELL), F32)
    middle = jnp.zeros((1, CELL), F32)
    for top in range(2):
        part = slice(top * half, (top + 1) * half)
        total = jnp.sum(table[part], axis=0, keepdims=True)
        centre = jnp.sum(by_centre[part], axis=0, keepdims=True) * (1.0 / half)
        moved = jnp.sum((by_centre[part] - centre) * by_moment[part], axis=0, keepdims=True)
        row = jnp.where(lane < 3, total * (1.0 / half), total + moved)
        tile = jnp.where(sublane == top, row, tile)
        middle = middle + 0.5 * row
    top_ref[...] = tile
    for i in range(3):
        centre_ref[i : i + 1, :] = jnp.broadcast_to(middle[:, i : i + 1], (1, CELL))
    centre_ref[3:8, :] = jnp.zeros((5, CELL), F32)


def first_kernel(
    cells,
    n_row,
    n_col,
    pos_ref,
    mom_ref,
    let_rows_ref,
    planes_ref,
    before_ref,
    after_ref,
    let_in,
    centre_ref,
    out_ref,
    let_ref,
    top_ref,
    top_in,
    feats,
    forms_rows,
    forms_stage,
    forms,
    coeffs,
    sums,
    side_send,
    side_recv,
    let_send,
    let_recv,
    top_send,
    top_recv,
):
    row = lax.axis_index("row")
    col = lax.axis_index("col")
    device = row * n_col + col
    devices = n_row * n_col
    col_bits = n_col.bit_length() - 1
    row_bits = n_row.bit_length() - 1
    sources = 2 * n_col
    pitch = pitch_of(cells)

    def flip(value, bit):
        return value + (1 << bit) * (1 - 2 * lax.rem(value // (1 << bit), 2))

    def flip_by(value, mask):
        for bit in range(mask.bit_length()):
            if mask >> bit & 1:
                value = flip(value, bit)
        return value

    def place_of(index):
        return (index // n_col, lax.rem(index, n_col))

    following = place_of(lax.rem(device + 1, devices))
    preceding = place_of(lax.rem(device + devices - 1, devices))

    four = [flip_by(col, k) for k in range(1, GROUP)]
    groups = [flip_by(col, k * GROUP) for k in range(1, n_col // GROUP)]
    barrier = pltpu.get_barrier_semaphore()
    partners = [(row, other) for other in four + groups]
    partners += [(flip(row, bit), col) for bit in range(row_bits)] + [following, preceding]
    for partner in partners:
        pl.semaphore_signal(barrier, inc=1, device_id=partner, device_id_type=MESH)

    def to_planes(b, carry):
        planes_ref[pl.ds(b, 3, stride=pitch), :] = pos_ref[:, lanes(b)]
        planes_ref[pl.ds(3 * pitch + b, 3, stride=pitch), :] = mom_ref[:, lanes(b)]
        return carry

    lax.fori_loop(0, cells, to_planes, 0, unroll=8)

    def side_copy(side, part, target, to):
        rows = slice(part * pitch, (part + 1) * pitch)
        return pltpu.make_async_remote_copy(
            src_ref=planes_ref.at[rows],
            dst_ref=target.at[rows],
            send_sem=side_send.at[6 * side + part],
            recv_sem=side_recv.at[6 * side + part],
            device_id=to,
            device_id_type=MESH,
        )

    place = [planes_ref[i * pitch : i * pitch + cells, :] for i in range(3)]
    moment = [planes_ref[(3 + i) * pitch : (3 + i) * pitch + cells, :] for i in range(3)]
    leaf, by_centre, by_moment = leaf_tables(place, moment)
    top_tables(leaf, by_centre, by_moment, top_ref, centre_ref)
    top_in[col] = top_ref[...]
    pl.semaphore_wait(barrier, len(partners))

    first_copies = [
        pltpu.make_async_remote_copy(
            src_ref=top_ref,
            dst_ref=top_in.at[col],
            send_sem=top_send.at[k],
            recv_sem=top_recv.at[k],
            device_id=(row, other),
            device_id_type=MESH,
        )
        for k, other in enumerate(four)
    ]
    for copy in first_copies:
        copy.start()

    leaf_sections(leaf, let_rows_ref, let_ref)
    sections = []
    for section in range(col_bits + row_bits):
        if section < col_bits:
            partner = (row, flip(col, section))
        else:
            partner = (flip(row, section - col_bits), col)
        sections.append(
            pltpu.make_async_remote_copy(
                src_ref=let_ref.at[section],
                dst_ref=let_in.at[section],
                send_sem=let_send.at[section],
                recv_sem=let_recv.at[section],
                device_id=partner,
                device_id_type=MESH,
            )
        )
    for copy in sections:
        copy.start()

    for copy in first_copies:
        copy.wait()
    mine = pl.ds(col // GROUP * GROUP, GROUP)
    second_copies = [
        pltpu.make_async_remote_copy(
            src_ref=top_in.at[mine],
            dst_ref=top_in.at[mine],
            send_sem=top_send.at[len(four) + k],
            recv_sem=top_recv.at[len(four) + k],
            device_id=(row, other),
            device_id_type=MESH,
        )
        for k, other in enumerate(groups)
    ]
    for copy in second_copies:
        copy.start()

    def build(group, carry):
        x = own_offsets(planes_ref, centre_ref, cells, group * 8)
        store_rows(feats, target_rows(x), group * 8, FAR_S)
        return carry

    lax.fori_loop(0, cells // 8, build, 0, unroll=2)
    for copy in second_copies:
        copy.wait()
    sides = []
    for part in range(6):
        sides.append(side_copy(0, part, before_ref, following))
        sides.append(side_copy(1, part, after_ref, preceding))
    for copy in sides:
        copy.start()
    top_in[col] = jnp.zeros(top_ref.shape, F32)

    table = jnp.concatenate(
        [top_in[:, top, :] for top in range(2)] + [jnp.zeros((CELL - sources, CELL), F32)], axis=0
    )
    table = table.T
    entries = [table[k : k + 1, :] for k in range(15)]
    entries = [entries[i] - centre_ref[i : i + 1, :] for i in range(3)] + entries[3:]
    square, first, second, outputs = expansion_coefficients(entries)
    zero = jnp.zeros_like(entries[0])
    g = [[outputs[7 + SIX.index((min(i, j), max(i, j)))] for j in range(3)] for i in range(3)]
    bent = [(-outputs[13 + i], g[i], None) for i in range(3)]
    for position, form in enumerate([square, first, second] + bent):
        base = position * FAR_K
        for k, value in enumerate(source_rows(form, zero)):
            forms_rows[base + k : base + k + 1, :] = value
    for position in range(FORMS):
        value = forms_rows[position * FAR_K : (position + 1) * FAR_K, :].T
        for tile in range(sources // 8):
            start = (tile * FORMS + position) * 8
            forms_stage[start : start + 8, :] = value[tile * 8 : (tile + 1) * 8, :]
    forms[...] = forms_stage[...].astype(BF16)
    for k, value in enumerate(entries[:3] + outputs[4:7]):
        forms_rows[k : k + 1, :] = value
    columns = forms_rows[0:CELL, :].T
    for k in range(6):
        coeffs[k * sources : (k + 1) * sources, :] = jnp.broadcast_to(
            columns[:sources, k : k + 1], (sources, CELL)
        )

    def step(pair, carry):
        for sub in range(TOP_UNROLL):
            cell = 2 * (TOP_UNROLL * pair + sub)
            features = jnp.concatenate(
                [
                    feats[pl.ds(pl.multiple_of((cell + k) * FAR_S, FAR_S), FAR_K), :]
                    for k in range(2)
                ],
                axis=1,
            ).astype(BF16)
            values = jnp.dot(forms[...], features, preferred_element_type=F32)
            for k in range(2):
                totals = None
                for tile in range(sources // 8):
                    form = [
                        values[
                            (tile * FORMS + f) * 8 : (tile * FORMS + f + 1) * 8,
                            k * CELL : (k + 1) * CELL,
                        ]
                        for f in range(FORMS)
                    ]
                    const = [
                        coeffs[f * sources + tile * 8 : f * sources + (tile + 1) * 8, :]
                        for f in range(6)
                    ]
                    weight, three, five = weights_of(*form[:3])
                    terms = [weight] + [
                        const[i] * weight + const[3 + i] * three + form[3 + i] * five
                        for i in range(3)
                    ]
                    totals = terms if totals is None else [t + u for t, u in zip(totals, terms)]
                for place_, value in enumerate(totals):
                    sums[rows8((place_ * cells + cell + k) * 8), :] = value
        return carry

    lax.fori_loop(0, cells // (2 * TOP_UNROLL), step, 0)

    def finish_top(group, carry):
        x = own_offsets(planes_ref, centre_ref, cells, group * 8)
        totals = []
        for place_ in range(4):
            base = (place_ * cells + group * 8) * 8
            parts = [sums[pl.ds(base + k, 8, stride=8), :] for k in range(8)]
            while len(parts) > 1:
                parts = [parts[k] + parts[k + 1] for k in range(0, len(parts), 2)]
            totals.append(parts[0])
        for i in range(3):
            out_ref[rows8(i * pitch + group * 8), :] = x[i] * totals[0] - totals[1 + i]
        return carry

    lax.fori_loop(0, cells // 8, finish_top, 0, unroll=2)

    for copy in sections:
        copy.wait()
    for copy in sides:
        copy.wait()


def near_source_rows(y, moment):
    zero = jnp.zeros_like(y[0])
    one = jnp.ones_like(y[0])
    back = [split3(-2.0 * entry) for entry in y]
    square = split3(y[0] * y[0] + y[1] * y[1] + y[2] * y[2] + SOFTEN)
    scaled = [(3.0 * COUPLING) * entry for entry in moment]
    const = split3(-(y[0] * scaled[0] + y[1] * scaled[1] + y[2] * scaled[2]))
    scaled = [split3(entry) for entry in scaled]
    rows = []
    for part in range(3):
        rows += [one] + [b[part] for b in back] + [s[part] for s in scaled] + [const[part]]
    for part, source in ((0, 0), (1, 1), (2, 0)):
        rows += [square[part]] + [b[source] for b in back] + [s[source] for s in scaled] + [zero]
    return rows


def near_target_rows(x):
    one = jnp.ones_like(x[0])
    zero = jnp.zeros_like(x[0])
    norm = split3(x[0] * x[0] + x[1] * x[1] + x[2] * x[2])
    pieces = [split3(entry) for entry in x]
    rows = []
    for part in range(3):
        high = [p[0] for p in pieces]
        rows += [norm[part]] + high + high + [one]
    for target in (1, 1, 2):
        chosen = [p[target] for p in pieces]
        rows += [one] + chosen + chosen + [zero]
    return rows


def near_kernel(
    cells,
    devices,
    n_col,
    near_ref,
    own_ref,
    prev_ref,
    next_ref,
    centre_ref,
    far_ref,
    let_ref,
    top_ref,
    near_out,
    let_out,
    top_out,
    near_sources,
    near_targets,
    far_sources,
    far_coeffs,
    far_targets,
    masks,
    near_sums,
    far_sums,
    field,
):
    sublane = lax.broadcasted_iota(jnp.int32, (8, CELL), 0)
    lane = lax.broadcasted_iota(jnp.int32, (8, CELL), 1)
    diagonal = lax.broadcasted_iota(jnp.int32, (CELL, CELL), 0) == lax.broadcasted_iota(
        jnp.int32, (CELL, CELL), 1
    )
    masks[0:CELL, :] = jnp.zeros((CELL, CELL), F32)
    masks[CELL : 2 * CELL, :] = jnp.where(diagonal, 1e30, 0.0)

    def build_sources(ref, first, keep):
        def build(group, carry):
            y = own_offsets(ref, centre_ref, cells, group * 8)
            moment = [ref[rows8((3 + i) * pitch_of(cells) + group * 8), :] for i in range(3)]
            if keep is not None:
                moment = [jnp.where(keep, entry, 0.0) for entry in moment]
            store_rows(near_sources, near_source_rows(y, moment), first + group * 8, NEAR_S)
            return carry

        lax.fori_loop(0, cells // 8, build, 0, unroll=2)

    device = lax.axis_index("row") * n_col + lax.axis_index("col")
    ordinal = jnp.full((8, CELL), device, jnp.int32)
    build_sources(prev_ref, 0, ordinal > 0)
    build_sources(own_ref, cells, None)
    build_sources(next_ref, 2 * cells, ordinal < devices - 1)

    def build_targets(group, carry):
        x = own_offsets(own_ref, centre_ref, cells, group * 8)
        store_rows(near_targets, near_target_rows(x), group * 8, NEAR_S)
        store_rows(far_targets, target_rows(x), group * 8, FAR_S)
        return carry

    lax.fori_loop(0, cells // 8, build_targets, 0, unroll=2)

    groups = cells // 8
    lists = far_ref[...].astype(F32)
    lists = jnp.concatenate([lists, jnp.zeros((lists.shape[0], 256 - cells), F32)], axis=1)
    lists = jnp.concatenate([lists, jnp.zeros((CELL - lists.shape[0], 256), F32)], axis=0)
    far_sums[0:256, :] = lists.T
    repeated = jnp.bitwise_and(lax.broadcasted_iota(jnp.int32, (groups, CELL), 1), 15)
    slot = jnp.right_shift(lax.broadcasted_iota(jnp.int32, (groups, CELL), 1), 4)
    listed = jnp.zeros((groups, CELL), F32)
    for k in range(8):
        rows = far_sums[pl.ds(k, groups, stride=8), :]
        listed = jnp.where(slot == k, jnp.take_along_axis(rows, repeated, axis=1), listed)
    listed = listed.astype(jnp.int32)
    low = jnp.bitwise_and(listed, CELL - 1)
    section = jnp.right_shift(listed, 7)
    dense = []
    for entry in range(15):
        table = let_ref[pl.ds(entry, 8, stride=16), :]
        value = jnp.zeros(listed.shape, F32)
        for k in range(8):
            source = jnp.broadcast_to(table[k : k + 1, :], listed.shape)
            value = jnp.where(section == k, jnp.take_along_axis(source, low, axis=1), value)
        dense.append(value)
    repeat = sublane * 16 + jnp.bitwise_and(lane, 15)
    for entry in range(15):
        far_sums[entry * groups : (entry + 1) * groups, :] = dense[entry]

    def build_far(group, carry):
        table = [
            jnp.take_along_axis(
                jnp.broadcast_to(far_sums[pl.ds(entry * groups + group, 1), :], (8, CELL)),
                repeat,
                axis=1,
            )
            for entry in range(15)
        ]
        table = [table[i] - centre_ref[i : i + 1, :] for i in range(3)] + table[3:]
        square, first, second, outputs = expansion_coefficients(table)
        zero = jnp.zeros((8, CELL), F32)
        forms = [source_rows(form, zero) for form in (square, first, second)]
        rows = [
            jnp.where(lane < 16, a, jnp.where(lane < 32, b, c)) for a, b, c in zip(*forms)
        ]
        store_rows(far_sources, rows, group * 8, FAR_S)
        pieces = [split3(value) for value in outputs]
        rows = []
        for part in range(3):
            for k in range(OUT_K):
                kind = 0 if k < 4 else 1 if k < 7 else 2
                inside = (lane >= 32 * kind) & (lane < 32 * kind + 32)
                rows.append(jnp.where(inside, pieces[k][part], 0.0))
        store_rows(far_coeffs, rows, group * 8, COEF_S)
        return carry

    lax.fori_loop(0, groups, build_far, 0, unroll=2)

    upper_rows = lax.rem(lax.broadcasted_iota(jnp.int32, (NEAR_K, CELL), 0), 8) < 4

    def near_part(cell):
        targets = near_targets[pl.ds(pl.multiple_of(cell * NEAR_S, NEAR_S), NEAR_K), :]
        features = jnp.concatenate(
            [jnp.where(upper_rows, targets, 0.0), jnp.where(upper_rows, 0.0, targets)], axis=1
        ).astype(BF16)
        total = None
        for e in range(2):
            block = near_ref[e, cell]
            source = near_sources[pl.ds(pl.multiple_of(block * NEAR_S, NEAR_S), NEAR_K), :]
            values = jnp.dot(source.astype(BF16).T, features, preferred_element_type=F32)
            own = (block == cells + cell).astype(jnp.int32)
            mask = masks[pl.ds(pl.multiple_of(own * CELL, CELL), CELL), :]
            inverse = lax.rsqrt(values[:, :CELL] + mask)
            two = inverse * inverse
            three = two * inverse
            projected = values[:, CELL:] * two * three
            p_high, p_low = split2(projected)
            t_high, t_low = split2(three)
            weights = jnp.concatenate(
                [
                    jnp.concatenate([p_high, t_high], axis=1),
                    jnp.concatenate([p_low, t_low], axis=1),
                ],
                axis=0,
            )
            coeffs = source[:32].astype(BF16)
            result = jnp.dot(
                jnp.concatenate([coeffs, coeffs], axis=1), weights, preferred_element_type=F32
            )
            result = result[0:8] + result[8:16] + result[16:24]
            total = result if total is None else total + result
        near_sums[pl.ds(cell, 8, stride=pitch_of(cells)), :] = jnp.where(
            sublane < 4, total[:, :CELL], total[:, CELL:]
        )

    def far_part(cell):
        source = far_sources[pl.ds(pl.multiple_of(cell * FAR_S, FAR_S), FAR_K), :]
        features = far_targets[pl.ds(pl.multiple_of(cell * FAR_S, FAR_S), FAR_K), :].astype(BF16)
        values = jnp.dot(source.astype(BF16).T[:48], features, preferred_element_type=F32)
        parts = weights_of(values[:16], values[16:32], values[32:48])
        weights = jnp.concatenate([half for part in parts for half in split2(part)], axis=0)
        coeffs = far_coeffs[pl.ds(pl.multiple_of(cell * COEF_S, COEF_S), 48), :][:, :96].astype(BF16)
        result = jnp.dot(coeffs, weights, preferred_element_type=F32)
        result = result[:OUT_K] + result[OUT_K : 2 * OUT_K] + result[2 * OUT_K :]
        far_sums[pl.ds(cell, OUT_K, stride=pitch_of(cells)), :] = result

    def step(pair, carry):
        for sub in range(NEAR_UNROLL):
            near_part(NEAR_UNROLL * pair + sub)
            far_part(NEAR_UNROLL * pair + sub)
        return carry

    lax.fori_loop(0, cells // NEAR_UNROLL, step, 0)

    def finish_near(group, carry):
        x = own_offsets(own_ref, centre_ref, cells, group * 8)
        totals = [near_sums[rows8(k * pitch_of(cells) + group * 8), :] for k in range(7)]
        for i in range(3):
            field[rows8(i * pitch_of(cells) + group * 8), :] = (
                (x[i] * totals[0] - totals[4 + i]) * (1.0 / 3.0) + 0.5 * totals[1 + i]
            )
        return carry

    lax.fori_loop(0, cells // 8, finish_near, 0, unroll=2)
    planes_to_output(field, near_out, cells)

    def finish_far(group, carry):
        x = own_offsets(own_ref, centre_ref, cells, group * 8)
        totals = [far_sums[rows8(k * pitch_of(cells) + group * 8), :] for k in range(OUT_K)]
        for i, value in enumerate(expansion_fields(x, totals)):
            field[rows8(i * pitch_of(cells) + group * 8), :] = value
        return carry

    lax.fori_loop(0, cells // 8, finish_far, 0, unroll=2)
    planes_to_output(field, let_out, cells)
    planes_to_output(top_ref, top_out, cells)


def vmem(count):
    return [pl.BlockSpec(memory_space=pltpu.VMEM)] * count


def make_first(cells, n_row, n_col):
    bits = n_row.bit_length() + n_col.bit_length() - 2
    sources = 2 * n_col
    planes = jax.ShapeDtypeStruct((6 * pitch_of(cells), CELL), F32)
    return pl.pallas_call(
        functools.partial(first_kernel, cells, n_row, n_col),
        out_shape=(
            planes,
            planes,
            planes,
            jax.ShapeDtypeStruct((bits, 16, CELL), F32),
            jax.ShapeDtypeStruct((8, CELL), F32),
            jax.ShapeDtypeStruct((3 * pitch_of(cells), CELL), F32),
        ),
        in_specs=vmem(3),
        out_specs=tuple(
            vmem(1) + [pl.BlockSpec(memory_space=pl.ANY)] * 2 + vmem(3)
        ),
        scratch_shapes=[
            pltpu.VMEM((bits, 16, CELL), F32),
            pltpu.VMEM((8, CELL), F32),
            pltpu.VMEM((n_col, 8, CELL), F32),
            pltpu.VMEM((cells * FAR_S, CELL), F32),
            pltpu.VMEM((FORMS * FAR_K, CELL), F32),
            pltpu.VMEM((FORMS * sources, FAR_K), F32),
            pltpu.VMEM((FORMS * sources, FAR_K), BF16),
            pltpu.VMEM((6 * sources, CELL), F32),
            pltpu.VMEM((4 * cells * 8, CELL), F32),
            pltpu.SemaphoreType.DMA((12,)),
            pltpu.SemaphoreType.DMA((12,)),
            pltpu.SemaphoreType.DMA((bits,)),
            pltpu.SemaphoreType.DMA((bits,)),
            pltpu.SemaphoreType.DMA((n_col,)),
            pltpu.SemaphoreType.DMA((n_col,)),
        ],
        compiler_params=pltpu.CompilerParams(
            collective_id=0, has_side_effects=True, vmem_limit_bytes=VMEM_LIMIT
        ),
        cost_estimate=pl.CostEstimate(
            flops=8_000_000_000, bytes_accessed=4_000_000, transcendentals=1_600_000
        ),
        name="tables_exchange_top",
    )


def make_near(cells, devices, n_col, n):
    return pl.pallas_call(
        functools.partial(near_kernel, cells, devices, n_col),
        out_shape=(jax.ShapeDtypeStruct((3, n), F32),) * 3,
        in_specs=[pl.BlockSpec(memory_space=pltpu.SMEM)] + vmem(7),
        out_specs=tuple(vmem(3)),
        scratch_shapes=[
            pltpu.VMEM((3 * cells * NEAR_S, CELL), F32),
            pltpu.VMEM((cells * NEAR_S, CELL), F32),
            pltpu.VMEM((cells * FAR_S, CELL), F32),
            pltpu.VMEM((cells * COEF_S, CELL), F32),
            pltpu.VMEM((cells * FAR_S, CELL), F32),
            pltpu.VMEM((2 * CELL, CELL), F32),
            pltpu.VMEM((8 * pitch_of(cells), CELL), F32),
            pltpu.VMEM((OUT_K * pitch_of(cells), CELL), F32),
            pltpu.VMEM((3 * pitch_of(cells), CELL), F32),
        ],
        compiler_params=pltpu.CompilerParams(vmem_limit_bytes=VMEM_LIMIT),
        cost_estimate=pl.CostEstimate(
            flops=30_000_000_000, bytes_accessed=4_000_000, transcendentals=6_600_000
        ),
        name="near_and_let_field",
    )


def body(positions, moments, near_list, far_list, let_rows):
    n = positions.shape[1]
    cells = n // CELL
    n_row, n_col = lax.axis_size("row"), lax.axis_size("col")
    bits = let_rows.shape[1]
    planes, before, after, let_in, centre, top = make_first(cells, n_row, n_col)(
        positions, moments, let_rows
    )
    return make_near(cells, n_row * n_col, n_col, n)(
        near_list.T,
        planes,
        before,
        after,
        centre,
        far_list.T,
        let_in.reshape(bits * 16, CELL),
        top,
    )


def solution(mesh):
    return jax.shard_map(
        body,
        mesh=mesh,
        in_specs=(
            P(None, ("row", "col")),
            P(None, ("row", "col")),
            P(("row", "col"), None),
            P(("row", "col"), None),
            P(("row", "col"), None, None),
        ),
        out_specs=(P(None, ("row", "col")), P(None, ("row", "col")), P(None, ("row", "col"))),
        check_vma=False,
    )
```

```python
import functools

import jax
import jax.numpy as jnp
from jax import lax
from jax.experimental import pallas as pl
from jax.experimental.pallas import tpu as pltpu
from jax.sharding import PartitionSpec as P

CELL = 128
SOFTEN = 0.09
COUPLING = 0.004
F32 = jnp.float32
BF16 = jnp.bfloat16
MESH = pl.DeviceIdType.MESH
VMEM_LIMIT = 58 * 1024 * 1024
SIX = ((0, 0), (0, 1), (0, 2), (1, 1), (1, 2), (2, 2))
NEAR_K = 48
FAR_K = 64
OUT_K = 16
NEAR_S = 56
FAR_S = 72
COEF_S = 56
FORMS = 6
GROUP = 4
TOP_UNROLL = 24
NEAR_UNROLL = 48
FAR_UNROLL = 32


def split3(value):
    high = value.astype(BF16).astype(F32)
    rest = value - high
    middle = rest.astype(BF16).astype(F32)
    return high, middle, rest - middle


def split2(value):
    high = value.astype(BF16)
    return high, (value - high.astype(F32)).astype(BF16)


def source_pairing(parts):
    return [parts[0], parts[1], parts[2], parts[0], parts[1], parts[0]]


def target_pairing(parts):
    return [parts[0], parts[0], parts[0], parts[1], parts[1], parts[2]]


def expansion_coefficients(table):
    c = table[0:3]
    m = [COUPLING * entry for entry in table[3:6]]
    q = [[COUPLING * table[6 + 3 * j + i] for i in range(3)] for j in range(3)]
    g = [[q[j][i] + q[i][j] for i in range(3)] for j in range(3)]
    t = q[0][0] + q[1][1] + q[2][2]
    gc = [g[i][0] * c[0] + g[i][1] * c[1] + g[i][2] * c[2] for i in range(3)]
    zero = jnp.zeros_like(c[0])
    one = jnp.ones_like(c[0])
    square = (
        c[0] * c[0] + c[1] * c[1] + c[2] * c[2] + SOFTEN,
        [-2.0 * c[i] for i in range(3)],
        [one if i == j else zero for i, j in SIX],
    )
    first = (
        -3.0 * (c[0] * m[0] + c[1] * m[1] + c[2] * m[2] + t),
        [3.0 * m[i] for i in range(3)],
        None,
    )
    second = (
        7.5 * (c[0] * gc[0] + c[1] * gc[1] + c[2] * gc[2]),
        [-15.0 * gc[i] for i in range(3)],
        [(7.5 if i == j else 15.0) * g[i][j] for i, j in SIX],
    )
    outputs = [one] + list(c) + m + [3.0 * g[i][j] for i, j in SIX] + [3.0 * gc[i] for i in range(3)]
    return square, first, second, outputs


def source_rows(form, zero):
    const, linear, quadratic = form
    rows = list(split3(const))
    for entry in linear:
        rows += source_pairing(split3(entry))
    if quadratic is None:
        rows += [zero] * 36
    else:
        for entry in quadratic:
            rows += source_pairing(split3(entry))
    return rows + [zero] * (FAR_K - len(rows))


def target_rows(x):
    one = jnp.ones_like(x[0])
    rows = [one, one, one]
    for entry in x:
        rows += target_pairing(split3(entry))
    for i, j in SIX:
        rows += target_pairing(split3(x[i] * x[j]))
    return rows + [jnp.zeros_like(one)] * (FAR_K - len(rows))


def weights_of(square, first, second):
    inverse = lax.rsqrt(square)
    two = inverse * inverse
    three = two * inverse
    five = three * two
    return five * (first + second * two), three, five


def expansion_fields(x, sums):
    g = {}
    for place, (i, j) in enumerate(SIX):
        g[i, j] = g[j, i] = sums[7 + place]
    return [
        x[i] * sums[0]
        - sums[1 + i]
        - sums[4 + i]
        - (g[i, 0] * x[0] + g[i, 1] * x[1] + g[i, 2] * x[2])
        + sums[13 + i]
        for i in range(3)
    ]


def pitch_of(cells):
    return cells + 8 * (1 - cells // 8 % 2)


def rows8(start):
    return pl.ds(pl.multiple_of(start, 8), 8)


def lanes(block):
    return pl.ds(pl.multiple_of(block * CELL, CELL), CELL)


def store_rows(ref, rows, first, stride):
    for place, value in enumerate(rows):
        ref[pl.ds(first * stride + place, 8, stride=stride), :] = value


def own_offsets(planes_ref, centre_ref, cells, start):
    return [
        planes_ref[rows8(i * pitch_of(cells) + start), :] - centre_ref[i : i + 1, :] for i in range(3)
    ]


def planes_to_output(planes_ref, out_ref, cells):
    def step(b, carry):
        out_ref[:, lanes(b)] = planes_ref[pl.ds(b, 3, stride=pitch_of(cells)), :]
        return carry

    lax.fori_loop(0, cells, step, 0, unroll=8)


def lane_iota(shape):
    return lax.broadcasted_iota(jnp.int32, shape, len(shape) - 1)


def spread_sums(planes, targets):
    total = None
    for plane, target in zip(planes, targets):
        parts = jnp.concatenate([part.astype(BF16) for part in split3(plane)], axis=1)
        marked = target(lane_iota((3 * CELL, CELL))).astype(F32).astype(BF16)
        value = jnp.dot(parts, marked, preferred_element_type=F32)
        total = value if total is None else total + value
    return total


def leaf_tables(place, moment):
    mean = 1.0 / CELL
    centres = [spread_sums([entry], [lambda l: l >= 0]) * mean for entry in place]
    spread = [entry - centre for entry, centre in zip(place, centres)]
    lane = lane_iota(centres[0].shape)
    table = spread_sums(
        moment + [spread[j] * moment[i] for j in range(3) for i in range(3)],
        [lambda l, k=k: l == 3 + k for k in range(12)],
    )
    inner = (lane >= 6) & (lane < 15)
    by_centre = jnp.zeros_like(table)
    for j in range(3):
        table = jnp.where(lane == j, centres[j], table)
        by_centre = jnp.where(inner & (lane // 3 == 2 + j), centres[j], by_centre)
    by_moment = spread_sums(
        moment,
        [lambda l, i=i: (l >= 6) & (l < 15) & (lax.rem(l, 3) == i) for i in range(3)],
    )
    return table, by_centre, by_moment


def leaf_sections(table, let_rows_ref, let_ref):
    cells = table.shape[0]
    rows = jnp.concatenate([table, jnp.zeros((256 - cells, CELL), F32)], axis=0).T
    chosen = let_rows_ref[0]
    low = jnp.bitwise_and(chosen, CELL - 1)
    upper = chosen >= CELL
    for entry in range(15):
        row = jnp.broadcast_to(rows[entry : entry + 1, :], (8, 256))
        let_ref[:, entry, :] = jnp.where(
            upper,
            jnp.take_along_axis(row[:, CELL:], low, axis=1),
            jnp.take_along_axis(row[:, :CELL], low, axis=1),
        )
    let_ref[:, 15, :] = jnp.zeros((8, CELL), F32)


def top_tables(table, by_centre, by_moment, top_ref, centre_ref):
    half = table.shape[0] // 2
    sublane = lax.broadcasted_iota(jnp.int32, (8, CELL), 0)
    lane = lane_iota((1, CELL))
    tile = jnp.zeros((8, CELL), F32)
    middle = jnp.zeros((1, CELL), F32)
    for top in range(2):
        part = slice(top * half, (top + 1) * half)
        total = jnp.sum(table[part], axis=0, keepdims=True)
        centre = jnp.sum(by_centre[part], axis=0, keepdims=True) * (1.0 / half)
        moved = jnp.sum((by_centre[part] - centre) * by_moment[part], axis=0, keepdims=True)
        row = jnp.where(lane < 3, total * (1.0 / half), total + moved)
        tile = jnp.where(sublane == top, row, tile)
        middle = middle + 0.5 * row
    top_ref[...] = tile
    for i in range(3):
        centre_ref[i : i + 1, :] = jnp.broadcast_to(middle[:, i : i + 1], (1, CELL))
    centre_ref[3:8, :] = jnp.zeros((5, CELL), F32)


def first_kernel(
    cells,
    n_row,
    n_col,
    pos_ref,
    mom_ref,
    let_rows_ref,
    far_ref,
    planes_ref,
    before_ref,
    after_ref,
    centre_ref,
    let_out_ref,
    out_ref,
    let_in,
    let_ref,
    top_ref,
    top_in,
    feats,
    forms_rows,
    forms_stage,
    forms,
    coeffs,
    sums,
    far_sources,
    far_coeffs,
    far_sums,
    side_send,
    side_recv,
    let_send,
    let_recv,
    top_send,
    top_recv,
):
    row = lax.axis_index("row")
    col = lax.axis_index("col")
    device = row * n_col + col
    devices = n_row * n_col
    col_bits = n_col.bit_length() - 1
    row_bits = n_row.bit_length() - 1
    sources = 2 * n_col
    pitch = pitch_of(cells)

    def flip(value, bit):
        return value + (1 << bit) * (1 - 2 * lax.rem(value // (1 << bit), 2))

    def flip_by(value, mask):
        for bit in range(mask.bit_length()):
            if mask >> bit & 1:
                value = flip(value, bit)
        return value

    def place_of(index):
        return (index // n_col, lax.rem(index, n_col))

    following = place_of(lax.rem(device + 1, devices))
    preceding = place_of(lax.rem(device + devices - 1, devices))

    four = [flip_by(col, k) for k in range(1, GROUP)]
    groups = [flip_by(col, k * GROUP) for k in range(1, n_col // GROUP)]
    barrier = pltpu.get_barrier_semaphore()
    partners = [(row, other) for other in four + groups]
    partners += [(flip(row, bit), col) for bit in range(row_bits)] + [following, preceding]
    for partner in partners:
        pl.semaphore_signal(barrier, inc=1, device_id=partner, device_id_type=MESH)

    def to_planes(b, carry):
        planes_ref[pl.ds(b, 3, stride=pitch), :] = pos_ref[:, lanes(b)]
        planes_ref[pl.ds(3 * pitch + b, 3, stride=pitch), :] = mom_ref[:, lanes(b)]
        return carry

    lax.fori_loop(0, cells, to_planes, 0, unroll=8)

    def side_copy(side, part, target, to):
        rows = slice(part * pitch, (part + 1) * pitch)
        return pltpu.make_async_remote_copy(
            src_ref=planes_ref.at[rows],
            dst_ref=target.at[rows],
            send_sem=side_send.at[6 * side + part],
            recv_sem=side_recv.at[6 * side + part],
            device_id=to,
            device_id_type=MESH,
        )

    place = [planes_ref[i * pitch : i * pitch + cells, :] for i in range(3)]
    moment = [planes_ref[(3 + i) * pitch : (3 + i) * pitch + cells, :] for i in range(3)]
    leaf, by_centre, by_moment = leaf_tables(place, moment)
    top_tables(leaf, by_centre, by_moment, top_ref, centre_ref)
    top_in[col] = top_ref[...]
    pl.semaphore_wait(barrier, len(partners))

    first_copies = [
        pltpu.make_async_remote_copy(
            src_ref=top_ref,
            dst_ref=top_in.at[col],
            send_sem=top_send.at[k],
            recv_sem=top_recv.at[k],
            device_id=(row, other),
            device_id_type=MESH,
        )
        for k, other in enumerate(four)
    ]
    for copy in first_copies:
        copy.start()

    leaf_sections(leaf, let_rows_ref, let_ref)
    sections = []
    for section in range(col_bits + row_bits):
        if section < col_bits:
            partner = (row, flip(col, section))
        else:
            partner = (flip(row, section - col_bits), col)
        sections.append(
            pltpu.make_async_remote_copy(
                src_ref=let_ref.at[section],
                dst_ref=let_in.at[section],
                send_sem=let_send.at[section],
                recv_sem=let_recv.at[section],
                device_id=partner,
                device_id_type=MESH,
            )
        )
    for copy in sections:
        copy.start()

    for copy in first_copies:
        copy.wait()
    mine = pl.ds(col // GROUP * GROUP, GROUP)
    second_copies = [
        pltpu.make_async_remote_copy(
            src_ref=top_in.at[mine],
            dst_ref=top_in.at[mine],
            send_sem=top_send.at[len(four) + k],
            recv_sem=top_recv.at[len(four) + k],
            device_id=(row, other),
            device_id_type=MESH,
        )
        for k, other in enumerate(groups)
    ]
    for copy in second_copies:
        copy.start()

    def build(group, carry):
        x = own_offsets(planes_ref, centre_ref, cells, group * 8)
        store_rows(feats, target_rows(x), group * 8, FAR_S)
        return carry

    lax.fori_loop(0, cells // 8, build, 0, unroll=2)
    for copy in second_copies:
        copy.wait()
    sides = []
    for part in range(6):
        sides.append(side_copy(0, part, before_ref, following))
        sides.append(side_copy(1, part, after_ref, preceding))
    for copy in sides:
        copy.start()
    top_in[col] = jnp.zeros(top_ref.shape, F32)

    table = jnp.concatenate(
        [top_in[:, top, :] for top in range(2)] + [jnp.zeros((CELL - sources, CELL), F32)], axis=0
    )
    table = table.T
    entries = [table[k : k + 1, :] for k in range(15)]
    entries = [entries[i] - centre_ref[i : i + 1, :] for i in range(3)] + entries[3:]
    square, first, second, outputs = expansion_coefficients(entries)
    zero = jnp.zeros_like(entries[0])
    g = [[outputs[7 + SIX.index((min(i, j), max(i, j)))] for j in range(3)] for i in range(3)]
    bent = [(-outputs[13 + i], g[i], None) for i in range(3)]
    for position, form in enumerate([square, first, second] + bent):
        base = position * FAR_K
        for k, value in enumerate(source_rows(form, zero)):
            forms_rows[base + k : base + k + 1, :] = value
    for position in range(FORMS):
        value = forms_rows[position * FAR_K : (position + 1) * FAR_K, :].T
        for tile in range(sources // 8):
            start = (tile * FORMS + position) * 8
            forms_stage[start : start + 8, :] = value[tile * 8 : (tile + 1) * 8, :]
    forms[...] = forms_stage[...].astype(BF16)
    for k, value in enumerate(entries[:3] + outputs[4:7]):
        forms_rows[k : k + 1, :] = value
    columns = forms_rows[0:CELL, :].T
    for k in range(6):
        coeffs[k * sources : (k + 1) * sources, :] = jnp.broadcast_to(
            columns[:sources, k : k + 1], (sources, CELL)
        )

    def step(pair, carry):
        for sub in range(TOP_UNROLL):
            cell = 2 * (TOP_UNROLL * pair + sub)
            features = jnp.concatenate(
                [
                    feats[pl.ds(pl.multiple_of((cell + k) * FAR_S, FAR_S), FAR_K), :]
                    for k in range(2)
                ],
                axis=1,
            ).astype(BF16)
            values = jnp.dot(forms[...], features, preferred_element_type=F32)
            for k in range(2):
                totals = None
                for tile in range(sources // 8):
                    form = [
                        values[
                            (tile * FORMS + f) * 8 : (tile * FORMS + f + 1) * 8,
                            k * CELL : (k + 1) * CELL,
                        ]
                        for f in range(FORMS)
                    ]
                    const = [
                        coeffs[f * sources + tile * 8 : f * sources + (tile + 1) * 8, :]
                        for f in range(6)
                    ]
                    weight, three, five = weights_of(*form[:3])
                    terms = [weight] + [
                        const[i] * weight + const[3 + i] * three + form[3 + i] * five
                        for i in range(3)
                    ]
                    totals = terms if totals is None else [t + u for t, u in zip(totals, terms)]
                for place_, value in enumerate(totals):
                    sums[rows8((place_ * cells + cell + k) * 8), :] = value
        return carry

    lax.fori_loop(0, cells // (2 * TOP_UNROLL), step, 0)

    for copy in sections:
        copy.wait()
    sublane = lax.broadcasted_iota(jnp.int32, (8, CELL), 0)
    lane = lax.broadcasted_iota(jnp.int32, (8, CELL), 1)

    groups = cells // 8
    lists = far_ref[...].astype(F32)
    lists = jnp.concatenate([lists, jnp.zeros((lists.shape[0], 256 - cells), F32)], axis=1)
    lists = jnp.concatenate([lists, jnp.zeros((CELL - lists.shape[0], 256), F32)], axis=0)
    far_sums[0:256, :] = lists.T
    repeated = jnp.bitwise_and(lax.broadcasted_iota(jnp.int32, (groups, CELL), 1), 15)
    slot = jnp.right_shift(lax.broadcasted_iota(jnp.int32, (groups, CELL), 1), 4)
    listed = jnp.zeros((groups, CELL), F32)
    for k in range(8):
        rows = far_sums[pl.ds(k, groups, stride=8), :]
        listed = jnp.where(slot == k, jnp.take_along_axis(rows, repeated, axis=1), listed)
    listed = listed.astype(jnp.int32)
    low = jnp.bitwise_and(listed, CELL - 1)
    section = jnp.right_shift(listed, 7)
    dense = []
    for entry in range(15):
        table = let_in[:, entry, :]
        value = jnp.zeros(listed.shape, F32)
        for k in range(8):
            source = jnp.broadcast_to(table[k : k + 1, :], listed.shape)
            value = jnp.where(section == k, jnp.take_along_axis(source, low, axis=1), value)
        dense.append(value)
    repeat = sublane * 16 + jnp.bitwise_and(lane, 15)
    for entry in range(15):
        far_sums[entry * groups : (entry + 1) * groups, :] = dense[entry]

    def build_far(group, carry):
        table = [
            jnp.take_along_axis(
                jnp.broadcast_to(far_sums[pl.ds(entry * groups + group, 1), :], (8, CELL)),
                repeat,
                axis=1,
            )
            for entry in range(15)
        ]
        table = [table[i] - centre_ref[i : i + 1, :] for i in range(3)] + table[3:]
        square, first, second, outputs = expansion_coefficients(table)
        zero = jnp.zeros((8, CELL), F32)
        forms = [source_rows(form, zero) for form in (square, first, second)]
        rows = [
            jnp.where(lane < 16, a, jnp.where(lane < 32, b, c)) for a, b, c in zip(*forms)
        ]
        store_rows(far_sources, rows, group * 8, FAR_S)
        pieces = [split3(value) for value in outputs]
        rows = []
        for part in range(3):
            for k in range(OUT_K):
                kind = 0 if k < 4 else 1 if k < 7 else 2
                inside = (lane >= 32 * kind) & (lane < 32 * kind + 32)
                rows.append(jnp.where(inside, pieces[k][part], 0.0))
        store_rows(far_coeffs, rows, group * 8, COEF_S)
        return carry

    lax.fori_loop(0, groups, build_far, 0, unroll=2)

    def far_part(cell):
        source = far_sources[pl.ds(pl.multiple_of(cell * FAR_S, FAR_S), FAR_K), :]
        features = feats[pl.ds(pl.multiple_of(cell * FAR_S, FAR_S), FAR_K), :].astype(BF16)
        values = jnp.dot(source.astype(BF16).T[:48], features, preferred_element_type=F32)
        parts = weights_of(values[:16], values[16:32], values[32:48])
        weights = jnp.concatenate([half for part in parts for half in split2(part)], axis=0)
        coeffs = far_coeffs[pl.ds(pl.multiple_of(cell * COEF_S, COEF_S), 48), :][:, :96].astype(BF16)
        result = jnp.dot(coeffs, weights, preferred_element_type=F32)
        result = result[:OUT_K] + result[OUT_K : 2 * OUT_K] + result[2 * OUT_K :]
        far_sums[pl.ds(cell, OUT_K, stride=pitch_of(cells)), :] = result

    def finish_top(group, carry):
        x = own_offsets(planes_ref, centre_ref, cells, group * 8)
        totals = []
        for place_ in range(4):
            base = (place_ * cells + group * 8) * 8
            parts = [sums[pl.ds(base + k, 8, stride=8), :] for k in range(8)]
            while len(parts) > 1:
                parts = [parts[k] + parts[k + 1] for k in range(0, len(parts), 2)]
            totals.append(parts[0])
        for i in range(3):
            out_ref[rows8(i * pitch + group * 8), :] = x[i] * totals[0] - totals[1 + i]
        return carry

    lax.fori_loop(0, cells // 8, finish_top, 0, unroll=2)

    def far_step(part, carry):
        for sub in range(FAR_UNROLL):
            far_part(FAR_UNROLL * part + sub)
        return carry

    lax.fori_loop(0, cells // FAR_UNROLL, far_step, 0)

    def finish_far(group, carry):
        x = own_offsets(planes_ref, centre_ref, cells, group * 8)
        totals = [far_sums[rows8(k * pitch_of(cells) + group * 8), :] for k in range(OUT_K)]
        for i, value in enumerate(expansion_fields(x, totals)):
            let_out_ref[rows8(i * pitch_of(cells) + group * 8), :] = value
        return carry

    lax.fori_loop(0, cells // 8, finish_far, 0, unroll=2)
    for copy in sides:
        copy.wait()


def near_source_rows(y, moment):
    zero = jnp.zeros_like(y[0])
    one = jnp.ones_like(y[0])
    back = [split3(-2.0 * entry) for entry in y]
    square = split3(y[0] * y[0] + y[1] * y[1] + y[2] * y[2] + SOFTEN)
    scaled = [(3.0 * COUPLING) * entry for entry in moment]
    const = split3(-(y[0] * scaled[0] + y[1] * scaled[1] + y[2] * scaled[2]))
    scaled = [split3(entry) for entry in scaled]
    rows = []
    for part in range(3):
        rows += [one] + [b[part] for b in back] + [s[part] for s in scaled] + [const[part]]
    for part, source in ((0, 0), (1, 1), (2, 0)):
        rows += [square[part]] + [b[source] for b in back] + [s[source] for s in scaled] + [zero]
    return rows


def near_target_rows(x):
    one = jnp.ones_like(x[0])
    zero = jnp.zeros_like(x[0])
    norm = split3(x[0] * x[0] + x[1] * x[1] + x[2] * x[2])
    pieces = [split3(entry) for entry in x]
    rows = []
    for part in range(3):
        high = [p[0] for p in pieces]
        rows += [norm[part]] + high + high + [one]
    for target in (1, 1, 2):
        chosen = [p[target] for p in pieces]
        rows += [one] + chosen + chosen + [zero]
    return rows


def near_kernel(
    cells,
    devices,
    n_col,
    near_ref,
    own_ref,
    prev_ref,
    next_ref,
    centre_ref,
    let_planes_ref,
    top_ref,
    near_out,
    let_out,
    top_out,
    near_sources,
    near_targets,
    masks,
    near_sums,
    field,
):
    sublane = lax.broadcasted_iota(jnp.int32, (8, CELL), 0)
    diagonal = lax.broadcasted_iota(jnp.int32, (CELL, CELL), 0) == lax.broadcasted_iota(
        jnp.int32, (CELL, CELL), 1
    )
    masks[0:CELL, :] = jnp.zeros((CELL, CELL), F32)
    masks[CELL : 2 * CELL, :] = jnp.where(diagonal, 1e30, 0.0)

    def build_sources(ref, first, keep):
        def build(group, carry):
            y = own_offsets(ref, centre_ref, cells, group * 8)
            moment = [ref[rows8((3 + i) * pitch_of(cells) + group * 8), :] for i in range(3)]
            if keep is not None:
                moment = [jnp.where(keep, entry, 0.0) for entry in moment]
            store_rows(near_sources, near_source_rows(y, moment), first + group * 8, NEAR_S)
            return carry

        lax.fori_loop(0, cells // 8, build, 0, unroll=2)

    device = lax.axis_index("row") * n_col + lax.axis_index("col")
    ordinal = jnp.full((8, CELL), device, jnp.int32)
    build_sources(prev_ref, 0, ordinal > 0)
    build_sources(own_ref, cells, None)
    build_sources(next_ref, 2 * cells, ordinal < devices - 1)

    def build_targets(group, carry):
        x = own_offsets(own_ref, centre_ref, cells, group * 8)
        store_rows(near_targets, near_target_rows(x), group * 8, NEAR_S)
        return carry

    lax.fori_loop(0, cells // 8, build_targets, 0, unroll=2)

    upper_rows = lax.rem(lax.broadcasted_iota(jnp.int32, (NEAR_K, CELL), 0), 8) < 4

    def near_part(cell):
        targets = near_targets[pl.ds(pl.multiple_of(cell * NEAR_S, NEAR_S), NEAR_K), :]
        features = jnp.concatenate(
            [jnp.where(upper_rows, targets, 0.0), jnp.where(upper_rows, 0.0, targets)], axis=1
        ).astype(BF16)
        total = None
        for e in range(2):
            block = near_ref[e, cell]
            source = near_sources[pl.ds(pl.multiple_of(block * NEAR_S, NEAR_S), NEAR_K), :]
            values = jnp.dot(source.astype(BF16).T, features, preferred_element_type=F32)
            own = (block == cells + cell).astype(jnp.int32)
            mask = masks[pl.ds(pl.multiple_of(own * CELL, CELL), CELL), :]
            inverse = lax.rsqrt(values[:, :CELL] + mask)
            two = inverse * inverse
            three = two * inverse
            projected = values[:, CELL:] * two * three
            p_high, p_low = split2(projected)
            t_high, t_low = split2(three)
            weights = jnp.concatenate(
                [
                    jnp.concatenate([p_high, t_high], axis=1),
                    jnp.concatenate([p_low, t_low], axis=1),
                ],
                axis=0,
            )
            coeffs = source[:32].astype(BF16)
            result = jnp.dot(
                jnp.concatenate([coeffs, coeffs], axis=1), weights, preferred_element_type=F32
            )
            result = result[0:8] + result[8:16] + result[16:24]
            total = result if total is None else total + result
        near_sums[pl.ds(cell, 8, stride=pitch_of(cells)), :] = jnp.where(
            sublane < 4, total[:, :CELL], total[:, CELL:]
        )

    def step(pair, carry):
        for sub in range(NEAR_UNROLL):
            near_part(NEAR_UNROLL * pair + sub)
        return carry

    lax.fori_loop(0, cells // NEAR_UNROLL, step, 0)

    def finish_near(group, carry):
        x = own_offsets(own_ref, centre_ref, cells, group * 8)
        totals = [near_sums[rows8(k * pitch_of(cells) + group * 8), :] for k in range(7)]
        for i in range(3):
            field[rows8(i * pitch_of(cells) + group * 8), :] = (
                (x[i] * totals[0] - totals[4 + i]) * (1.0 / 3.0) + 0.5 * totals[1 + i]
            )
        return carry

    lax.fori_loop(0, cells // 8, finish_near, 0, unroll=2)
    planes_to_output(field, near_out, cells)

    planes_to_output(let_planes_ref, let_out, cells)
    planes_to_output(top_ref, top_out, cells)


def vmem(count):
    return [pl.BlockSpec(memory_space=pltpu.VMEM)] * count


def make_first(cells, n_row, n_col):
    bits = n_row.bit_length() + n_col.bit_length() - 2
    sources = 2 * n_col
    planes = jax.ShapeDtypeStruct((6 * pitch_of(cells), CELL), F32)
    return pl.pallas_call(
        functools.partial(first_kernel, cells, n_row, n_col),
        out_shape=(
            planes,
            planes,
            planes,
            jax.ShapeDtypeStruct((8, CELL), F32),
            jax.ShapeDtypeStruct((3 * pitch_of(cells), CELL), F32),
            jax.ShapeDtypeStruct((3 * pitch_of(cells), CELL), F32),
        ),
        in_specs=vmem(4),
        out_specs=tuple(
            vmem(1) + [pl.BlockSpec(memory_space=pl.ANY)] * 2 + vmem(3)
        ),
        scratch_shapes=[
            pltpu.VMEM((bits, 16, CELL), F32),
            pltpu.VMEM((bits, 16, CELL), F32),
            pltpu.VMEM((8, CELL), F32),
            pltpu.VMEM((n_col, 8, CELL), F32),
            pltpu.VMEM((cells * FAR_S, CELL), F32),
            pltpu.VMEM((FORMS * FAR_K, CELL), F32),
            pltpu.VMEM((FORMS * sources, FAR_K), F32),
            pltpu.VMEM((FORMS * sources, FAR_K), BF16),
            pltpu.VMEM((6 * sources, CELL), F32),
            pltpu.VMEM((4 * cells * 8, CELL), F32),
            pltpu.VMEM((cells * FAR_S, CELL), F32),
            pltpu.VMEM((cells * COEF_S, CELL), F32),
            pltpu.VMEM((OUT_K * pitch_of(cells), CELL), F32),
            pltpu.SemaphoreType.DMA((12,)),
            pltpu.SemaphoreType.DMA((12,)),
            pltpu.SemaphoreType.DMA((bits,)),
            pltpu.SemaphoreType.DMA((bits,)),
            pltpu.SemaphoreType.DMA((n_col,)),
            pltpu.SemaphoreType.DMA((n_col,)),
        ],
        compiler_params=pltpu.CompilerParams(
            collective_id=0, has_side_effects=True, vmem_limit_bytes=VMEM_LIMIT
        ),
        cost_estimate=pl.CostEstimate(
            flops=8_000_000_000, bytes_accessed=4_000_000, transcendentals=1_600_000
        ),
        name="tables_exchange_top",
    )


def make_near(cells, devices, n_col, n):
    return pl.pallas_call(
        functools.partial(near_kernel, cells, devices, n_col),
        out_shape=(jax.ShapeDtypeStruct((3, n), F32),) * 3,
        in_specs=[pl.BlockSpec(memory_space=pltpu.SMEM)] + vmem(6),
        out_specs=tuple(vmem(3)),
        scratch_shapes=[
            pltpu.VMEM((3 * cells * NEAR_S, CELL), F32),
            pltpu.VMEM((cells * NEAR_S, CELL), F32),
            pltpu.VMEM((2 * CELL, CELL), F32),
            pltpu.VMEM((8 * pitch_of(cells), CELL), F32),
            pltpu.VMEM((3 * pitch_of(cells), CELL), F32),
        ],
        compiler_params=pltpu.CompilerParams(vmem_limit_bytes=VMEM_LIMIT),
        cost_estimate=pl.CostEstimate(
            flops=30_000_000_000, bytes_accessed=4_000_000, transcendentals=6_600_000
        ),
        name="near_and_let_field",
    )


def body(positions, moments, near_list, far_list, let_rows):
    n = positions.shape[1]
    cells = n // CELL
    n_row, n_col = lax.axis_size("row"), lax.axis_size("col")
    planes, before, after, centre, remote, top = make_first(cells, n_row, n_col)(
        positions, moments, let_rows, far_list.T
    )
    return make_near(cells, n_row * n_col, n_col, n)(
        near_list.T,
        planes,
        before,
        after,
        centre,
        remote,
        top,
    )


def solution(mesh):
    return jax.shard_map(
        body,
        mesh=mesh,
        in_specs=(
            P(None, ("row", "col")),
            P(None, ("row", "col")),
            P(("row", "col"), None),
            P(("row", "col"), None),
            P(("row", "col"), None, None),
        ),
        out_specs=(P(None, ("row", "col")), P(None, ("row", "col")), P(None, ("row", "col"))),
        check_vma=False,
    )
```

```python
import functools

import jax
import jax.numpy as jnp
from jax import lax
from jax.experimental import pallas as pl
from jax.experimental.pallas import tpu as pltpu
from jax.sharding import PartitionSpec as P

CELL = 128
SOFTEN = 0.09
COUPLING = 0.004
F32 = jnp.float32
BF16 = jnp.bfloat16
MESH = pl.DeviceIdType.MESH
VMEM_LIMIT = 58 * 1024 * 1024
SIX = ((0, 0), (0, 1), (0, 2), (1, 1), (1, 2), (2, 2))
NEAR_K = 48
FAR_K = 64
OUT_K = 16
NEAR_S = 56
FAR_S = 72
COEF_S = 56
FORMS = 6
GROUP = 4
TOP_UNROLL = 24
NEAR_UNROLL = 48
FAR_UNROLL = 32


def split3(value):
    high = value.astype(BF16).astype(F32)
    rest = value - high
    middle = rest.astype(BF16).astype(F32)
    return high, middle, rest - middle


def split2(value):
    high = value.astype(BF16)
    return high, (value - high.astype(F32)).astype(BF16)


def source_pairing(parts):
    return [parts[0], parts[1], parts[2], parts[0], parts[1], parts[0]]


def target_pairing(parts):
    return [parts[0], parts[0], parts[0], parts[1], parts[1], parts[2]]


def expansion_coefficients(table):
    c = table[0:3]
    m = [COUPLING * entry for entry in table[3:6]]
    q = [[COUPLING * table[6 + 3 * j + i] for i in range(3)] for j in range(3)]
    g = [[q[j][i] + q[i][j] for i in range(3)] for j in range(3)]
    t = q[0][0] + q[1][1] + q[2][2]
    gc = [g[i][0] * c[0] + g[i][1] * c[1] + g[i][2] * c[2] for i in range(3)]
    zero = jnp.zeros_like(c[0])
    one = jnp.ones_like(c[0])
    square = (
        c[0] * c[0] + c[1] * c[1] + c[2] * c[2] + SOFTEN,
        [-2.0 * c[i] for i in range(3)],
        [one if i == j else zero for i, j in SIX],
    )
    first = (
        -3.0 * (c[0] * m[0] + c[1] * m[1] + c[2] * m[2] + t),
        [3.0 * m[i] for i in range(3)],
        None,
    )
    second = (
        7.5 * (c[0] * gc[0] + c[1] * gc[1] + c[2] * gc[2]),
        [-15.0 * gc[i] for i in range(3)],
        [(7.5 if i == j else 15.0) * g[i][j] for i, j in SIX],
    )
    outputs = [one] + list(c) + m + [3.0 * g[i][j] for i, j in SIX] + [3.0 * gc[i] for i in range(3)]
    return square, first, second, outputs


def source_rows(form, zero):
    const, linear, quadratic = form
    rows = list(split3(const))
    for entry in linear:
        rows += source_pairing(split3(entry))
    if quadratic is None:
        rows += [zero] * 36
    else:
        for entry in quadratic:
            rows += source_pairing(split3(entry))
    return rows + [zero] * (FAR_K - len(rows))


def target_rows(x):
    one = jnp.ones_like(x[0])
    rows = [one, one, one]
    for entry in x:
        rows += target_pairing(split3(entry))
    for i, j in SIX:
        rows += target_pairing(split3(x[i] * x[j]))
    return rows + [jnp.zeros_like(one)] * (FAR_K - len(rows))


def weights_of(square, first, second):
    inverse = lax.rsqrt(square)
    two = inverse * inverse
    three = two * inverse
    five = three * two
    return five * (first + second * two), three, five


def expansion_fields(x, sums):
    g = {}
    for place, (i, j) in enumerate(SIX):
        g[i, j] = g[j, i] = sums[7 + place]
    return [
        x[i] * sums[0]
        - sums[1 + i]
        - sums[4 + i]
        - (g[i, 0] * x[0] + g[i, 1] * x[1] + g[i, 2] * x[2])
        + sums[13 + i]
        for i in range(3)
    ]


def pitch_of(cells):
    return cells + 8 * (1 - cells // 8 % 2)


def rows8(start):
    return pl.ds(pl.multiple_of(start, 8), 8)


def lanes(block):
    return pl.ds(pl.multiple_of(block * CELL, CELL), CELL)


def store_rows(ref, rows, first, stride):
    for place, value in enumerate(rows):
        ref[pl.ds(first * stride + place, 8, stride=stride), :] = value


def own_offsets(planes_ref, centre_ref, cells, start):
    return [
        planes_ref[rows8(i * pitch_of(cells) + start), :] - centre_ref[i : i + 1, :] for i in range(3)
    ]


def planes_to_output(planes_ref, out_ref, cells):
    def step(b, carry):
        out_ref[:, lanes(b)] = planes_ref[pl.ds(b, 3, stride=pitch_of(cells)), :]
        return carry

    lax.fori_loop(0, cells, step, 0, unroll=8)


def lane_iota(shape):
    return lax.broadcasted_iota(jnp.int32, shape, len(shape) - 1)


def spread_sums(planes, targets):
    total = None
    for plane, target in zip(planes, targets):
        parts = jnp.concatenate([part.astype(BF16) for part in split3(plane)], axis=1)
        marked = target(lane_iota((3 * CELL, CELL))).astype(F32).astype(BF16)
        value = jnp.dot(parts, marked, preferred_element_type=F32)
        total = value if total is None else total + value
    return total


def leaf_tables(place, moment):
    mean = 1.0 / CELL
    centres = [spread_sums([entry], [lambda l: l >= 0]) * mean for entry in place]
    spread = [entry - centre for entry, centre in zip(place, centres)]
    lane = lane_iota(centres[0].shape)
    table = spread_sums(
        moment + [spread[j] * moment[i] for j in range(3) for i in range(3)],
        [lambda l, k=k: l == 3 + k for k in range(12)],
    )
    inner = (lane >= 6) & (lane < 15)
    by_centre = jnp.zeros_like(table)
    for j in range(3):
        table = jnp.where(lane == j, centres[j], table)
        by_centre = jnp.where(inner & (lane // 3 == 2 + j), centres[j], by_centre)
    by_moment = spread_sums(
        moment,
        [lambda l, i=i: (l >= 6) & (l < 15) & (lax.rem(l, 3) == i) for i in range(3)],
    )
    return table, by_centre, by_moment


def leaf_sections(table, let_rows_ref, let_ref):
    cells = table.shape[0]
    rows = jnp.concatenate([table, jnp.zeros((256 - cells, CELL), F32)], axis=0).T
    chosen = let_rows_ref[0]
    low = jnp.bitwise_and(chosen, CELL - 1)
    upper = chosen >= CELL
    for entry in range(15):
        row = jnp.broadcast_to(rows[entry : entry + 1, :], (8, 256))
        let_ref[:, entry, :] = jnp.where(
            upper,
            jnp.take_along_axis(row[:, CELL:], low, axis=1),
            jnp.take_along_axis(row[:, :CELL], low, axis=1),
        )
    let_ref[:, 15, :] = jnp.zeros((8, CELL), F32)


def top_tables(table, by_centre, by_moment, top_ref, centre_ref):
    half = table.shape[0] // 2
    sublane = lax.broadcasted_iota(jnp.int32, (8, CELL), 0)
    lane = lane_iota((1, CELL))
    tile = jnp.zeros((8, CELL), F32)
    middle = jnp.zeros((1, CELL), F32)
    for top in range(2):
        part = slice(top * half, (top + 1) * half)
        total = jnp.sum(table[part], axis=0, keepdims=True)
        centre = jnp.sum(by_centre[part], axis=0, keepdims=True) * (1.0 / half)
        moved = jnp.sum((by_centre[part] - centre) * by_moment[part], axis=0, keepdims=True)
        row = jnp.where(lane < 3, total * (1.0 / half), total + moved)
        tile = jnp.where(sublane == top, row, tile)
        middle = middle + 0.5 * row
    top_ref[...] = tile
    for i in range(3):
        centre_ref[i : i + 1, :] = jnp.broadcast_to(middle[:, i : i + 1], (1, CELL))
    centre_ref[3:8, :] = jnp.zeros((5, CELL), F32)


def first_kernel(
    cells,
    n_row,
    n_col,
    pos_ref,
    mom_ref,
    let_rows_ref,
    far_ref,
    planes_ref,
    before_ref,
    after_ref,
    centre_ref,
    let_out_ref,
    out_ref,
    let_in,
    let_ref,
    top_ref,
    top_in,
    feats,
    forms_rows,
    forms_stage,
    forms,
    coeffs,
    sums,
    far_sources,
    far_coeffs,
    far_sums,
    side_send,
    side_recv,
    let_send,
    let_recv,
    top_send,
    top_recv,
):
    row = lax.axis_index("row")
    col = lax.axis_index("col")
    device = row * n_col + col
    devices = n_row * n_col
    col_bits = n_col.bit_length() - 1
    row_bits = n_row.bit_length() - 1
    sources = 2 * n_col
    pitch = pitch_of(cells)

    def flip(value, bit):
        return value + (1 << bit) * (1 - 2 * lax.rem(value // (1 << bit), 2))

    def flip_by(value, mask):
        for bit in range(mask.bit_length()):
            if mask >> bit & 1:
                value = flip(value, bit)
        return value

    def place_of(index):
        return (index // n_col, lax.rem(index, n_col))

    following = place_of(lax.rem(device + 1, devices))
    preceding = place_of(lax.rem(device + devices - 1, devices))

    four = [flip_by(col, k) for k in range(1, GROUP)]
    groups = [flip_by(col, k * GROUP) for k in range(1, n_col // GROUP)]
    barrier = pltpu.get_barrier_semaphore()
    partners = [(row, other) for other in four + groups]
    partners += [(flip(row, bit), col) for bit in range(row_bits)] + [following, preceding]
    for partner in partners:
        pl.semaphore_signal(barrier, inc=1, device_id=partner, device_id_type=MESH)

    def to_planes(b, carry):
        planes_ref[pl.ds(b, 3, stride=pitch), :] = pos_ref[:, lanes(b)]
        planes_ref[pl.ds(3 * pitch + b, 3, stride=pitch), :] = mom_ref[:, lanes(b)]
        return carry

    lax.fori_loop(0, cells, to_planes, 0, unroll=8)

    def side_copy(side, part, target, to):
        rows = slice(part * pitch, (part + 1) * pitch)
        return pltpu.make_async_remote_copy(
            src_ref=planes_ref.at[rows],
            dst_ref=target.at[rows],
            send_sem=side_send.at[6 * side + part],
            recv_sem=side_recv.at[6 * side + part],
            device_id=to,
            device_id_type=MESH,
        )

    place = [planes_ref[i * pitch : i * pitch + cells, :] for i in range(3)]
    moment = [planes_ref[(3 + i) * pitch : (3 + i) * pitch + cells, :] for i in range(3)]
    leaf, by_centre, by_moment = leaf_tables(place, moment)
    top_tables(leaf, by_centre, by_moment, top_ref, centre_ref)
    top_in[col] = top_ref[...]
    pl.semaphore_wait(barrier, len(partners))

    first_copies = [
        pltpu.make_async_remote_copy(
            src_ref=top_ref,
            dst_ref=top_in.at[col],
            send_sem=top_send.at[k],
            recv_sem=top_recv.at[k],
            device_id=(row, other),
            device_id_type=MESH,
        )
        for k, other in enumerate(four)
    ]
    for copy in first_copies:
        copy.start()

    leaf_sections(leaf, let_rows_ref, let_ref)
    sections = []
    for section in range(col_bits + row_bits):
        if section < col_bits:
            partner = (row, flip(col, section))
        else:
            partner = (flip(row, section - col_bits), col)
        sections.append(
            pltpu.make_async_remote_copy(
                src_ref=let_ref.at[section],
                dst_ref=let_in.at[section],
                send_sem=let_send.at[section],
                recv_sem=let_recv.at[section],
                device_id=partner,
                device_id_type=MESH,
            )
        )
    for copy in sections:
        copy.start()

    for copy in first_copies:
        copy.wait()
    mine = pl.ds(col // GROUP * GROUP, GROUP)
    second_copies = [
        pltpu.make_async_remote_copy(
            src_ref=top_in.at[mine],
            dst_ref=top_in.at[mine],
            send_sem=top_send.at[len(four) + k],
            recv_sem=top_recv.at[len(four) + k],
            device_id=(row, other),
            device_id_type=MESH,
        )
        for k, other in enumerate(groups)
    ]
    for copy in second_copies:
        copy.start()

    def build(group, carry):
        x = own_offsets(planes_ref, centre_ref, cells, group * 8)
        store_rows(feats, target_rows(x), group * 8, FAR_S)
        return carry

    lax.fori_loop(0, cells // 8, build, 0, unroll=2)
    for copy in second_copies:
        copy.wait()
    sides = []
    for part in range(6):
        sides.append(side_copy(0, part, before_ref, following))
        sides.append(side_copy(1, part, after_ref, preceding))
    for copy in sides:
        copy.start()
    top_in[col] = jnp.zeros(top_ref.shape, F32)

    table = jnp.concatenate(
        [top_in[:, top, :] for top in range(2)] + [jnp.zeros((CELL - sources, CELL), F32)], axis=0
    )
    table = table.T
    entries = [table[k : k + 1, :] for k in range(15)]
    entries = [entries[i] - centre_ref[i : i + 1, :] for i in range(3)] + entries[3:]
    square, first, second, outputs = expansion_coefficients(entries)
    zero = jnp.zeros_like(entries[0])
    g = [[outputs[7 + SIX.index((min(i, j), max(i, j)))] for j in range(3)] for i in range(3)]
    bent = [(-outputs[13 + i], g[i], None) for i in range(3)]
    for position, form in enumerate([square, first, second] + bent):
        base = position * FAR_K
        for k, value in enumerate(source_rows(form, zero)):
            forms_rows[base + k : base + k + 1, :] = value
    for position in range(FORMS):
        value = forms_rows[position * FAR_K : (position + 1) * FAR_K, :].T
        for tile in range(sources // 8):
            start = (tile * FORMS + position) * 8
            forms_stage[start : start + 8, :] = value[tile * 8 : (tile + 1) * 8, :]
    forms[...] = forms_stage[...].astype(BF16)
    for k, value in enumerate(entries[:3] + outputs[4:7]):
        forms_rows[k : k + 1, :] = value
    columns = forms_rows[0:CELL, :].T
    for k in range(6):
        coeffs[k * sources : (k + 1) * sources, :] = jnp.broadcast_to(
            columns[:sources, k : k + 1], (sources, CELL)
        )

    def step(pair, carry):
        for sub in range(TOP_UNROLL):
            cell = 2 * (TOP_UNROLL * pair + sub)
            features = jnp.concatenate(
                [
                    feats[pl.ds(pl.multiple_of((cell + k) * FAR_S, FAR_S), FAR_K), :]
                    for k in range(2)
                ],
                axis=1,
            ).astype(BF16)
            values = jnp.dot(forms[...], features, preferred_element_type=F32)
            for k in range(2):
                totals = None
                for tile in range(sources // 8):
                    form = [
                        values[
                            (tile * FORMS + f) * 8 : (tile * FORMS + f + 1) * 8,
                            k * CELL : (k + 1) * CELL,
                        ]
                        for f in range(FORMS)
                    ]
                    const = [
                        coeffs[f * sources + tile * 8 : f * sources + (tile + 1) * 8, :]
                        for f in range(6)
                    ]
                    weight, three, five = weights_of(*form[:3])
                    terms = [weight] + [
                        const[i] * weight + const[3 + i] * three + form[3 + i] * five
                        for i in range(3)
                    ]
                    totals = terms if totals is None else [t + u for t, u in zip(totals, terms)]
                for place_, value in enumerate(totals):
                    sums[rows8((place_ * cells + cell + k) * 8), :] = value
        return carry

    lax.fori_loop(0, cells // (2 * TOP_UNROLL), step, 0)

    for copy in sections:
        copy.wait()
    sublane = lax.broadcasted_iota(jnp.int32, (8, CELL), 0)
    lane = lax.broadcasted_iota(jnp.int32, (8, CELL), 1)

    groups = cells // 8
    lists = far_ref[...].astype(F32)
    lists = jnp.concatenate([lists, jnp.zeros((lists.shape[0], 256 - cells), F32)], axis=1)
    lists = jnp.concatenate([lists, jnp.zeros((CELL - lists.shape[0], 256), F32)], axis=0)
    far_sums[0:256, :] = lists.T
    repeated = jnp.bitwise_and(lax.broadcasted_iota(jnp.int32, (groups, CELL), 1), 15)
    slot = jnp.right_shift(lax.broadcasted_iota(jnp.int32, (groups, CELL), 1), 4)
    listed = jnp.zeros((groups, CELL), F32)
    for k in range(8):
        rows = far_sums[pl.ds(k, groups, stride=8), :]
        listed = jnp.where(slot == k, jnp.take_along_axis(rows, repeated, axis=1), listed)
    listed = listed.astype(jnp.int32)
    low = jnp.bitwise_and(listed, CELL - 1)
    section = jnp.right_shift(listed, 7)
    dense = []
    for entry in range(15):
        table = let_in[:, entry, :]
        value = jnp.zeros(listed.shape, F32)
        for k in range(8):
            source = jnp.broadcast_to(table[k : k + 1, :], listed.shape)
            value = jnp.where(section == k, jnp.take_along_axis(source, low, axis=1), value)
        dense.append(value)
    repeat = sublane * 16 + jnp.bitwise_and(lane, 15)
    for entry in range(15):
        far_sums[entry * groups : (entry + 1) * groups, :] = dense[entry]

    paired = jnp.bitwise_and(sublane, 3) * 32 + jnp.right_shift(lane, 6) * 16
    paired = paired + jnp.bitwise_and(lane, 15)
    quarter = jnp.bitwise_and(lane, 63)

    def listed_table(group, spread):
        rows = [far_sums[pl.ds(entry * groups + group, 1), :] for entry in range(15)]
        return [
            jnp.take_along_axis(jnp.broadcast_to(row, (8, CELL)), spread, axis=1) for row in rows
        ]

    def centred(table):
        return [table[i] - centre_ref[i : i + 1, :] for i in range(3)] + table[3:]

    def build_far_sources(two, carry):
        tables = [listed_table(2 * two + k, paired) for k in range(2)]
        table = centred([jnp.where(sublane < 4, a, b) for a, b in zip(*tables)])
        square, first, second, _ = expansion_coefficients(table)
        zero = jnp.zeros((8, CELL), F32)
        forms = [source_rows(form, zero) for form in (square, first, second)]
        rows = [
            jnp.where(quarter < 16, a, jnp.where(quarter < 32, b, c)) for a, b, c in zip(*forms)
        ]
        store_rows(far_sources, rows, two * 8, FAR_S)
        return carry

    lax.fori_loop(0, groups // 2, build_far_sources, 0, unroll=2)

    def build_far(group, carry):
        _, _, _, outputs = expansion_coefficients(centred(listed_table(group, repeat)))
        pieces = [split3(value) for value in outputs]
        rows = []
        for part in range(3):
            for k in range(OUT_K):
                kind = 0 if k < 4 else 1 if k < 7 else 2
                inside = (lane >= 32 * kind) & (lane < 32 * kind + 32)
                rows.append(jnp.where(inside, pieces[k][part], 0.0))
        store_rows(far_coeffs, rows, group * 8, COEF_S)
        return carry

    lax.fori_loop(0, groups, build_far, 0, unroll=2)

    def far_pair(cell):
        source = far_sources[pl.ds(pl.multiple_of(cell // 2 * FAR_S, FAR_S), FAR_K), :]
        turned = source.astype(BF16).T
        for k in range(2):
            start = (cell + k) * FAR_S
            features = feats[pl.ds(pl.multiple_of(start, FAR_S), FAR_K), :].astype(BF16)
            values = jnp.dot(
                turned[64 * k : 64 * k + 48], features, preferred_element_type=F32
            )
            parts = weights_of(values[:16], values[16:32], values[32:48])
            weights = jnp.concatenate([half for part in parts for half in split2(part)], axis=0)
            start = (cell + k) * COEF_S
            rows = far_coeffs[pl.ds(pl.multiple_of(start, COEF_S), 48), :][:, :96].astype(BF16)
            result = jnp.dot(rows, weights, preferred_element_type=F32)
            result = result[:OUT_K] + result[OUT_K : 2 * OUT_K] + result[2 * OUT_K :]
            far_sums[pl.ds(cell + k, OUT_K, stride=pitch), :] = result

    def finish_top(group, carry):
        x = own_offsets(planes_ref, centre_ref, cells, group * 8)
        totals = []
        for place_ in range(4):
            base = (place_ * cells + group * 8) * 8
            parts = [sums[pl.ds(base + k, 8, stride=8), :] for k in range(8)]
            while len(parts) > 1:
                parts = [parts[k] + parts[k + 1] for k in range(0, len(parts), 2)]
            totals.append(parts[0])
        for i in range(3):
            out_ref[rows8(i * pitch + group * 8), :] = x[i] * totals[0] - totals[1 + i]
        return carry

    lax.fori_loop(0, cells // 8, finish_top, 0, unroll=2)

    def far_step(part, carry):
        for sub in range(0, FAR_UNROLL, 2):
            far_pair(FAR_UNROLL * part + sub)
        return carry

    lax.fori_loop(0, cells // FAR_UNROLL, far_step, 0)

    def finish_far(group, carry):
        x = own_offsets(planes_ref, centre_ref, cells, group * 8)
        totals = [far_sums[rows8(k * pitch_of(cells) + group * 8), :] for k in range(OUT_K)]
        for i, value in enumerate(expansion_fields(x, totals)):
            let_out_ref[rows8(i * pitch_of(cells) + group * 8), :] = value
        return carry

    lax.fori_loop(0, cells // 8, finish_far, 0, unroll=2)
    for copy in sides:
        copy.wait()


def near_source_rows(y, moment):
    zero = jnp.zeros_like(y[0])
    one = jnp.ones_like(y[0])
    back = [split3(-2.0 * entry) for entry in y]
    square = split3(y[0] * y[0] + y[1] * y[1] + y[2] * y[2] + SOFTEN)
    scaled = [(3.0 * COUPLING) * entry for entry in moment]
    const = split3(-(y[0] * scaled[0] + y[1] * scaled[1] + y[2] * scaled[2]))
    scaled = [split3(entry) for entry in scaled]
    rows = []
    for part in range(3):
        rows += [one] + [b[part] for b in back] + [s[part] for s in scaled] + [const[part]]
    for part, source in ((0, 0), (1, 1), (2, 0)):
        rows += [square[part]] + [b[source] for b in back] + [s[source] for s in scaled] + [zero]
    return rows


def near_target_rows(x):
    one = jnp.ones_like(x[0])
    zero = jnp.zeros_like(x[0])
    norm = split3(x[0] * x[0] + x[1] * x[1] + x[2] * x[2])
    pieces = [split3(entry) for entry in x]
    rows = []
    for part in range(3):
        high = [p[0] for p in pieces]
        rows += [norm[part]] + high + high + [one]
    for target in (1, 1, 2):
        chosen = [p[target] for p in pieces]
        rows += [one] + chosen + chosen + [zero]
    return rows


def near_kernel(
    cells,
    devices,
    n_col,
    near_ref,
    own_ref,
    prev_ref,
    next_ref,
    centre_ref,
    let_planes_ref,
    top_ref,
    near_out,
    let_out,
    top_out,
    near_sources,
    near_targets,
    masks,
    near_sums,
    field,
):
    sublane = lax.broadcasted_iota(jnp.int32, (8, CELL), 0)
    diagonal = lax.broadcasted_iota(jnp.int32, (CELL, CELL), 0) == lax.broadcasted_iota(
        jnp.int32, (CELL, CELL), 1
    )
    masks[0:CELL, :] = jnp.zeros((CELL, CELL), F32)
    masks[CELL : 2 * CELL, :] = jnp.where(diagonal, 1e30, 0.0)

    def build_sources(ref, first, keep):
        def build(group, carry):
            y = own_offsets(ref, centre_ref, cells, group * 8)
            moment = [ref[rows8((3 + i) * pitch_of(cells) + group * 8), :] for i in range(3)]
            if keep is not None:
                moment = [jnp.where(keep, entry, 0.0) for entry in moment]
            store_rows(near_sources, near_source_rows(y, moment), first + group * 8, NEAR_S)
            return carry

        lax.fori_loop(0, cells // 8, build, 0, unroll=2)

    device = lax.axis_index("row") * n_col + lax.axis_index("col")
    ordinal = jnp.full((8, CELL), device, jnp.int32)
    build_sources(prev_ref, 0, ordinal > 0)
    build_sources(own_ref, cells, None)
    build_sources(next_ref, 2 * cells, ordinal < devices - 1)

    def build_targets(group, carry):
        x = own_offsets(own_ref, centre_ref, cells, group * 8)
        store_rows(near_targets, near_target_rows(x), group * 8, NEAR_S)
        return carry

    lax.fori_loop(0, cells // 8, build_targets, 0, unroll=2)

    upper_rows = lax.rem(lax.broadcasted_iota(jnp.int32, (NEAR_K, CELL), 0), 8) < 4

    def near_part(cell):
        targets = near_targets[pl.ds(pl.multiple_of(cell * NEAR_S, NEAR_S), NEAR_K), :]
        features = jnp.concatenate(
            [jnp.where(upper_rows, targets, 0.0), jnp.where(upper_rows, 0.0, targets)], axis=1
        ).astype(BF16)
        total = None
        for e in range(2):
            block = near_ref[e, cell]
            source = near_sources[pl.ds(pl.multiple_of(block * NEAR_S, NEAR_S), NEAR_K), :]
            values = jnp.dot(source.astype(BF16).T, features, preferred_element_type=F32)
            own = (block == cells + cell).astype(jnp.int32)
            mask = masks[pl.ds(pl.multiple_of(own * CELL, CELL), CELL), :]
            inverse = lax.rsqrt(values[:, :CELL] + mask)
            two = inverse * inverse
            three = two * inverse
            projected = values[:, CELL:] * two * three
            p_high, p_low = split2(projected)
            t_high, t_low = split2(three)
            weights = jnp.concatenate(
                [
                    jnp.concatenate([p_high, t_high], axis=1),
                    jnp.concatenate([p_low, t_low], axis=1),
                ],
                axis=0,
            )
            coeffs = source[:32].astype(BF16)
            result = jnp.dot(
                jnp.concatenate([coeffs, coeffs], axis=1), weights, preferred_element_type=F32
            )
            result = result[0:8] + result[8:16] + result[16:24]
            total = result if total is None else total + result
        near_sums[pl.ds(cell, 8, stride=pitch_of(cells)), :] = jnp.where(
            sublane < 4, total[:, :CELL], total[:, CELL:]
        )

    def step(pair, carry):
        for sub in range(NEAR_UNROLL):
            near_part(NEAR_UNROLL * pair + sub)
        return carry

    lax.fori_loop(0, cells // NEAR_UNROLL, step, 0)

    def finish_near(group, carry):
        x = own_offsets(own_ref, centre_ref, cells, group * 8)
        totals = [near_sums[rows8(k * pitch_of(cells) + group * 8), :] for k in range(7)]
        for i in range(3):
            field[rows8(i * pitch_of(cells) + group * 8), :] = (
                (x[i] * totals[0] - totals[4 + i]) * (1.0 / 3.0) + 0.5 * totals[1 + i]
            )
        return carry

    lax.fori_loop(0, cells // 8, finish_near, 0, unroll=2)
    planes_to_output(field, near_out, cells)

    planes_to_output(let_planes_ref, let_out, cells)
    planes_to_output(top_ref, top_out, cells)


def vmem(count):
    return [pl.BlockSpec(memory_space=pltpu.VMEM)] * count


def make_first(cells, n_row, n_col):
    bits = n_row.bit_length() + n_col.bit_length() - 2
    sources = 2 * n_col
    planes = jax.ShapeDtypeStruct((6 * pitch_of(cells), CELL), F32)
    return pl.pallas_call(
        functools.partial(first_kernel, cells, n_row, n_col),
        out_shape=(
            planes,
            planes,
            planes,
            jax.ShapeDtypeStruct((8, CELL), F32),
            jax.ShapeDtypeStruct((3 * pitch_of(cells), CELL), F32),
            jax.ShapeDtypeStruct((3 * pitch_of(cells), CELL), F32),
        ),
        in_specs=vmem(4),
        out_specs=tuple(
            vmem(1) + [pl.BlockSpec(memory_space=pl.ANY)] * 2 + vmem(3)
        ),
        scratch_shapes=[
            pltpu.VMEM((bits, 16, CELL), F32),
            pltpu.VMEM((bits, 16, CELL), F32),
            pltpu.VMEM((8, CELL), F32),
            pltpu.VMEM((n_col, 8, CELL), F32),
            pltpu.VMEM((cells * FAR_S, CELL), F32),
            pltpu.VMEM((FORMS * FAR_K, CELL), F32),
            pltpu.VMEM((FORMS * sources, FAR_K), F32),
            pltpu.VMEM((FORMS * sources, FAR_K), BF16),
            pltpu.VMEM((6 * sources, CELL), F32),
            pltpu.VMEM((4 * cells * 8, CELL), F32),
            pltpu.VMEM((cells // 2 * FAR_S, CELL), F32),
            pltpu.VMEM((cells * COEF_S, CELL), F32),
            pltpu.VMEM((OUT_K * pitch_of(cells), CELL), F32),
            pltpu.SemaphoreType.DMA((12,)),
            pltpu.SemaphoreType.DMA((12,)),
            pltpu.SemaphoreType.DMA((bits,)),
            pltpu.SemaphoreType.DMA((bits,)),
            pltpu.SemaphoreType.DMA((n_col,)),
            pltpu.SemaphoreType.DMA((n_col,)),
        ],
        compiler_params=pltpu.CompilerParams(
            collective_id=0, has_side_effects=True, vmem_limit_bytes=VMEM_LIMIT
        ),
        cost_estimate=pl.CostEstimate(
            flops=8_000_000_000, bytes_accessed=4_000_000, transcendentals=1_600_000
        ),
        name="tables_exchange_top",
    )


def make_near(cells, devices, n_col, n):
    return pl.pallas_call(
        functools.partial(near_kernel, cells, devices, n_col),
        out_shape=(jax.ShapeDtypeStruct((3, n), F32),) * 3,
        in_specs=[pl.BlockSpec(memory_space=pltpu.SMEM)] + vmem(6),
        out_specs=tuple(vmem(3)),
        scratch_shapes=[
            pltpu.VMEM((3 * cells * NEAR_S, CELL), F32),
            pltpu.VMEM((cells * NEAR_S, CELL), F32),
            pltpu.VMEM((2 * CELL, CELL), F32),
            pltpu.VMEM((8 * pitch_of(cells), CELL), F32),
            pltpu.VMEM((3 * pitch_of(cells), CELL), F32),
        ],
        compiler_params=pltpu.CompilerParams(vmem_limit_bytes=VMEM_LIMIT),
        cost_estimate=pl.CostEstimate(
            flops=30_000_000_000, bytes_accessed=4_000_000, transcendentals=6_600_000
        ),
        name="near_and_let_field",
    )


def body(positions, moments, near_list, far_list, let_rows):
    n = positions.shape[1]
    cells = n // CELL
    n_row, n_col = lax.axis_size("row"), lax.axis_size("col")
    planes, before, after, centre, remote, top = make_first(cells, n_row, n_col)(
        positions, moments, let_rows, far_list.T
    )
    return make_near(cells, n_row * n_col, n_col, n)(
        near_list.T,
        planes,
        before,
        after,
        centre,
        remote,
        top,
    )


def solution(mesh):
    return jax.shard_map(
        body,
        mesh=mesh,
        in_specs=(
            P(None, ("row", "col")),
            P(None, ("row", "col")),
            P(("row", "col"), None),
            P(("row", "col"), None),
            P(("row", "col"), None, None),
        ),
        out_specs=(P(None, ("row", "col")), P(None, ("row", "col")), P(None, ("row", "col"))),
        check_vma=False,
    )
```

```python
import functools

import jax
import jax.numpy as jnp
from jax import lax
from jax.experimental import pallas as pl
from jax.experimental.pallas import tpu as pltpu
from jax.sharding import PartitionSpec as P

CELL = 128
SOFTEN = 0.09
COUPLING = 0.004
F32 = jnp.float32
BF16 = jnp.bfloat16
MESH = pl.DeviceIdType.MESH
VMEM_LIMIT = 58 * 1024 * 1024
SIX = ((0, 0), (0, 1), (0, 2), (1, 1), (1, 2), (2, 2))
NEAR_K = 48
FAR_K = 64
OUT_K = 16
NEAR_S = 56
FAR_S = 72
COEF_S = 56
FORMS = 6
GROUP = 4
TOP_UNROLL = 24
NEAR_UNROLL = 48


def split3(value):
    high = value.astype(BF16).astype(F32)
    rest = value - high
    middle = rest.astype(BF16).astype(F32)
    return high, middle, rest - middle


def split2(value):
    high = value.astype(BF16)
    return high, (value - high.astype(F32)).astype(BF16)


def source_pairing(parts):
    return [parts[0], parts[1], parts[2], parts[0], parts[1], parts[0]]


def target_pairing(parts):
    return [parts[0], parts[0], parts[0], parts[1], parts[1], parts[2]]


def expansion_coefficients(table):
    c = table[0:3]
    m = [COUPLING * entry for entry in table[3:6]]
    q = [[COUPLING * table[6 + 3 * j + i] for i in range(3)] for j in range(3)]
    g = [[q[j][i] + q[i][j] for i in range(3)] for j in range(3)]
    t = q[0][0] + q[1][1] + q[2][2]
    gc = [g[i][0] * c[0] + g[i][1] * c[1] + g[i][2] * c[2] for i in range(3)]
    zero = jnp.zeros_like(c[0])
    one = jnp.ones_like(c[0])
    square = (
        c[0] * c[0] + c[1] * c[1] + c[2] * c[2] + SOFTEN,
        [-2.0 * c[i] for i in range(3)],
        [one if i == j else zero for i, j in SIX],
    )
    first = (
        -3.0 * (c[0] * m[0] + c[1] * m[1] + c[2] * m[2] + t),
        [3.0 * m[i] for i in range(3)],
        None,
    )
    second = (
        7.5 * (c[0] * gc[0] + c[1] * gc[1] + c[2] * gc[2]),
        [-15.0 * gc[i] for i in range(3)],
        [(7.5 if i == j else 15.0) * g[i][j] for i, j in SIX],
    )
    outputs = [one] + list(c) + m + [3.0 * g[i][j] for i, j in SIX] + [3.0 * gc[i] for i in range(3)]
    return square, first, second, outputs


def source_rows(form, zero):
    const, linear, quadratic = form
    rows = list(split3(const))
    for entry in linear:
        rows += source_pairing(split3(entry))
    if quadratic is None:
        rows += [zero] * 36
    else:
        for entry in quadratic:
            rows += source_pairing(split3(entry))
    return rows + [zero] * (FAR_K - len(rows))


def target_rows(x):
    one = jnp.ones_like(x[0])
    rows = [one, one, one]
    for entry in x:
        rows += target_pairing(split3(entry))
    for i, j in SIX:
        rows += target_pairing(split3(x[i] * x[j]))
    return rows + [jnp.zeros_like(one)] * (FAR_K - len(rows))


def weights_of(square, first, second):
    inverse = lax.rsqrt(square)
    two = inverse * inverse
    three = two * inverse
    five = three * two
    return five * (first + second * two), three, five


def expansion_fields(x, sums):
    g = {}
    for place, (i, j) in enumerate(SIX):
        g[i, j] = g[j, i] = sums[7 + place]
    return [
        x[i] * sums[0]
        - sums[1 + i]
        - sums[4 + i]
        - (g[i, 0] * x[0] + g[i, 1] * x[1] + g[i, 2] * x[2])
        + sums[13 + i]
        for i in range(3)
    ]


def pitch_of(cells):
    return cells + 8 * (1 - cells // 8 % 2)


def rows8(start):
    return pl.ds(pl.multiple_of(start, 8), 8)


def lanes(block):
    return pl.ds(pl.multiple_of(block * CELL, CELL), CELL)


def store_rows(ref, rows, first, stride):
    for place, value in enumerate(rows):
        ref[pl.ds(first * stride + place, 8, stride=stride), :] = value


def own_offsets(planes_ref, centre_ref, cells, start):
    return [
        planes_ref[rows8(i * pitch_of(cells) + start), :] - centre_ref[i : i + 1, :] for i in range(3)
    ]


def planes_to_output(planes_ref, out_ref, cells):
    def step(b, carry):
        out_ref[:, lanes(b)] = planes_ref[pl.ds(b, 3, stride=pitch_of(cells)), :]
        return carry

    lax.fori_loop(0, cells, step, 0, unroll=8)


def lane_iota(shape):
    return lax.broadcasted_iota(jnp.int32, shape, len(shape) - 1)


def spread_sums(planes, targets, terms):
    total = None
    for plane, target in zip(planes, targets):
        parts = jnp.concatenate([part.astype(BF16) for part in split3(plane)[:terms]], axis=1)
        marked = target(lane_iota((terms * CELL, CELL))).astype(F32).astype(BF16)
        value = jnp.dot(parts, marked, preferred_element_type=F32)
        total = value if total is None else total + value
    return total


def leaf_tables(place, moment):
    mean = 1.0 / CELL
    centres = [spread_sums([entry], [lambda l: l >= 0], 3) * mean for entry in place]
    spread = [entry - centre for entry, centre in zip(place, centres)]
    lane = lane_iota(centres[0].shape)
    table = spread_sums(
        moment + [spread[j] * moment[i] for j in range(3) for i in range(3)],
        [lambda l, k=k: l == 3 + k for k in range(12)],
        2,
    )
    inner = (lane >= 6) & (lane < 15)
    by_centre = jnp.zeros_like(table)
    for j in range(3):
        table = jnp.where(lane == j, centres[j], table)
        by_centre = jnp.where(inner & (lane // 3 == 2 + j), centres[j], by_centre)
    by_moment = spread_sums(
        moment,
        [lambda l, i=i: (l >= 6) & (l < 15) & (lax.rem(l, 3) == i) for i in range(3)],
        2,
    )
    return table, by_centre, by_moment


def leaf_sections(table, let_rows_ref, let_ref):
    cells = table.shape[0]
    rows = jnp.concatenate([table, jnp.zeros((256 - cells, CELL), F32)], axis=0).T
    chosen = let_rows_ref[0]
    low = jnp.bitwise_and(chosen, CELL - 1)
    upper = chosen >= CELL
    for entry in range(15):
        row = jnp.broadcast_to(rows[entry : entry + 1, :], (8, 256))
        let_ref[:, entry, :] = jnp.where(
            upper,
            jnp.take_along_axis(row[:, CELL:], low, axis=1),
            jnp.take_along_axis(row[:, :CELL], low, axis=1),
        )
    let_ref[:, 15, :] = jnp.zeros((8, CELL), F32)


def top_tables(table, by_centre, by_moment, top_ref, centre_ref):
    half = table.shape[0] // 2
    sublane = lax.broadcasted_iota(jnp.int32, (8, CELL), 0)
    lane = lane_iota((1, CELL))
    tile = jnp.zeros((8, CELL), F32)
    middle = jnp.zeros((1, CELL), F32)
    for top in range(2):
        part = slice(top * half, (top + 1) * half)
        total = jnp.sum(table[part], axis=0, keepdims=True)
        centre = jnp.sum(by_centre[part], axis=0, keepdims=True) * (1.0 / half)
        moved = jnp.sum((by_centre[part] - centre) * by_moment[part], axis=0, keepdims=True)
        row = jnp.where(lane < 3, total * (1.0 / half), total + moved)
        tile = jnp.where(sublane == top, row, tile)
        middle = middle + 0.5 * row
    top_ref[...] = tile
    for i in range(3):
        centre_ref[i : i + 1, :] = jnp.broadcast_to(middle[:, i : i + 1], (1, CELL))
    centre_ref[3:8, :] = jnp.zeros((5, CELL), F32)


def first_kernel(
    cells,
    n_row,
    n_col,
    pos_ref,
    mom_ref,
    let_rows_ref,
    planes_ref,
    before_ref,
    after_ref,
    let_in,
    centre_ref,
    out_ref,
    let_ref,
    top_ref,
    top_in,
    feats,
    forms_rows,
    forms_stage,
    forms,
    coeffs,
    sums,
    side_send,
    side_recv,
    let_send,
    let_recv,
    top_send,
    top_recv,
):
    row = lax.axis_index("row")
    col = lax.axis_index("col")
    device = row * n_col + col
    devices = n_row * n_col
    col_bits = n_col.bit_length() - 1
    row_bits = n_row.bit_length() - 1
    sources = 2 * n_col
    pitch = pitch_of(cells)

    def flip(value, bit):
        return value + (1 << bit) * (1 - 2 * lax.rem(value // (1 << bit), 2))

    def flip_by(value, mask):
        for bit in range(mask.bit_length()):
            if mask >> bit & 1:
                value = flip(value, bit)
        return value

    def place_of(index):
        return (index // n_col, lax.rem(index, n_col))

    following = place_of(lax.rem(device + 1, devices))
    preceding = place_of(lax.rem(device + devices - 1, devices))

    four = [flip_by(col, k) for k in range(1, GROUP)]
    groups = [flip_by(col, k * GROUP) for k in range(1, n_col // GROUP)]
    barrier = pltpu.get_barrier_semaphore()
    partners = [(row, other) for other in four + groups]
    partners += [(flip(row, bit), col) for bit in range(row_bits)] + [following, preceding]
    for partner in partners:
        pl.semaphore_signal(barrier, inc=1, device_id=partner, device_id_type=MESH)

    def to_planes(b, carry):
        planes_ref[pl.ds(b, 3, stride=pitch), :] = pos_ref[:, lanes(b)]
        planes_ref[pl.ds(3 * pitch + b, 3, stride=pitch), :] = mom_ref[:, lanes(b)]
        return carry

    lax.fori_loop(0, cells, to_planes, 0, unroll=8)

    def side_copy(side, part, target, to):
        rows = slice(part * pitch, (part + 1) * pitch)
        return pltpu.make_async_remote_copy(
            src_ref=planes_ref.at[rows],
            dst_ref=target.at[rows],
            send_sem=side_send.at[6 * side + part],
            recv_sem=side_recv.at[6 * side + part],
            device_id=to,
            device_id_type=MESH,
        )

    place = [planes_ref[i * pitch : i * pitch + cells, :] for i in range(3)]
    moment = [planes_ref[(3 + i) * pitch : (3 + i) * pitch + cells, :] for i in range(3)]
    leaf, by_centre, by_moment = leaf_tables(place, moment)
    top_tables(leaf, by_centre, by_moment, top_ref, centre_ref)
    top_in[col] = top_ref[...]
    pl.semaphore_wait(barrier, len(partners))

    first_copies = [
        pltpu.make_async_remote_copy(
            src_ref=top_ref,
            dst_ref=top_in.at[col],
            send_sem=top_send.at[k],
            recv_sem=top_recv.at[k],
            device_id=(row, other),
            device_id_type=MESH,
        )
        for k, other in enumerate(four)
    ]
    for copy in first_copies:
        copy.start()

    leaf_sections(leaf, let_rows_ref, let_ref)
    sections = []
    for section in range(col_bits + row_bits):
        if section < col_bits:
            partner = (row, flip(col, section))
        else:
            partner = (flip(row, section - col_bits), col)
        sections.append(
            pltpu.make_async_remote_copy(
                src_ref=let_ref.at[section],
                dst_ref=let_in.at[section],
                send_sem=let_send.at[section],
                recv_sem=let_recv.at[section],
                device_id=partner,
                device_id_type=MESH,
            )
        )
    for copy in sections:
        copy.start()

    for copy in first_copies:
        copy.wait()
    mine = pl.ds(col // GROUP * GROUP, GROUP)
    second_copies = [
        pltpu.make_async_remote_copy(
            src_ref=top_in.at[mine],
            dst_ref=top_in.at[mine],
            send_sem=top_send.at[len(four) + k],
            recv_sem=top_recv.at[len(four) + k],
            device_id=(row, other),
            device_id_type=MESH,
        )
        for k, other in enumerate(groups)
    ]
    for copy in second_copies:
        copy.start()
    sides = []
    for part in range(6):
        sides.append(side_copy(0, part, before_ref, following))
        sides.append(side_copy(1, part, after_ref, preceding))
    for copy in sides[:6]:
        copy.start()

    def build(group, carry):
        x = own_offsets(planes_ref, centre_ref, cells, group * 8)
        store_rows(feats, target_rows(x), group * 8, FAR_S)
        return carry

    lax.fori_loop(0, cells // 8, build, 0, unroll=2)
    for copy in second_copies:
        copy.wait()
    for copy in sides[6:]:
        copy.start()
    top_in[col] = jnp.zeros(top_ref.shape, F32)

    table = jnp.concatenate(
        [top_in[:, top, :] for top in range(2)] + [jnp.zeros((CELL - sources, CELL), F32)], axis=0
    )
    table = table.T
    entries = [table[k : k + 1, :] for k in range(15)]
    entries = [entries[i] - centre_ref[i : i + 1, :] for i in range(3)] + entries[3:]
    square, first, second, outputs = expansion_coefficients(entries)
    zero = jnp.zeros_like(entries[0])
    g = [[outputs[7 + SIX.index((min(i, j), max(i, j)))] for j in range(3)] for i in range(3)]
    bent = [(-outputs[13 + i], g[i], None) for i in range(3)]
    for position, form in enumerate([square, first, second] + bent):
        base = position * FAR_K
        for k, value in enumerate(source_rows(form, zero)):
            forms_rows[base + k : base + k + 1, :] = value
    for position in range(FORMS):
        value = forms_rows[position * FAR_K : (position + 1) * FAR_K, :].T
        for tile in range(sources // 8):
            start = (tile * FORMS + position) * 8
            forms_stage[start : start + 8, :] = value[tile * 8 : (tile + 1) * 8, :]
    forms[...] = forms_stage[...].astype(BF16)
    for k, value in enumerate(entries[:3] + outputs[4:7]):
        forms_rows[k : k + 1, :] = value
    columns = forms_rows[0:CELL, :].T
    for k in range(6):
        coeffs[k * sources : (k + 1) * sources, :] = jnp.broadcast_to(
            columns[:sources, k : k + 1], (sources, CELL)
        )

    def step(pair, carry):
        for sub in range(TOP_UNROLL):
            cell = 2 * (TOP_UNROLL * pair + sub)
            features = jnp.concatenate(
                [
                    feats[pl.ds(pl.multiple_of((cell + k) * FAR_S, FAR_S), FAR_K), :]
                    for k in range(2)
                ],
                axis=1,
            ).astype(BF16)
            values = jnp.dot(forms[...], features, preferred_element_type=F32)
            for k in range(2):
                totals = None
                for tile in range(sources // 8):
                    form = [
                        values[
                            (tile * FORMS + f) * 8 : (tile * FORMS + f + 1) * 8,
                            k * CELL : (k + 1) * CELL,
                        ]
                        for f in range(FORMS)
                    ]
                    const = [
                        coeffs[f * sources + tile * 8 : f * sources + (tile + 1) * 8, :]
                        for f in range(6)
                    ]
                    weight, three, five = weights_of(*form[:3])
                    terms = [weight] + [
                        const[i] * weight + const[3 + i] * three + form[3 + i] * five
                        for i in range(3)
                    ]
                    totals = terms if totals is None else [t + u for t, u in zip(totals, terms)]
                for place_, value in enumerate(totals):
                    sums[rows8((place_ * cells + cell + k) * 8), :] = value
        return carry

    lax.fori_loop(0, cells // (2 * TOP_UNROLL), step, 0)

    def finish_top(group, carry):
        x = own_offsets(planes_ref, centre_ref, cells, group * 8)
        totals = []
        for place_ in range(4):
            base = (place_ * cells + group * 8) * 8
            parts = [sums[pl.ds(base + k, 8, stride=8), :] for k in range(8)]
            while len(parts) > 1:
                parts = [parts[k] + parts[k + 1] for k in range(0, len(parts), 2)]
            totals.append(parts[0])
        for i in range(3):
            out_ref[rows8(i * pitch + group * 8), :] = x[i] * totals[0] - totals[1 + i]
        return carry

    lax.fori_loop(0, cells // 8, finish_top, 0, unroll=2)

    for copy in sections:
        copy.wait()
    for copy in sides:
        copy.wait()


def near_source_rows(y, moment):
    zero = jnp.zeros_like(y[0])
    one = jnp.ones_like(y[0])
    back = [split3(-2.0 * entry) for entry in y]
    square = split3(y[0] * y[0] + y[1] * y[1] + y[2] * y[2] + SOFTEN)
    scaled = [(3.0 * COUPLING) * entry for entry in moment]
    const = split3(-(y[0] * scaled[0] + y[1] * scaled[1] + y[2] * scaled[2]))
    scaled = [split3(entry) for entry in scaled]
    rows = []
    for part in range(3):
        rows += [one] + [b[part] for b in back] + [s[part] for s in scaled] + [const[part]]
    for part, source in ((0, 0), (1, 1), (2, 0)):
        rows += [square[part]] + [b[source] for b in back] + [s[source] for s in scaled] + [zero]
    return rows


def near_target_rows(x):
    one = jnp.ones_like(x[0])
    zero = jnp.zeros_like(x[0])
    norm = split3(x[0] * x[0] + x[1] * x[1] + x[2] * x[2])
    pieces = [split3(entry) for entry in x]
    rows = []
    for part in range(3):
        high = [p[0] for p in pieces]
        rows += [norm[part]] + high + high + [one]
    for target in (1, 1, 2):
        chosen = [p[target] for p in pieces]
        rows += [one] + chosen + chosen + [zero]
    return rows


def near_kernel(
    cells,
    devices,
    n_col,
    near_ref,
    own_ref,
    prev_ref,
    next_ref,
    centre_ref,
    far_ref,
    let_ref,
    top_ref,
    near_out,
    let_out,
    top_out,
    near_sources,
    near_targets,
    far_sources,
    far_coeffs,
    far_targets,
    masks,
    near_sums,
    far_sums,
    field,
    prev_planes,
    next_planes,
    fetch_sem,
):
    fetches = [
        pltpu.make_async_copy(prev_ref, prev_planes, fetch_sem.at[0]),
        pltpu.make_async_copy(next_ref, next_planes, fetch_sem.at[1]),
    ]
    for fetch in fetches:
        fetch.start()

    sublane = lax.broadcasted_iota(jnp.int32, (8, CELL), 0)
    lane = lax.broadcasted_iota(jnp.int32, (8, CELL), 1)
    diagonal = lax.broadcasted_iota(jnp.int32, (CELL, CELL), 0) == lax.broadcasted_iota(
        jnp.int32, (CELL, CELL), 1
    )
    masks[0:CELL, :] = jnp.zeros((CELL, CELL), F32)
    masks[CELL : 2 * CELL, :] = jnp.where(diagonal, 1e30, 0.0)

    def build_sources(ref, first, keep):
        def build(group, carry):
            y = own_offsets(ref, centre_ref, cells, group * 8)
            moment = [ref[rows8((3 + i) * pitch_of(cells) + group * 8), :] for i in range(3)]
            if keep is not None:
                moment = [jnp.where(keep, entry, 0.0) for entry in moment]
            store_rows(near_sources, near_source_rows(y, moment), first + group * 8, NEAR_S)
            return carry

        lax.fori_loop(0, cells // 8, build, 0, unroll=2)

    device = lax.axis_index("row") * n_col + lax.axis_index("col")
    ordinal = jnp.full((8, CELL), device, jnp.int32)
    build_sources(own_ref, cells, None)

    def build_targets(group, carry):
        x = own_offsets(own_ref, centre_ref, cells, group * 8)
        store_rows(near_targets, near_target_rows(x), group * 8, NEAR_S)
        store_rows(far_targets, target_rows(x), group * 8, FAR_S)
        return carry

    lax.fori_loop(0, cells // 8, build_targets, 0, unroll=2)

    groups = cells // 8
    lists = far_ref[...].astype(F32)
    lists = jnp.concatenate([lists, jnp.zeros((lists.shape[0], 256 - cells), F32)], axis=1)
    lists = jnp.concatenate([lists, jnp.zeros((CELL - lists.shape[0], 256), F32)], axis=0)
    far_sums[0:256, :] = lists.T
    repeated = jnp.bitwise_and(lax.broadcasted_iota(jnp.int32, (groups, CELL), 1), 15)
    slot = jnp.right_shift(lax.broadcasted_iota(jnp.int32, (groups, CELL), 1), 4)
    listed = jnp.zeros((groups, CELL), F32)
    for k in range(8):
        rows = far_sums[pl.ds(k, groups, stride=8), :]
        listed = jnp.where(slot == k, jnp.take_along_axis(rows, repeated, axis=1), listed)
    listed = listed.astype(jnp.int32)
    low = jnp.bitwise_and(listed, CELL - 1)
    section = jnp.right_shift(listed, 7)
    dense = []
    for entry in range(15):
        table = let_ref[pl.ds(entry, 8, stride=16), :]
        value = jnp.zeros(listed.shape, F32)
        for k in range(8):
            source = jnp.broadcast_to(table[k : k + 1, :], listed.shape)
            value = jnp.where(section == k, jnp.take_along_axis(source, low, axis=1), value)
        dense.append(value)
    repeat = sublane * 16 + jnp.bitwise_and(lane, 15)
    for entry in range(15):
        far_sums[entry * groups : (entry + 1) * groups, :] = dense[entry]

    def build_far(group, carry):
        table = [
            jnp.take_along_axis(
                jnp.broadcast_to(far_sums[pl.ds(entry * groups + group, 1), :], (8, CELL)),
                repeat,
                axis=1,
            )
            for entry in range(15)
        ]
        table = [table[i] - centre_ref[i : i + 1, :] for i in range(3)] + table[3:]
        square, first, second, outputs = expansion_coefficients(table)
        zero = jnp.zeros((8, CELL), F32)
        forms = [source_rows(form, zero) for form in (square, first, second)]
        rows = [
            jnp.where(lane < 16, a, jnp.where(lane < 32, b, c)) for a, b, c in zip(*forms)
        ]
        store_rows(far_sources, rows, group * 8, FAR_S)
        pieces = [split3(value) for value in outputs]
        rows = []
        for part in range(3):
            for k in range(OUT_K):
                kind = 0 if k < 4 else 1 if k < 7 else 2
                inside = (lane >= 32 * kind) & (lane < 32 * kind + 32)
                rows.append(jnp.where(inside, pieces[k][part], 0.0))
        store_rows(far_coeffs, rows, group * 8, COEF_S)
        return carry

    lax.fori_loop(0, groups, build_far, 0, unroll=2)

    for fetch in fetches:
        fetch.wait()
    build_sources(prev_planes, 0, ordinal > 0)
    build_sources(next_planes, 2 * cells, ordinal < devices - 1)

    upper_rows = lax.rem(lax.broadcasted_iota(jnp.int32, (NEAR_K, CELL), 0), 8) < 4

    def near_part(cell):
        targets = near_targets[pl.ds(pl.multiple_of(cell * NEAR_S, NEAR_S), NEAR_K), :]
        features = jnp.concatenate(
            [jnp.where(upper_rows, targets, 0.0), jnp.where(upper_rows, 0.0, targets)], axis=1
        ).astype(BF16)
        total = None
        for e in range(2):
            block = near_ref[e, cell]
            source = near_sources[pl.ds(pl.multiple_of(block * NEAR_S, NEAR_S), NEAR_K), :]
            values = jnp.dot(source.astype(BF16).T, features, preferred_element_type=F32)
            own = (block == cells + cell).astype(jnp.int32)
            mask = masks[pl.ds(pl.multiple_of(own * CELL, CELL), CELL), :]
            inverse = lax.rsqrt(values[:, :CELL] + mask)
            two = inverse * inverse
            three = two * inverse
            projected = values[:, CELL:] * two * three
            p_high, p_low = split2(projected)
            t_high, t_low = split2(three)
            weights = jnp.concatenate(
                [
                    jnp.concatenate([p_high, t_high], axis=1),
                    jnp.concatenate([p_low, t_low], axis=1),
                ],
                axis=0,
            )
            coeffs = source[:32].astype(BF16)
            result = jnp.dot(
                jnp.concatenate([coeffs, coeffs], axis=1), weights, preferred_element_type=F32
            )
            result = result[0:8] + result[8:16] + result[16:24]
            total = result if total is None else total + result
        near_sums[pl.ds(cell, 8, stride=pitch_of(cells)), :] = jnp.where(
            sublane < 4, total[:, :CELL], total[:, CELL:]
        )

    def far_part(cell):
        source = far_sources[pl.ds(pl.multiple_of(cell * FAR_S, FAR_S), FAR_K), :]
        features = far_targets[pl.ds(pl.multiple_of(cell * FAR_S, FAR_S), FAR_K), :].astype(BF16)
        values = jnp.dot(source.astype(BF16).T[:48], features, preferred_element_type=F32)
        parts = weights_of(values[:16], values[16:32], values[32:48])
        weights = jnp.concatenate([half for part in parts for half in split2(part)], axis=0)
        coeffs = far_coeffs[pl.ds(pl.multiple_of(cell * COEF_S, COEF_S), 48), :][:, :96].astype(BF16)
        result = jnp.dot(coeffs, weights, preferred_element_type=F32)
        result = result[:OUT_K] + result[OUT_K : 2 * OUT_K] + result[2 * OUT_K :]
        far_sums[pl.ds(cell, OUT_K, stride=pitch_of(cells)), :] = result

    def step(pair, carry):
        for sub in range(NEAR_UNROLL):
            near_part(NEAR_UNROLL * pair + sub)
            far_part(NEAR_UNROLL * pair + sub)
        return carry

    lax.fori_loop(0, cells // NEAR_UNROLL, step, 0)

    def finish_near(group, carry):
        x = own_offsets(own_ref, centre_ref, cells, group * 8)
        totals = [near_sums[rows8(k * pitch_of(cells) + group * 8), :] for k in range(7)]
        for i in range(3):
            field[rows8(i * pitch_of(cells) + group * 8), :] = (
                (x[i] * totals[0] - totals[4 + i]) * (1.0 / 3.0) + 0.5 * totals[1 + i]
            )
        return carry

    lax.fori_loop(0, cells // 8, finish_near, 0, unroll=2)
    planes_to_output(field, near_out, cells)

    def finish_far(group, carry):
        x = own_offsets(own_ref, centre_ref, cells, group * 8)
        totals = [far_sums[rows8(k * pitch_of(cells) + group * 8), :] for k in range(OUT_K)]
        for i, value in enumerate(expansion_fields(x, totals)):
            field[rows8(i * pitch_of(cells) + group * 8), :] = value
        return carry

    lax.fori_loop(0, cells // 8, finish_far, 0, unroll=2)
    planes_to_output(field, let_out, cells)
    planes_to_output(top_ref, top_out, cells)


def vmem(count):
    return [pl.BlockSpec(memory_space=pltpu.VMEM)] * count


def make_first(cells, n_row, n_col):
    bits = n_row.bit_length() + n_col.bit_length() - 2
    sources = 2 * n_col
    planes = jax.ShapeDtypeStruct((6 * pitch_of(cells), CELL), F32)
    return pl.pallas_call(
        functools.partial(first_kernel, cells, n_row, n_col),
        out_shape=(
            planes,
            planes,
            planes,
            jax.ShapeDtypeStruct((bits, 16, CELL), F32),
            jax.ShapeDtypeStruct((8, CELL), F32),
            jax.ShapeDtypeStruct((3 * pitch_of(cells), CELL), F32),
        ),
        in_specs=vmem(3),
        out_specs=tuple(
            vmem(1) + [pl.BlockSpec(memory_space=pl.ANY)] * 2 + vmem(3)
        ),
        scratch_shapes=[
            pltpu.VMEM((bits, 16, CELL), F32),
            pltpu.VMEM((8, CELL), F32),
            pltpu.VMEM((n_col, 8, CELL), F32),
            pltpu.VMEM((cells * FAR_S, CELL), F32),
            pltpu.VMEM((FORMS * FAR_K, CELL), F32),
            pltpu.VMEM((FORMS * sources, FAR_K), F32),
            pltpu.VMEM((FORMS * sources, FAR_K), BF16),
            pltpu.VMEM((6 * sources, CELL), F32),
            pltpu.VMEM((4 * cells * 8, CELL), F32),
            pltpu.SemaphoreType.DMA((12,)),
            pltpu.SemaphoreType.DMA((12,)),
            pltpu.SemaphoreType.DMA((bits,)),
            pltpu.SemaphoreType.DMA((bits,)),
            pltpu.SemaphoreType.DMA((n_col,)),
            pltpu.SemaphoreType.DMA((n_col,)),
        ],
        compiler_params=pltpu.CompilerParams(
            collective_id=0, has_side_effects=True, vmem_limit_bytes=VMEM_LIMIT
        ),
        cost_estimate=pl.CostEstimate(
            flops=8_000_000_000, bytes_accessed=4_000_000, transcendentals=1_600_000
        ),
        name="tables_exchange_top",
    )


def make_near(cells, devices, n_col, n):
    return pl.pallas_call(
        functools.partial(near_kernel, cells, devices, n_col),
        out_shape=(jax.ShapeDtypeStruct((3, n), F32),) * 3,
        in_specs=[pl.BlockSpec(memory_space=pltpu.SMEM)]
        + vmem(1)
        + [pl.BlockSpec(memory_space=pl.ANY)] * 2
        + vmem(4),
        out_specs=tuple(vmem(3)),
        scratch_shapes=[
            pltpu.VMEM((3 * cells * NEAR_S, CELL), F32),
            pltpu.VMEM((cells * NEAR_S, CELL), F32),
            pltpu.VMEM((cells * FAR_S, CELL), F32),
            pltpu.VMEM((cells * COEF_S, CELL), F32),
            pltpu.VMEM((cells * FAR_S, CELL), F32),
            pltpu.VMEM((2 * CELL, CELL), F32),
            pltpu.VMEM((8 * pitch_of(cells), CELL), F32),
            pltpu.VMEM((OUT_K * pitch_of(cells), CELL), F32),
            pltpu.VMEM((3 * pitch_of(cells), CELL), F32),
            pltpu.VMEM((6 * pitch_of(cells), CELL), F32),
            pltpu.VMEM((6 * pitch_of(cells), CELL), F32),
            pltpu.SemaphoreType.DMA((2,)),
        ],
        compiler_params=pltpu.CompilerParams(vmem_limit_bytes=VMEM_LIMIT),
        cost_estimate=pl.CostEstimate(
            flops=30_000_000_000, bytes_accessed=4_000_000, transcendentals=6_600_000
        ),
        name="near_and_let_field",
    )


def body(positions, moments, near_list, far_list, let_rows):
    n = positions.shape[1]
    cells = n // CELL
    n_row, n_col = lax.axis_size("row"), lax.axis_size("col")
    bits = let_rows.shape[1]
    planes, before, after, let_in, centre, top = make_first(cells, n_row, n_col)(
        positions, moments, let_rows
    )
    return make_near(cells, n_row * n_col, n_col, n)(
        near_list.T,
        planes,
        before,
        after,
        centre,
        far_list.T,
        let_in.reshape(bits * 16, CELL),
        top,
    )


def solution(mesh):
    return jax.shard_map(
        body,
        mesh=mesh,
        in_specs=(
            P(None, ("row", "col")),
            P(None, ("row", "col")),
            P(("row", "col"), None),
            P(("row", "col"), None),
            P(("row", "col"), None, None),
        ),
        out_specs=(P(None, ("row", "col")), P(None, ("row", "col")), P(None, ("row", "col"))),
        check_vma=False,
    )
```

```python
import functools

import jax
import jax.numpy as jnp
from jax import lax
from jax.experimental import pallas as pl
from jax.experimental.pallas import tpu as pltpu
from jax.sharding import PartitionSpec as P

CELL = 128
SOFTEN = 0.09
COUPLING = 0.004
F32 = jnp.float32
BF16 = jnp.bfloat16
MESH = pl.DeviceIdType.MESH
VMEM_LIMIT = 58 * 1024 * 1024
SIX = ((0, 0), (0, 1), (0, 2), (1, 1), (1, 2), (2, 2))
NEAR_K = 48
FAR_K = 64
OUT_K = 16
NEAR_S = 56
FAR_S = 72
COEF_S = 56
FORMS = 6
SOURCE_KEPT = (*range(24), 24, 32, 40)
TARGET_KEPT = (*range(8), 8, 16, *range(24, 32), *range(40, 48))
GROUP = 4
TOP_UNROLL = 32
NEAR_UNROLL = 64


def split3(value):
    high = value.astype(BF16).astype(F32)
    rest = value - high
    middle = rest.astype(BF16).astype(F32)
    return high, middle, rest - middle


def split2(value):
    high = value.astype(BF16)
    return high, (value - high.astype(F32)).astype(BF16)


def source_pairing(parts):
    return [parts[0], parts[1], parts[2], parts[0], parts[1], parts[0]]


def target_pairing(parts):
    return [parts[0], parts[0], parts[0], parts[1], parts[1], parts[2]]


def expansion_coefficients(table):
    c = table[0:3]
    m = [COUPLING * entry for entry in table[3:6]]
    q = [[COUPLING * table[6 + 3 * j + i] for i in range(3)] for j in range(3)]
    g = [[q[j][i] + q[i][j] for i in range(3)] for j in range(3)]
    t = q[0][0] + q[1][1] + q[2][2]
    gc = [g[i][0] * c[0] + g[i][1] * c[1] + g[i][2] * c[2] for i in range(3)]
    zero = jnp.zeros_like(c[0])
    one = jnp.ones_like(c[0])
    square = (
        c[0] * c[0] + c[1] * c[1] + c[2] * c[2] + SOFTEN,
        [-2.0 * c[i] for i in range(3)],
        [one if i == j else zero for i, j in SIX],
    )
    first = (
        -3.0 * (c[0] * m[0] + c[1] * m[1] + c[2] * m[2] + t),
        [3.0 * m[i] for i in range(3)],
        None,
    )
    second = (
        7.5 * (c[0] * gc[0] + c[1] * gc[1] + c[2] * gc[2]),
        [-15.0 * gc[i] for i in range(3)],
        [(7.5 if i == j else 15.0) * g[i][j] for i, j in SIX],
    )
    outputs = [one] + list(c) + m + [3.0 * g[i][j] for i, j in SIX] + [3.0 * gc[i] for i in range(3)]
    return square, first, second, outputs


def source_rows(form, zero):
    const, linear, quadratic = form
    rows = list(split3(const))
    for entry in linear:
        rows += source_pairing(split3(entry))
    if quadratic is None:
        rows += [zero] * 36
    else:
        for entry in quadratic:
            rows += source_pairing(split3(entry))
    return rows + [zero] * (FAR_K - len(rows))


def target_rows(x):
    one = jnp.ones_like(x[0])
    rows = [one, one, one]
    for entry in x:
        rows += target_pairing(split3(entry))
    for i, j in SIX:
        rows += target_pairing(split3(x[i] * x[j]))
    return rows + [jnp.zeros_like(one)] * (FAR_K - len(rows))


def weights_of(square, first, second):
    inverse = lax.rsqrt(square)
    two = inverse * inverse
    three = two * inverse
    five = three * two
    return five * (first + second * two), three, five


def expansion_fields(x, sums):
    g = {}
    for place, (i, j) in enumerate(SIX):
        g[i, j] = g[j, i] = sums[7 + place]
    return [
        x[i] * sums[0]
        - sums[1 + i]
        - sums[4 + i]
        - (g[i, 0] * x[0] + g[i, 1] * x[1] + g[i, 2] * x[2])
        + sums[13 + i]
        for i in range(3)
    ]


def pitch_of(cells):
    return cells + 8 * (1 - cells // 8 % 2)


def rows8(start):
    return pl.ds(pl.multiple_of(start, 8), 8)


def lanes(block):
    return pl.ds(pl.multiple_of(block * CELL, CELL), CELL)


def store_rows(ref, rows, first, stride, kept=None):
    for place, value in enumerate(rows):
        if kept is None or place in kept:
            ref[pl.ds(first * stride + place, 8, stride=stride), :] = value


def own_offsets(planes_ref, centre_ref, cells, start):
    return [
        planes_ref[rows8(i * pitch_of(cells) + start), :] - centre_ref[i : i + 1, :] for i in range(3)
    ]


def planes_to_output(planes_ref, out_ref, cells):
    def step(b, carry):
        out_ref[:, lanes(b)] = planes_ref[pl.ds(b, 3, stride=pitch_of(cells)), :]
        return carry

    lax.fori_loop(0, cells, step, 0, unroll=8)


def lane_iota(shape):
    return lax.broadcasted_iota(jnp.int32, shape, len(shape) - 1)


def spread_sums(planes, targets, terms):
    total = None
    for plane, target in zip(planes, targets):
        parts = jnp.concatenate([part.astype(BF16) for part in split3(plane)[:terms]], axis=1)
        marked = target(lane_iota((terms * CELL, CELL))).astype(F32).astype(BF16)
        value = jnp.dot(parts, marked, preferred_element_type=F32)
        total = value if total is None else total + value
    return total


def leaf_tables(place, moment):
    mean = 1.0 / CELL
    centres = [spread_sums([entry], [lambda l: l >= 0], 3) * mean for entry in place]
    spread = [entry - centre for entry, centre in zip(place, centres)]
    lane = lane_iota(centres[0].shape)
    table = spread_sums(
        moment + [spread[j] * moment[i] for j in range(3) for i in range(3)],
        [lambda l, k=k: l == 3 + k for k in range(12)],
        2,
    )
    inner = (lane >= 6) & (lane < 15)
    by_centre = jnp.zeros_like(table)
    for j in range(3):
        table = jnp.where(lane == j, centres[j], table)
        by_centre = jnp.where(inner & (lane // 3 == 2 + j), centres[j], by_centre)
    by_moment = spread_sums(
        moment,
        [lambda l, i=i: (l >= 6) & (l < 15) & (lax.rem(l, 3) == i) for i in range(3)],
        2,
    )
    return table, by_centre, by_moment


def leaf_sections(table, let_rows_ref, let_ref):
    cells = table.shape[0]
    rows = jnp.concatenate([table, jnp.zeros((256 - cells, CELL), F32)], axis=0).T
    chosen = let_rows_ref[0]
    low = jnp.bitwise_and(chosen, CELL - 1)
    upper = chosen >= CELL
    for entry in range(15):
        row = jnp.broadcast_to(rows[entry : entry + 1, :], (8, 256))
        let_ref[:, entry, :] = jnp.where(
            upper,
            jnp.take_along_axis(row[:, CELL:], low, axis=1),
            jnp.take_along_axis(row[:, :CELL], low, axis=1),
        )
    let_ref[:, 15, :] = jnp.zeros((8, CELL), F32)


def top_tables(table, by_centre, by_moment, top_ref, centre_ref):
    half = table.shape[0] // 2
    sublane = lax.broadcasted_iota(jnp.int32, (8, CELL), 0)
    lane = lane_iota((1, CELL))
    tile = jnp.zeros((8, CELL), F32)
    middle = jnp.zeros((1, CELL), F32)
    for top in range(2):
        part = slice(top * half, (top + 1) * half)
        total = jnp.sum(table[part], axis=0, keepdims=True)
        centre = jnp.sum(by_centre[part], axis=0, keepdims=True) * (1.0 / half)
        moved = jnp.sum((by_centre[part] - centre) * by_moment[part], axis=0, keepdims=True)
        row = jnp.where(lane < 3, total * (1.0 / half), total + moved)
        tile = jnp.where(sublane == top, row, tile)
        middle = middle + 0.5 * row
    top_ref[...] = tile
    for i in range(3):
        centre_ref[i : i + 1, :] = jnp.broadcast_to(middle[:, i : i + 1], (1, CELL))
    centre_ref[3:8, :] = jnp.zeros((5, CELL), F32)


def first_kernel(
    cells,
    n_row,
    n_col,
    pos_ref,
    mom_ref,
    let_rows_ref,
    planes_ref,
    before_ref,
    after_ref,
    let_in,
    centre_ref,
    out_ref,
    let_ref,
    top_ref,
    top_in,
    feats,
    forms_rows,
    forms_stage,
    forms,
    coeffs,
    sums,
    side_send,
    side_recv,
    let_send,
    let_recv,
    top_send,
    top_recv,
):
    row = lax.axis_index("row")
    col = lax.axis_index("col")
    device = row * n_col + col
    devices = n_row * n_col
    col_bits = n_col.bit_length() - 1
    row_bits = n_row.bit_length() - 1
    sources = 2 * n_col
    pitch = pitch_of(cells)

    def flip(value, bit):
        return value + (1 << bit) * (1 - 2 * lax.rem(value // (1 << bit), 2))

    def flip_by(value, mask):
        for bit in range(mask.bit_length()):
            if mask >> bit & 1:
                value = flip(value, bit)
        return value

    def place_of(index):
        return (index // n_col, lax.rem(index, n_col))

    following = place_of(lax.rem(device + 1, devices))
    preceding = place_of(lax.rem(device + devices - 1, devices))

    four = [flip_by(col, k) for k in range(1, GROUP)]
    groups = [flip_by(col, k * GROUP) for k in range(1, n_col // GROUP)]
    barrier = pltpu.get_barrier_semaphore()
    partners = [(row, other) for other in four + groups]
    partners += [(flip(row, bit), col) for bit in range(row_bits)] + [following, preceding]
    for partner in partners:
        pl.semaphore_signal(barrier, inc=1, device_id=partner, device_id_type=MESH)

    def to_planes(b, carry):
        planes_ref[pl.ds(b, 3, stride=pitch), :] = pos_ref[:, lanes(b)]
        planes_ref[pl.ds(3 * pitch + b, 3, stride=pitch), :] = mom_ref[:, lanes(b)]
        return carry

    lax.fori_loop(0, cells, to_planes, 0, unroll=8)

    def side_copy(side, part, target, to):
        rows = slice(part * pitch, (part + 1) * pitch)
        return pltpu.make_async_remote_copy(
            src_ref=planes_ref.at[rows],
            dst_ref=target.at[rows],
            send_sem=side_send.at[6 * side + part],
            recv_sem=side_recv.at[6 * side + part],
            device_id=to,
            device_id_type=MESH,
        )

    place = [planes_ref[i * pitch : i * pitch + cells, :] for i in range(3)]
    moment = [planes_ref[(3 + i) * pitch : (3 + i) * pitch + cells, :] for i in range(3)]
    leaf, by_centre, by_moment = leaf_tables(place, moment)
    top_tables(leaf, by_centre, by_moment, top_ref, centre_ref)
    top_in[col] = top_ref[...]
    pl.semaphore_wait(barrier, len(partners))

    first_copies = [
        pltpu.make_async_remote_copy(
            src_ref=top_ref,
            dst_ref=top_in.at[col],
            send_sem=top_send.at[k],
            recv_sem=top_recv.at[k],
            device_id=(row, other),
            device_id_type=MESH,
        )
        for k, other in enumerate(four)
    ]
    for copy in first_copies:
        copy.start()

    leaf_sections(leaf, let_rows_ref, let_ref)
    sections = []
    for section in range(col_bits + row_bits):
        if section < col_bits:
            partner = (row, flip(col, section))
        else:
            partner = (flip(row, section - col_bits), col)
        sections.append(
            pltpu.make_async_remote_copy(
                src_ref=let_ref.at[section],
                dst_ref=let_in.at[section],
                send_sem=let_send.at[section],
                recv_sem=let_recv.at[section],
                device_id=partner,
                device_id_type=MESH,
            )
        )
    for copy in sections:
        copy.start()

    for copy in first_copies:
        copy.wait()
    mine = pl.ds(col // GROUP * GROUP, GROUP)
    second_copies = [
        pltpu.make_async_remote_copy(
            src_ref=top_in.at[mine],
            dst_ref=top_in.at[mine],
            send_sem=top_send.at[len(four) + k],
            recv_sem=top_recv.at[len(four) + k],
            device_id=(row, other),
            device_id_type=MESH,
        )
        for k, other in enumerate(groups)
    ]
    for copy in second_copies:
        copy.start()
    sides = []
    for part in range(6):
        sides.append(side_copy(0, part, before_ref, following))
        sides.append(side_copy(1, part, after_ref, preceding))
    for copy in sides:
        copy.start()

    def build(group, carry):
        x = own_offsets(planes_ref, centre_ref, cells, group * 8)
        store_rows(feats, target_rows(x), group * 8, FAR_S)
        return carry

    lax.fori_loop(0, cells // 8, build, 0, unroll=2)
    for copy in second_copies:
        copy.wait()
    top_in[col] = jnp.zeros(top_ref.shape, F32)

    table = jnp.concatenate(
        [top_in[:, top, :] for top in range(2)] + [jnp.zeros((CELL - sources, CELL), F32)], axis=0
    )
    table = table.T
    entries = [table[k : k + 1, :] for k in range(15)]
    entries = [entries[i] - centre_ref[i : i + 1, :] for i in range(3)] + entries[3:]
    square, first, second, outputs = expansion_coefficients(entries)
    zero = jnp.zeros_like(entries[0])
    g = [[outputs[7 + SIX.index((min(i, j), max(i, j)))] for j in range(3)] for i in range(3)]
    bent = [(-outputs[13 + i], g[i], None) for i in range(3)]
    for position, form in enumerate([square, first, second] + bent):
        base = position * FAR_K
        for k, value in enumerate(source_rows(form, zero)):
            forms_rows[base + k : base + k + 1, :] = value
    for position in range(FORMS):
        value = forms_rows[position * FAR_K : (position + 1) * FAR_K, :].T
        for tile in range(sources // 8):
            start = (tile * FORMS + position) * 8
            forms_stage[start : start + 8, :] = value[tile * 8 : (tile + 1) * 8, :]
    forms[...] = forms_stage[...].astype(BF16)
    for k, value in enumerate(entries[:3] + outputs[4:7]):
        forms_rows[k : k + 1, :] = value
    columns = forms_rows[0:CELL, :].T
    for k in range(6):
        coeffs[k * sources : (k + 1) * sources, :] = jnp.broadcast_to(
            columns[:sources, k : k + 1], (sources, CELL)
        )

    def step(pair, carry):
        for sub in range(TOP_UNROLL):
            cell = 2 * (TOP_UNROLL * pair + sub)
            features = jnp.concatenate(
                [
                    feats[pl.ds(pl.multiple_of((cell + k) * FAR_S, FAR_S), FAR_K), :]
                    for k in range(2)
                ],
                axis=1,
            ).astype(BF16)
            values = jnp.dot(forms[...], features, preferred_element_type=F32)
            for k in range(2):
                totals = None
                for tile in range(sources // 8):
                    form = [
                        values[
                            (tile * FORMS + f) * 8 : (tile * FORMS + f + 1) * 8,
                            k * CELL : (k + 1) * CELL,
                        ]
                        for f in range(FORMS)
                    ]
                    const = [
                        coeffs[f * sources + tile * 8 : f * sources + (tile + 1) * 8, :]
                        for f in range(6)
                    ]
                    weight, three, five = weights_of(*form[:3])
                    terms = [weight] + [
                        const[i] * weight + const[3 + i] * three + form[3 + i] * five
                        for i in range(3)
                    ]
                    totals = terms if totals is None else [t + u for t, u in zip(totals, terms)]
                for place_, value in enumerate(totals):
                    sums[rows8((place_ * cells + cell + k) * 8), :] = value
        return carry

    lax.fori_loop(0, cells // (2 * TOP_UNROLL), step, 0)

    def finish_top(group, carry):
        x = own_offsets(planes_ref, centre_ref, cells, group * 8)
        totals = []
        for place_ in range(4):
            base = (place_ * cells + group * 8) * 8
            parts = [sums[pl.ds(base + k, 8, stride=8), :] for k in range(8)]
            while len(parts) > 1:
                parts = [parts[k] + parts[k + 1] for k in range(0, len(parts), 2)]
            totals.append(parts[0])
        for i in range(3):
            out_ref[rows8(i * pitch + group * 8), :] = x[i] * totals[0] - totals[1 + i]
        return carry

    lax.fori_loop(0, cells // 8, finish_top, 0, unroll=2)

    for copy in sections:
        copy.wait()
    for copy in sides:
        copy.wait()


def near_source_rows(y, moment):
    zero = jnp.zeros_like(y[0])
    one = jnp.ones_like(y[0])
    back = [split3(-2.0 * entry) for entry in y]
    square = split3(y[0] * y[0] + y[1] * y[1] + y[2] * y[2] + SOFTEN)
    scaled = [(3.0 * COUPLING) * entry for entry in moment]
    const = split3(-(y[0] * scaled[0] + y[1] * scaled[1] + y[2] * scaled[2]))
    scaled = [split3(entry) for entry in scaled]
    rows = []
    for part in range(3):
        rows += [one] + [b[part] for b in back] + [s[part] for s in scaled] + [const[part]]
    for part, source in ((0, 0), (1, 1), (2, 0)):
        rows += [square[part]] + [b[source] for b in back] + [s[source] for s in scaled] + [zero]
    return rows


def near_target_rows(x):
    one = jnp.ones_like(x[0])
    zero = jnp.zeros_like(x[0])
    norm = split3(x[0] * x[0] + x[1] * x[1] + x[2] * x[2])
    pieces = [split3(entry) for entry in x]
    rows = []
    for part in range(3):
        high = [p[0] for p in pieces]
        rows += [norm[part]] + high + high + [one]
    for target in (1, 1, 2):
        chosen = [p[target] for p in pieces]
        rows += [one] + chosen + chosen + [zero]
    return rows


def near_kernel(
    cells,
    devices,
    n_col,
    near_ref,
    own_ref,
    prev_ref,
    next_ref,
    centre_ref,
    far_ref,
    let_ref,
    top_ref,
    near_out,
    let_out,
    top_out,
    near_sources,
    near_targets,
    far_sources,
    far_coeffs,
    far_targets,
    masks,
    near_sums,
    far_sums,
    field,
    prev_planes,
    next_planes,
    fetch_sem,
):
    fetches = [
        pltpu.make_async_copy(prev_ref, prev_planes, fetch_sem.at[0]),
        pltpu.make_async_copy(next_ref, next_planes, fetch_sem.at[1]),
    ]
    for fetch in fetches:
        fetch.start()

    sublane = lax.broadcasted_iota(jnp.int32, (8, CELL), 0)
    lane = lax.broadcasted_iota(jnp.int32, (8, CELL), 1)
    diagonal = lax.broadcasted_iota(jnp.int32, (CELL, CELL), 0) == lax.broadcasted_iota(
        jnp.int32, (CELL, CELL), 1
    )
    masks[0:CELL, :] = jnp.zeros((CELL, CELL), F32)
    masks[CELL : 2 * CELL, :] = jnp.where(diagonal, 1e30, 0.0)

    def build_sources(ref, first, keep):
        def build(group, carry):
            y = own_offsets(ref, centre_ref, cells, group * 8)
            moment = [ref[rows8((3 + i) * pitch_of(cells) + group * 8), :] for i in range(3)]
            if keep is not None:
                moment = [jnp.where(keep, entry, 0.0) for entry in moment]
            rows = near_source_rows(y, moment)
            store_rows(near_sources, rows, first + group * 8, NEAR_S, SOURCE_KEPT)
            return carry

        lax.fori_loop(0, cells // 8, build, 0, unroll=2)

    device = lax.axis_index("row") * n_col + lax.axis_index("col")
    ordinal = jnp.full((8, CELL), device, jnp.int32)
    build_sources(own_ref, cells, None)

    def build_targets(group, carry):
        x = own_offsets(own_ref, centre_ref, cells, group * 8)
        store_rows(near_targets, near_target_rows(x), group * 8, NEAR_S, TARGET_KEPT)
        store_rows(far_targets, target_rows(x), group * 8, FAR_S)
        return carry

    lax.fori_loop(0, cells // 8, build_targets, 0, unroll=2)

    groups = cells // 8
    lists = far_ref[...].astype(F32)
    lists = jnp.concatenate([lists, jnp.zeros((lists.shape[0], 256 - cells), F32)], axis=1)
    lists = jnp.concatenate([lists, jnp.zeros((CELL - lists.shape[0], 256), F32)], axis=0)
    far_sums[0:256, :] = lists.T
    repeated = jnp.bitwise_and(lax.broadcasted_iota(jnp.int32, (groups, CELL), 1), 15)
    slot = jnp.right_shift(lax.broadcasted_iota(jnp.int32, (groups, CELL), 1), 4)
    listed = jnp.zeros((groups, CELL), F32)
    for k in range(8):
        rows = far_sums[pl.ds(k, groups, stride=8), :]
        listed = jnp.where(slot == k, jnp.take_along_axis(rows, repeated, axis=1), listed)
    listed = listed.astype(jnp.int32)
    low = jnp.bitwise_and(listed, CELL - 1)
    section = jnp.right_shift(listed, 7)
    dense = []
    for entry in range(15):
        table = let_ref[pl.ds(entry, 8, stride=16), :]
        value = jnp.zeros(listed.shape, F32)
        for k in range(8):
            source = jnp.broadcast_to(table[k : k + 1, :], listed.shape)
            value = jnp.where(section == k, jnp.take_along_axis(source, low, axis=1), value)
        dense.append(value)
    repeat = sublane * 16 + jnp.bitwise_and(lane, 15)
    for entry in range(15):
        far_sums[entry * groups : (entry + 1) * groups, :] = dense[entry]

    def build_far(group, carry):
        table = [
            jnp.take_along_axis(
                jnp.broadcast_to(far_sums[pl.ds(entry * groups + group, 1), :], (8, CELL)),
                repeat,
                axis=1,
            )
            for entry in range(15)
        ]
        table = [table[i] - centre_ref[i : i + 1, :] for i in range(3)] + table[3:]
        square, first, second, outputs = expansion_coefficients(table)
        zero = jnp.zeros((8, CELL), F32)
        forms = [source_rows(form, zero) for form in (square, first, second)]
        rows = [
            jnp.where(lane < 16, a, jnp.where(lane < 32, b, c)) for a, b, c in zip(*forms)
        ]
        store_rows(far_sources, rows, group * 8, FAR_S)
        pieces = [split3(value) for value in outputs]
        rows = []
        for part in range(3):
            for k in range(OUT_K):
                kind = 0 if k < 4 else 1 if k < 7 else 2
                inside = (lane >= 32 * kind) & (lane < 32 * kind + 32)
                rows.append(jnp.where(inside, pieces[k][part], 0.0))
        store_rows(far_coeffs, rows, group * 8, COEF_S)
        return carry

    lax.fori_loop(0, groups, build_far, 0, unroll=2)

    for fetch in fetches:
        fetch.wait()
    build_sources(prev_planes, 0, ordinal > 0)
    build_sources(next_planes, 2 * cells, ordinal < devices - 1)

    upper_rows = lax.rem(lax.broadcasted_iota(jnp.int32, (NEAR_K, CELL), 0), 8) < 4

    def near_part(cell):
        kept = near_targets[pl.ds(pl.multiple_of(cell * NEAR_S, NEAR_S), NEAR_K), :]
        tiles = [kept[8 * k : 8 * k + 8] for k in range(6)]
        for k in (1, 2):
            tiles[k] = jnp.where(sublane == 0, tiles[k], tiles[0])
        tiles[4] = tiles[3]
        targets = jnp.concatenate(tiles, axis=0)
        features = jnp.concatenate(
            [jnp.where(upper_rows, targets, 0.0), jnp.where(upper_rows, 0.0, targets)], axis=1
        ).astype(BF16)
        total = None
        for e in range(2):
            block = near_ref[e, cell]
            kept = near_sources[pl.ds(pl.multiple_of(block * NEAR_S, NEAR_S), NEAR_K), :]
            tiles = [kept[8 * k : 8 * k + 8] for k in range(6)]
            for k, origin in ((3, 0), (4, 1), (5, 0)):
                tiles[k] = jnp.where(sublane == 0, tiles[k], tiles[origin])
            source = jnp.concatenate(tiles, axis=0)
            values = jnp.dot(source.astype(BF16).T, features, preferred_element_type=F32)
            own = (block == cells + cell).astype(jnp.int32)
            mask = masks[pl.ds(pl.multiple_of(own * CELL, CELL), CELL), :]
            inverse = lax.rsqrt(values[:, :CELL] + mask)
            two = inverse * inverse
            three = two * inverse
            projected = values[:, CELL:] * two * three
            p_high, p_low = split2(projected)
            t_high, t_low = split2(three)
            weights = jnp.concatenate(
                [
                    jnp.concatenate([p_high, t_high], axis=1),
                    jnp.concatenate([p_low, t_low], axis=1),
                ],
                axis=0,
            )
            coeffs = source[:32].astype(BF16)
            result = jnp.dot(
                jnp.concatenate([coeffs, coeffs], axis=1), weights, preferred_element_type=F32
            )
            result = result[0:8] + result[8:16] + result[16:24]
            total = result if total is None else total + result
        near_sums[pl.ds(cell, 8, stride=pitch_of(cells)), :] = jnp.where(
            sublane < 4, total[:, :CELL], total[:, CELL:]
        )

    def far_part(cell):
        source = far_sources[pl.ds(pl.multiple_of(cell * FAR_S, FAR_S), FAR_K), :]
        features = far_targets[pl.ds(pl.multiple_of(cell * FAR_S, FAR_S), FAR_K), :].astype(BF16)
        values = jnp.dot(source.astype(BF16).T[:48], features, preferred_element_type=F32)
        parts = weights_of(values[:16], values[16:32], values[32:48])
        weights = jnp.concatenate([half for part in parts for half in split2(part)], axis=0)
        coeffs = far_coeffs[pl.ds(pl.multiple_of(cell * COEF_S, COEF_S), 48), :][:, :96].astype(BF16)
        result = jnp.dot(coeffs, weights, preferred_element_type=F32)
        result = result[:OUT_K] + result[OUT_K : 2 * OUT_K] + result[2 * OUT_K :]
        far_sums[pl.ds(cell, OUT_K, stride=pitch_of(cells)), :] = result

    def step(pair, carry):
        for sub in range(NEAR_UNROLL):
            near_part(NEAR_UNROLL * pair + sub)
            far_part(NEAR_UNROLL * pair + sub)
        return carry

    lax.fori_loop(0, cells // NEAR_UNROLL, step, 0)

    def finish_near(group, carry):
        x = own_offsets(own_ref, centre_ref, cells, group * 8)
        totals = [near_sums[rows8(k * pitch_of(cells) + group * 8), :] for k in range(7)]
        for i in range(3):
            field[rows8(i * pitch_of(cells) + group * 8), :] = (
                (x[i] * totals[0] - totals[4 + i]) * (1.0 / 3.0) + 0.5 * totals[1 + i]
            )
        return carry

    lax.fori_loop(0, cells // 8, finish_near, 0, unroll=2)
    planes_to_output(field, near_out, cells)

    def finish_far(group, carry):
        x = own_offsets(own_ref, centre_ref, cells, group * 8)
        totals = [far_sums[rows8(k * pitch_of(cells) + group * 8), :] for k in range(OUT_K)]
        for i, value in enumerate(expansion_fields(x, totals)):
            field[rows8(i * pitch_of(cells) + group * 8), :] = value
        return carry

    lax.fori_loop(0, cells // 8, finish_far, 0, unroll=2)
    planes_to_output(field, let_out, cells)
    planes_to_output(top_ref, top_out, cells)


def vmem(count):
    return [pl.BlockSpec(memory_space=pltpu.VMEM)] * count


def make_first(cells, n_row, n_col):
    bits = n_row.bit_length() + n_col.bit_length() - 2
    sources = 2 * n_col
    planes = jax.ShapeDtypeStruct((6 * pitch_of(cells), CELL), F32)
    return pl.pallas_call(
        functools.partial(first_kernel, cells, n_row, n_col),
        out_shape=(
            planes,
            planes,
            planes,
            jax.ShapeDtypeStruct((bits, 16, CELL), F32),
            jax.ShapeDtypeStruct((8, CELL), F32),
            jax.ShapeDtypeStruct((3 * pitch_of(cells), CELL), F32),
        ),
        in_specs=vmem(3),
        out_specs=tuple(
            vmem(1) + [pl.BlockSpec(memory_space=pl.ANY)] * 2 + vmem(3)
        ),
        scratch_shapes=[
            pltpu.VMEM((bits, 16, CELL), F32),
            pltpu.VMEM((8, CELL), F32),
            pltpu.VMEM((n_col, 8, CELL), F32),
            pltpu.VMEM((cells * FAR_S, CELL), F32),
            pltpu.VMEM((FORMS * FAR_K, CELL), F32),
            pltpu.VMEM((FORMS * sources, FAR_K), F32),
            pltpu.VMEM((FORMS * sources, FAR_K), BF16),
            pltpu.VMEM((6 * sources, CELL), F32),
            pltpu.VMEM((4 * cells * 8, CELL), F32),
            pltpu.SemaphoreType.DMA((12,)),
            pltpu.SemaphoreType.DMA((12,)),
            pltpu.SemaphoreType.DMA((bits,)),
            pltpu.SemaphoreType.DMA((bits,)),
            pltpu.SemaphoreType.DMA((n_col,)),
            pltpu.SemaphoreType.DMA((n_col,)),
        ],
        compiler_params=pltpu.CompilerParams(
            collective_id=0, has_side_effects=True, vmem_limit_bytes=VMEM_LIMIT
        ),
        cost_estimate=pl.CostEstimate(
            flops=8_000_000_000, bytes_accessed=4_000_000, transcendentals=1_600_000
        ),
        name="tables_exchange_top",
    )


def make_near(cells, devices, n_col, n):
    return pl.pallas_call(
        functools.partial(near_kernel, cells, devices, n_col),
        out_shape=(jax.ShapeDtypeStruct((3, n), F32),) * 3,
        in_specs=[pl.BlockSpec(memory_space=pltpu.SMEM)]
        + vmem(1)
        + [pl.BlockSpec(memory_space=pl.ANY)] * 2
        + vmem(4),
        out_specs=tuple(vmem(3)),
        scratch_shapes=[
            pltpu.VMEM((3 * cells * NEAR_S, CELL), F32),
            pltpu.VMEM((cells * NEAR_S, CELL), F32),
            pltpu.VMEM((cells * FAR_S, CELL), F32),
            pltpu.VMEM((cells * COEF_S, CELL), F32),
            pltpu.VMEM((cells * FAR_S, CELL), F32),
            pltpu.VMEM((2 * CELL, CELL), F32),
            pltpu.VMEM((8 * pitch_of(cells), CELL), F32),
            pltpu.VMEM((OUT_K * pitch_of(cells), CELL), F32),
            pltpu.VMEM((3 * pitch_of(cells), CELL), F32),
            pltpu.VMEM((6 * pitch_of(cells), CELL), F32),
            pltpu.VMEM((6 * pitch_of(cells), CELL), F32),
            pltpu.SemaphoreType.DMA((2,)),
        ],
        compiler_params=pltpu.CompilerParams(vmem_limit_bytes=VMEM_LIMIT),
        cost_estimate=pl.CostEstimate(
            flops=30_000_000_000, bytes_accessed=4_000_000, transcendentals=6_600_000
        ),
        name="near_and_let_field",
    )


def body(positions, moments, near_list, far_list, let_rows):
    n = positions.shape[1]
    cells = n // CELL
    n_row, n_col = lax.axis_size("row"), lax.axis_size("col")
    bits = let_rows.shape[1]
    planes, before, after, let_in, centre, top = make_first(cells, n_row, n_col)(
        positions, moments, let_rows
    )
    return make_near(cells, n_row * n_col, n_col, n)(
        near_list.T,
        planes,
        before,
        after,
        centre,
        far_list.T,
        let_in.reshape(bits * 16, CELL),
        top,
    )


def solution(mesh):
    return jax.shard_map(
        body,
        mesh=mesh,
        in_specs=(
            P(None, ("row", "col")),
            P(None, ("row", "col")),
            P(("row", "col"), None),
            P(("row", "col"), None),
            P(("row", "col"), None, None),
        ),
        out_specs=(P(None, ("row", "col")), P(None, ("row", "col")), P(None, ("row", "col"))),
        check_vma=False,
    )
```

```python
import functools

import jax
import jax.numpy as jnp
from jax import lax
from jax.experimental import pallas as pl
from jax.experimental.pallas import tpu as pltpu
from jax.sharding import PartitionSpec as P

CELL = 128
SOFTEN = 0.09
COUPLING = 0.004
F32 = jnp.float32
BF16 = jnp.bfloat16
MESH = pl.DeviceIdType.MESH
VMEM_LIMIT = 58 * 1024 * 1024
SIX = ((0, 0), (0, 1), (0, 2), (1, 1), (1, 2), (2, 2))
NEAR_K = 48
FAR_K = 64
OUT_K = 16
NEAR_S = 56
FAR_S = 72
COEF_S = 56
FORMS = 6
SOURCE_KEPT = (*range(24), 24, 32, 40)
TARGET_KEPT = (*range(8), 8, 16, *range(24, 32), *range(40, 48))
GROUP = 4
TOP_UNROLL = 48
NEAR_UNROLL = 96


def split3(value):
    high = value.astype(BF16).astype(F32)
    rest = value - high
    middle = rest.astype(BF16).astype(F32)
    return high, middle, rest - middle


def split2(value):
    high = value.astype(BF16)
    return high, (value - high.astype(F32)).astype(BF16)


def source_pairing(parts):
    return [parts[0], parts[1], parts[2], parts[0], parts[1], parts[0]]


def target_pairing(parts):
    return [parts[0], parts[0], parts[0], parts[1], parts[1], parts[2]]


def expansion_coefficients(table):
    c = table[0:3]
    m = [COUPLING * entry for entry in table[3:6]]
    q = [[COUPLING * table[6 + 3 * j + i] for i in range(3)] for j in range(3)]
    g = [[q[j][i] + q[i][j] for i in range(3)] for j in range(3)]
    t = q[0][0] + q[1][1] + q[2][2]
    gc = [g[i][0] * c[0] + g[i][1] * c[1] + g[i][2] * c[2] for i in range(3)]
    zero = jnp.zeros_like(c[0])
    one = jnp.ones_like(c[0])
    square = (
        c[0] * c[0] + c[1] * c[1] + c[2] * c[2] + SOFTEN,
        [-2.0 * c[i] for i in range(3)],
        [one if i == j else zero for i, j in SIX],
    )
    first = (
        -3.0 * (c[0] * m[0] + c[1] * m[1] + c[2] * m[2] + t),
        [3.0 * m[i] for i in range(3)],
        None,
    )
    second = (
        7.5 * (c[0] * gc[0] + c[1] * gc[1] + c[2] * gc[2]),
        [-15.0 * gc[i] for i in range(3)],
        [(7.5 if i == j else 15.0) * g[i][j] for i, j in SIX],
    )
    outputs = [one] + list(c) + m + [3.0 * g[i][j] for i, j in SIX] + [3.0 * gc[i] for i in range(3)]
    return square, first, second, outputs


def source_rows(form, zero):
    const, linear, quadratic = form
    rows = list(split3(const))
    for entry in linear:
        rows += source_pairing(split3(entry))
    if quadratic is None:
        rows += [zero] * 36
    else:
        for entry in quadratic:
            rows += source_pairing(split3(entry))
    return rows + [zero] * (FAR_K - len(rows))


def target_rows(x):
    one = jnp.ones_like(x[0])
    rows = [one, one, one]
    for entry in x:
        rows += target_pairing(split3(entry))
    for i, j in SIX:
        rows += target_pairing(split3(x[i] * x[j]))
    return rows + [jnp.zeros_like(one)] * (FAR_K - len(rows))


def weights_of(square, first, second):
    inverse = lax.rsqrt(square)
    two = inverse * inverse
    three = two * inverse
    five = three * two
    return five * (first + second * two), three, five


def expansion_fields(x, sums):
    g = {}
    for place, (i, j) in enumerate(SIX):
        g[i, j] = g[j, i] = sums[7 + place]
    return [
        x[i] * sums[0]
        - sums[1 + i]
        - sums[4 + i]
        - (g[i, 0] * x[0] + g[i, 1] * x[1] + g[i, 2] * x[2])
        + sums[13 + i]
        for i in range(3)
    ]


def pitch_of(cells):
    return cells + 8 * (1 - cells // 8 % 2)


def rows8(start):
    return pl.ds(pl.multiple_of(start, 8), 8)


def lanes(block):
    return pl.ds(pl.multiple_of(block * CELL, CELL), CELL)


def store_rows(ref, rows, first, stride, kept=None):
    for place, value in enumerate(rows):
        if kept is None or place in kept:
            ref[pl.ds(first * stride + place, 8, stride=stride), :] = value


def own_offsets(planes_ref, centre_ref, cells, start):
    return [
        planes_ref[rows8(i * pitch_of(cells) + start), :] - centre_ref[i : i + 1, :] for i in range(3)
    ]


def planes_to_output(planes_ref, out_ref, cells):
    def step(b, carry):
        out_ref[:, lanes(b)] = planes_ref[pl.ds(b, 3, stride=pitch_of(cells)), :]
        return carry

    lax.fori_loop(0, cells, step, 0, unroll=8)


def lane_iota(shape):
    return lax.broadcasted_iota(jnp.int32, shape, len(shape) - 1)


def spread_sums(planes, targets, terms):
    total = None
    for plane, target in zip(planes, targets):
        parts = jnp.concatenate([part.astype(BF16) for part in split3(plane)[:terms]], axis=1)
        marked = target(lane_iota((terms * CELL, CELL))).astype(F32).astype(BF16)
        value = jnp.dot(parts, marked, preferred_element_type=F32)
        total = value if total is None else total + value
    return total


def leaf_tables(place, moment):
    mean = 1.0 / CELL
    centres = [spread_sums([entry], [lambda l: l >= 0], 3) * mean for entry in place]
    spread = [entry - centre for entry, centre in zip(place, centres)]
    lane = lane_iota(centres[0].shape)
    table = spread_sums(
        moment + [spread[j] * moment[i] for j in range(3) for i in range(3)],
        [lambda l, k=k: l == 3 + k for k in range(12)],
        2,
    )
    inner = (lane >= 6) & (lane < 15)
    by_centre = jnp.zeros_like(table)
    for j in range(3):
        table = jnp.where(lane == j, centres[j], table)
        by_centre = jnp.where(inner & (lane // 3 == 2 + j), centres[j], by_centre)
    by_moment = spread_sums(
        moment,
        [lambda l, i=i: (l >= 6) & (l < 15) & (lax.rem(l, 3) == i) for i in range(3)],
        2,
    )
    return table, by_centre, by_moment


def leaf_sections(table, let_rows_ref, let_ref):
    cells = table.shape[0]
    rows = jnp.concatenate([table, jnp.zeros((256 - cells, CELL), F32)], axis=0).T
    chosen = let_rows_ref[0]
    low = jnp.bitwise_and(chosen, CELL - 1)
    upper = chosen >= CELL
    for entry in range(15):
        row = jnp.broadcast_to(rows[entry : entry + 1, :], (8, 256))
        let_ref[:, entry, :] = jnp.where(
            upper,
            jnp.take_along_axis(row[:, CELL:], low, axis=1),
            jnp.take_along_axis(row[:, :CELL], low, axis=1),
        )
    let_ref[:, 15, :] = jnp.zeros((8, CELL), F32)


def top_tables(table, by_centre, by_moment, top_ref, centre_ref):
    half = table.shape[0] // 2
    sublane = lax.broadcasted_iota(jnp.int32, (8, CELL), 0)
    lane = lane_iota((1, CELL))
    tile = jnp.zeros((8, CELL), F32)
    middle = jnp.zeros((1, CELL), F32)
    for top in range(2):
        part = slice(top * half, (top + 1) * half)
        total = jnp.sum(table[part], axis=0, keepdims=True)
        centre = jnp.sum(by_centre[part], axis=0, keepdims=True) * (1.0 / half)
        moved = jnp.sum((by_centre[part] - centre) * by_moment[part], axis=0, keepdims=True)
        row = jnp.where(lane < 3, total * (1.0 / half), total + moved)
        tile = jnp.where(sublane == top, row, tile)
        middle = middle + 0.5 * row
    top_ref[...] = tile
    for i in range(3):
        centre_ref[i : i + 1, :] = jnp.broadcast_to(middle[:, i : i + 1], (1, CELL))
    centre_ref[3:8, :] = jnp.zeros((5, CELL), F32)


def first_kernel(
    cells,
    n_row,
    n_col,
    pos_ref,
    mom_ref,
    let_rows_ref,
    planes_ref,
    before_ref,
    after_ref,
    let_in,
    centre_ref,
    out_ref,
    let_ref,
    top_ref,
    top_in,
    feats,
    forms_rows,
    forms_stage,
    forms,
    coeffs,
    sums,
    side_send,
    side_recv,
    let_send,
    let_recv,
    top_send,
    top_recv,
):
    row = lax.axis_index("row")
    col = lax.axis_index("col")
    device = row * n_col + col
    devices = n_row * n_col
    col_bits = n_col.bit_length() - 1
    row_bits = n_row.bit_length() - 1
    sources = 2 * n_col
    pitch = pitch_of(cells)

    def flip(value, bit):
        return value + (1 << bit) * (1 - 2 * lax.rem(value // (1 << bit), 2))

    def flip_by(value, mask):
        for bit in range(mask.bit_length()):
            if mask >> bit & 1:
                value = flip(value, bit)
        return value

    def place_of(index):
        return (index // n_col, lax.rem(index, n_col))

    following = place_of(lax.rem(device + 1, devices))
    preceding = place_of(lax.rem(device + devices - 1, devices))

    four = [flip_by(col, k) for k in range(1, GROUP)]
    groups = [flip_by(col, k * GROUP) for k in range(1, n_col // GROUP)]
    barrier = pltpu.get_barrier_semaphore()
    partners = [(row, other) for other in four + groups]
    partners += [(flip(row, bit), col) for bit in range(row_bits)] + [following, preceding]
    for partner in partners:
        pl.semaphore_signal(barrier, inc=1, device_id=partner, device_id_type=MESH)

    def to_planes(b, carry):
        planes_ref[pl.ds(b, 3, stride=pitch), :] = pos_ref[:, lanes(b)]
        planes_ref[pl.ds(3 * pitch + b, 3, stride=pitch), :] = mom_ref[:, lanes(b)]
        return carry

    lax.fori_loop(0, cells, to_planes, 0, unroll=8)

    def side_copy(side, part, target, to):
        rows = slice(part * pitch, (part + 1) * pitch)
        return pltpu.make_async_remote_copy(
            src_ref=planes_ref.at[rows],
            dst_ref=target.at[rows],
            send_sem=side_send.at[6 * side + part],
            recv_sem=side_recv.at[6 * side + part],
            device_id=to,
            device_id_type=MESH,
        )

    place = [planes_ref[i * pitch : i * pitch + cells, :] for i in range(3)]
    moment = [planes_ref[(3 + i) * pitch : (3 + i) * pitch + cells, :] for i in range(3)]
    leaf, by_centre, by_moment = leaf_tables(place, moment)
    top_tables(leaf, by_centre, by_moment, top_ref, centre_ref)
    top_in[col] = top_ref[...]
    pl.semaphore_wait(barrier, len(partners))

    first_copies = [
        pltpu.make_async_remote_copy(
            src_ref=top_ref,
            dst_ref=top_in.at[col],
            send_sem=top_send.at[k],
            recv_sem=top_recv.at[k],
            device_id=(row, other),
            device_id_type=MESH,
        )
        for k, other in enumerate(four)
    ]
    for copy in first_copies:
        copy.start()

    leaf_sections(leaf, let_rows_ref, let_ref)
    sections = []
    for section in range(col_bits + row_bits):
        if section < col_bits:
            partner = (row, flip(col, section))
        else:
            partner = (flip(row, section - col_bits), col)
        sections.append(
            pltpu.make_async_remote_copy(
                src_ref=let_ref.at[section],
                dst_ref=let_in.at[section],
                send_sem=let_send.at[section],
                recv_sem=let_recv.at[section],
                device_id=partner,
                device_id_type=MESH,
            )
        )
    for copy in sections:
        copy.start()

    for copy in first_copies:
        copy.wait()
    mine = pl.ds(col // GROUP * GROUP, GROUP)
    second_copies = [
        pltpu.make_async_remote_copy(
            src_ref=top_in.at[mine],
            dst_ref=top_in.at[mine],
            send_sem=top_send.at[len(four) + k],
            recv_sem=top_recv.at[len(four) + k],
            device_id=(row, other),
            device_id_type=MESH,
        )
        for k, other in enumerate(groups)
    ]
    for copy in second_copies:
        copy.start()
    sides = []
    for part in range(6):
        sides.append(side_copy(0, part, before_ref, following))
        sides.append(side_copy(1, part, after_ref, preceding))
    for copy in sides:
        copy.start()

    def build(group, carry):
        x = own_offsets(planes_ref, centre_ref, cells, group * 8)
        store_rows(feats, target_rows(x), group * 8, FAR_S)
        return carry

    lax.fori_loop(0, cells // 8, build, 0, unroll=2)
    for copy in second_copies:
        copy.wait()
    top_in[col] = jnp.zeros(top_ref.shape, F32)

    table = jnp.concatenate(
        [top_in[:, top, :] for top in range(2)] + [jnp.zeros((CELL - sources, CELL), F32)], axis=0
    )
    table = table.T
    entries = [table[k : k + 1, :] for k in range(15)]
    entries = [entries[i] - centre_ref[i : i + 1, :] for i in range(3)] + entries[3:]
    square, first, second, outputs = expansion_coefficients(entries)
    zero = jnp.zeros_like(entries[0])
    g = [[outputs[7 + SIX.index((min(i, j), max(i, j)))] for j in range(3)] for i in range(3)]
    bent = [(-outputs[13 + i], g[i], None) for i in range(3)]
    for position, form in enumerate([square, first, second] + bent):
        base = position * FAR_K
        for k, value in enumerate(source_rows(form, zero)):
            forms_rows[base + k : base + k + 1, :] = value
    for position in range(FORMS):
        value = forms_rows[position * FAR_K : (position + 1) * FAR_K, :].T
        for tile in range(sources // 8):
            start = (tile * FORMS + position) * 8
            forms_stage[start : start + 8, :] = value[tile * 8 : (tile + 1) * 8, :]
    forms[...] = forms_stage[...].astype(BF16)
    for k, value in enumerate(entries[:3] + outputs[4:7]):
        forms_rows[k : k + 1, :] = value
    columns = forms_rows[0:CELL, :].T
    for k in range(6):
        coeffs[k * sources : (k + 1) * sources, :] = jnp.broadcast_to(
            columns[:sources, k : k + 1], (sources, CELL)
        )

    def step(pair, carry):
        for sub in range(TOP_UNROLL):
            cell = 2 * (TOP_UNROLL * pair + sub)
            features = jnp.concatenate(
                [
                    feats[pl.ds(pl.multiple_of((cell + k) * FAR_S, FAR_S), FAR_K), :]
                    for k in range(2)
                ],
                axis=1,
            ).astype(BF16)
            values = jnp.dot(forms[...], features, preferred_element_type=F32)
            for k in range(2):
                totals = None
                for tile in range(sources // 8):
                    form = [
                        values[
                            (tile * FORMS + f) * 8 : (tile * FORMS + f + 1) * 8,
                            k * CELL : (k + 1) * CELL,
                        ]
                        for f in range(FORMS)
                    ]
                    const = [
                        coeffs[f * sources + tile * 8 : f * sources + (tile + 1) * 8, :]
                        for f in range(6)
                    ]
                    weight, three, five = weights_of(*form[:3])
                    terms = [weight] + [
                        const[i] * weight + const[3 + i] * three + form[3 + i] * five
                        for i in range(3)
                    ]
                    totals = terms if totals is None else [t + u for t, u in zip(totals, terms)]
                for place_, value in enumerate(totals):
                    sums[rows8((place_ * cells + cell + k) * 8), :] = value
        return carry

    lax.fori_loop(0, cells // (2 * TOP_UNROLL), step, 0)

    def finish_top(group, carry):
        x = own_offsets(planes_ref, centre_ref, cells, group * 8)
        totals = []
        for place_ in range(4):
            base = (place_ * cells + group * 8) * 8
            parts = [sums[pl.ds(base + k, 8, stride=8), :] for k in range(8)]
            while len(parts) > 1:
                parts = [parts[k] + parts[k + 1] for k in range(0, len(parts), 2)]
            totals.append(parts[0])
        for i in range(3):
            out_ref[rows8(i * pitch + group * 8), :] = x[i] * totals[0] - totals[1 + i]
        return carry

    lax.fori_loop(0, cells // 8, finish_top, 0, unroll=2)

    for copy in sections:
        copy.wait()
    for copy in sides:
        copy.wait()


def near_source_rows(y, moment):
    zero = jnp.zeros_like(y[0])
    one = jnp.ones_like(y[0])
    back = [split3(-2.0 * entry) for entry in y]
    square = split3(y[0] * y[0] + y[1] * y[1] + y[2] * y[2] + SOFTEN)
    scaled = [(3.0 * COUPLING) * entry for entry in moment]
    const = split3(-(y[0] * scaled[0] + y[1] * scaled[1] + y[2] * scaled[2]))
    scaled = [split3(entry) for entry in scaled]
    rows = []
    for part in range(3):
        rows += [one] + [b[part] for b in back] + [s[part] for s in scaled] + [const[part]]
    for part, source in ((0, 0), (1, 1), (2, 0)):
        rows += [square[part]] + [b[source] for b in back] + [s[source] for s in scaled] + [zero]
    return rows


def near_target_rows(x):
    one = jnp.ones_like(x[0])
    zero = jnp.zeros_like(x[0])
    norm = split3(x[0] * x[0] + x[1] * x[1] + x[2] * x[2])
    pieces = [split3(entry) for entry in x]
    rows = []
    for part in range(3):
        high = [p[0] for p in pieces]
        rows += [norm[part]] + high + high + [one]
    for target in (1, 1, 2):
        chosen = [p[target] for p in pieces]
        rows += [one] + chosen + chosen + [zero]
    return rows


def near_kernel(
    cells,
    devices,
    n_col,
    near_ref,
    own_ref,
    prev_ref,
    next_ref,
    centre_ref,
    far_ref,
    let_ref,
    top_ref,
    near_out,
    let_out,
    top_out,
    near_sources,
    near_targets,
    far_sources,
    far_coeffs,
    far_targets,
    masks,
    near_sums,
    far_sums,
    field,
    prev_planes,
    next_planes,
    fetch_sem,
):
    fetches = [
        pltpu.make_async_copy(prev_ref, prev_planes, fetch_sem.at[0]),
        pltpu.make_async_copy(next_ref, next_planes, fetch_sem.at[1]),
    ]
    for fetch in fetches:
        fetch.start()

    sublane = lax.broadcasted_iota(jnp.int32, (8, CELL), 0)
    lane = lax.broadcasted_iota(jnp.int32, (8, CELL), 1)
    diagonal = lax.broadcasted_iota(jnp.int32, (CELL, CELL), 0) == lax.broadcasted_iota(
        jnp.int32, (CELL, CELL), 1
    )
    masks[0:CELL, :] = jnp.zeros((CELL, CELL), F32)
    masks[CELL : 2 * CELL, :] = jnp.where(diagonal, 1e30, 0.0)

    def build_sources(ref, first, keep):
        def build(group, carry):
            y = own_offsets(ref, centre_ref, cells, group * 8)
            moment = [ref[rows8((3 + i) * pitch_of(cells) + group * 8), :] for i in range(3)]
            if keep is not None:
                moment = [jnp.where(keep, entry, 0.0) for entry in moment]
            rows = near_source_rows(y, moment)
            store_rows(near_sources, rows, first + group * 8, NEAR_S, SOURCE_KEPT)
            return carry

        lax.fori_loop(0, cells // 8, build, 0, unroll=2)

    device = lax.axis_index("row") * n_col + lax.axis_index("col")
    ordinal = jnp.full((8, CELL), device, jnp.int32)
    build_sources(own_ref, cells, None)

    def build_targets(group, carry):
        x = own_offsets(own_ref, centre_ref, cells, group * 8)
        store_rows(near_targets, near_target_rows(x), group * 8, NEAR_S, TARGET_KEPT)
        store_rows(far_targets, target_rows(x), group * 8, FAR_S)
        return carry

    lax.fori_loop(0, cells // 8, build_targets, 0, unroll=2)

    groups = cells // 8
    lists = far_ref[...].astype(F32)
    lists = jnp.concatenate([lists, jnp.zeros((lists.shape[0], 256 - cells), F32)], axis=1)
    lists = jnp.concatenate([lists, jnp.zeros((CELL - lists.shape[0], 256), F32)], axis=0)
    far_sums[0:256, :] = lists.T
    repeated = jnp.bitwise_and(lax.broadcasted_iota(jnp.int32, (groups, CELL), 1), 15)
    slot = jnp.right_shift(lax.broadcasted_iota(jnp.int32, (groups, CELL), 1), 4)
    listed = jnp.zeros((groups, CELL), F32)
    for k in range(8):
        rows = far_sums[pl.ds(k, groups, stride=8), :]
        listed = jnp.where(slot == k, jnp.take_along_axis(rows, repeated, axis=1), listed)
    listed = listed.astype(jnp.int32)
    low = jnp.bitwise_and(listed, CELL - 1)
    section = jnp.right_shift(listed, 7)
    dense = []
    for entry in range(15):
        table = let_ref[pl.ds(entry, 8, stride=16), :]
        value = jnp.zeros(listed.shape, F32)
        for k in range(8):
            source = jnp.broadcast_to(table[k : k + 1, :], listed.shape)
            value = jnp.where(section == k, jnp.take_along_axis(source, low, axis=1), value)
        dense.append(value)
    repeat = sublane * 16 + jnp.bitwise_and(lane, 15)
    for entry in range(15):
        far_sums[entry * groups : (entry + 1) * groups, :] = dense[entry]

    def build_far(group, carry):
        table = [
            jnp.take_along_axis(
                jnp.broadcast_to(far_sums[pl.ds(entry * groups + group, 1), :], (8, CELL)),
                repeat,
                axis=1,
            )
            for entry in range(15)
        ]
        table = [table[i] - centre_ref[i : i + 1, :] for i in range(3)] + table[3:]
        square, first, second, outputs = expansion_coefficients(table)
        zero = jnp.zeros((8, CELL), F32)
        forms = [source_rows(form, zero) for form in (square, first, second)]
        rows = [
            jnp.where(lane < 16, a, jnp.where(lane < 32, b, c)) for a, b, c in zip(*forms)
        ]
        store_rows(far_sources, rows, group * 8, FAR_S)
        pieces = [split3(value) for value in outputs]
        rows = []
        for part in range(3):
            for k in range(OUT_K):
                kind = 0 if k < 4 else 1 if k < 7 else 2
                inside = (lane >= 32 * kind) & (lane < 32 * kind + 32)
                rows.append(jnp.where(inside, pieces[k][part], 0.0))
        store_rows(far_coeffs, rows, group * 8, COEF_S)
        return carry

    lax.fori_loop(0, groups, build_far, 0, unroll=2)

    for fetch in fetches:
        fetch.wait()
    build_sources(prev_planes, 0, ordinal > 0)
    build_sources(next_planes, 2 * cells, ordinal < devices - 1)

    upper_rows = lax.rem(lax.broadcasted_iota(jnp.int32, (NEAR_K, CELL), 0), 8) < 4

    def near_part(cell):
        kept = near_targets[pl.ds(pl.multiple_of(cell * NEAR_S, NEAR_S), NEAR_K), :]
        tiles = [kept[8 * k : 8 * k + 8] for k in range(6)]
        for k in (1, 2):
            tiles[k] = jnp.where(sublane == 0, tiles[k], tiles[0])
        tiles[4] = tiles[3]
        targets = jnp.concatenate(tiles, axis=0)
        features = jnp.concatenate(
            [jnp.where(upper_rows, targets, 0.0), jnp.where(upper_rows, 0.0, targets)], axis=1
        ).astype(BF16)
        total = None
        for e in range(2):
            block = near_ref[e, cell]
            kept = near_sources[pl.ds(pl.multiple_of(block * NEAR_S, NEAR_S), NEAR_K), :]
            tiles = [kept[8 * k : 8 * k + 8] for k in range(6)]
            for k, origin in ((3, 0), (4, 1), (5, 0)):
                tiles[k] = jnp.where(sublane == 0, tiles[k], tiles[origin])
            source = jnp.concatenate(tiles, axis=0)
            values = jnp.dot(source.astype(BF16).T, features, preferred_element_type=F32)
            own = (block == cells + cell).astype(jnp.int32)
            mask = masks[pl.ds(pl.multiple_of(own * CELL, CELL), CELL), :]
            inverse = lax.rsqrt(values[:, :CELL] + mask)
            two = inverse * inverse
            three = two * inverse
            projected = values[:, CELL:] * two * three
            p_high, p_low = split2(projected)
            t_high, t_low = split2(three)
            weights = jnp.concatenate(
                [
                    jnp.concatenate([p_high, t_high], axis=1),
                    jnp.concatenate([p_low, t_low], axis=1),
                ],
                axis=0,
            )
            coeffs = source[:32].astype(BF16)
            result = jnp.dot(
                jnp.concatenate([coeffs, coeffs], axis=1), weights, preferred_element_type=F32
            )
            result = result[0:8] + result[8:16] + result[16:24]
            total = result if total is None else total + result
        near_sums[pl.ds(cell, 8, stride=pitch_of(cells)), :] = jnp.where(
            sublane < 4, total[:, :CELL], total[:, CELL:]
        )

    def far_part(cell):
        source = far_sources[pl.ds(pl.multiple_of(cell * FAR_S, FAR_S), FAR_K), :]
        features = far_targets[pl.ds(pl.multiple_of(cell * FAR_S, FAR_S), FAR_K), :].astype(BF16)
        values = jnp.dot(source.astype(BF16).T[:48], features, preferred_element_type=F32)
        parts = weights_of(values[:16], values[16:32], values[32:48])
        weights = jnp.concatenate([half for part in parts for half in split2(part)], axis=0)
        coeffs = far_coeffs[pl.ds(pl.multiple_of(cell * COEF_S, COEF_S), 48), :][:, :96].astype(BF16)
        result = jnp.dot(coeffs, weights, preferred_element_type=F32)
        result = result[:OUT_K] + result[OUT_K : 2 * OUT_K] + result[2 * OUT_K :]
        far_sums[pl.ds(cell, OUT_K, stride=pitch_of(cells)), :] = result

    def step(pair, carry):
        for sub in range(NEAR_UNROLL):
            near_part(NEAR_UNROLL * pair + sub)
            far_part(NEAR_UNROLL * pair + sub)
        return carry

    lax.fori_loop(0, cells // NEAR_UNROLL, step, 0)

    def finish_near(group, carry):
        x = own_offsets(own_ref, centre_ref, cells, group * 8)
        totals = [near_sums[rows8(k * pitch_of(cells) + group * 8), :] for k in range(7)]
        for i in range(3):
            field[rows8(i * pitch_of(cells) + group * 8), :] = (
                (x[i] * totals[0] - totals[4 + i]) * (1.0 / 3.0) + 0.5 * totals[1 + i]
            )
        return carry

    lax.fori_loop(0, cells // 8, finish_near, 0, unroll=2)
    planes_to_output(field, near_out, cells)

    def finish_far(group, carry):
        x = own_offsets(own_ref, centre_ref, cells, group * 8)
        totals = [far_sums[rows8(k * pitch_of(cells) + group * 8), :] for k in range(OUT_K)]
        for i, value in enumerate(expansion_fields(x, totals)):
            field[rows8(i * pitch_of(cells) + group * 8), :] = value
        return carry

    lax.fori_loop(0, cells // 8, finish_far, 0, unroll=2)
    planes_to_output(field, let_out, cells)
    planes_to_output(top_ref, top_out, cells)


def vmem(count):
    return [pl.BlockSpec(memory_space=pltpu.VMEM)] * count


def make_first(cells, n_row, n_col):
    bits = n_row.bit_length() + n_col.bit_length() - 2
    sources = 2 * n_col
    planes = jax.ShapeDtypeStruct((6 * pitch_of(cells), CELL), F32)
    return pl.pallas_call(
        functools.partial(first_kernel, cells, n_row, n_col),
        out_shape=(
            planes,
            planes,
            planes,
            jax.ShapeDtypeStruct((bits, 16, CELL), F32),
            jax.ShapeDtypeStruct((8, CELL), F32),
            jax.ShapeDtypeStruct((3 * pitch_of(cells), CELL), F32),
        ),
        in_specs=vmem(3),
        out_specs=tuple(
            vmem(1) + [pl.BlockSpec(memory_space=pl.ANY)] * 2 + vmem(3)
        ),
        scratch_shapes=[
            pltpu.VMEM((bits, 16, CELL), F32),
            pltpu.VMEM((8, CELL), F32),
            pltpu.VMEM((n_col, 8, CELL), F32),
            pltpu.VMEM((cells * FAR_S, CELL), F32),
            pltpu.VMEM((FORMS * FAR_K, CELL), F32),
            pltpu.VMEM((FORMS * sources, FAR_K), F32),
            pltpu.VMEM((FORMS * sources, FAR_K), BF16),
            pltpu.VMEM((6 * sources, CELL), F32),
            pltpu.VMEM((4 * cells * 8, CELL), F32),
            pltpu.SemaphoreType.DMA((12,)),
            pltpu.SemaphoreType.DMA((12,)),
            pltpu.SemaphoreType.DMA((bits,)),
            pltpu.SemaphoreType.DMA((bits,)),
            pltpu.SemaphoreType.DMA((n_col,)),
            pltpu.SemaphoreType.DMA((n_col,)),
        ],
        compiler_params=pltpu.CompilerParams(
            collective_id=0, has_side_effects=True, vmem_limit_bytes=VMEM_LIMIT
        ),
        cost_estimate=pl.CostEstimate(
            flops=8_000_000_000, bytes_accessed=4_000_000, transcendentals=1_600_000
        ),
        name="tables_exchange_top",
    )


def make_near(cells, devices, n_col, n):
    return pl.pallas_call(
        functools.partial(near_kernel, cells, devices, n_col),
        out_shape=(jax.ShapeDtypeStruct((3, n), F32),) * 3,
        in_specs=[pl.BlockSpec(memory_space=pltpu.SMEM)]
        + vmem(1)
        + [pl.BlockSpec(memory_space=pl.ANY)] * 2
        + vmem(4),
        out_specs=tuple(vmem(3)),
        scratch_shapes=[
            pltpu.VMEM((3 * cells * NEAR_S, CELL), F32),
            pltpu.VMEM((cells * NEAR_S, CELL), F32),
            pltpu.VMEM((cells * FAR_S, CELL), F32),
            pltpu.VMEM((cells * COEF_S, CELL), F32),
            pltpu.VMEM((cells * FAR_S, CELL), F32),
            pltpu.VMEM((2 * CELL, CELL), F32),
            pltpu.VMEM((8 * pitch_of(cells), CELL), F32),
            pltpu.VMEM((OUT_K * pitch_of(cells), CELL), F32),
            pltpu.VMEM((3 * pitch_of(cells), CELL), F32),
            pltpu.VMEM((6 * pitch_of(cells), CELL), F32),
            pltpu.VMEM((6 * pitch_of(cells), CELL), F32),
            pltpu.SemaphoreType.DMA((2,)),
        ],
        compiler_params=pltpu.CompilerParams(vmem_limit_bytes=VMEM_LIMIT),
        cost_estimate=pl.CostEstimate(
            flops=30_000_000_000, bytes_accessed=4_000_000, transcendentals=6_600_000
        ),
        name="near_and_let_field",
    )


def body(positions, moments, near_list, far_list, let_rows):
    n = positions.shape[1]
    cells = n // CELL
    n_row, n_col = lax.axis_size("row"), lax.axis_size("col")
    bits = let_rows.shape[1]
    planes, before, after, let_in, centre, top = make_first(cells, n_row, n_col)(
        positions, moments, let_rows
    )
    return make_near(cells, n_row * n_col, n_col, n)(
        near_list.T,
        planes,
        before,
        after,
        centre,
        far_list.T,
        let_in.reshape(bits * 16, CELL),
        top,
    )


def solution(mesh):
    return jax.shard_map(
        body,
        mesh=mesh,
        in_specs=(
            P(None, ("row", "col")),
            P(None, ("row", "col")),
            P(("row", "col"), None),
            P(("row", "col"), None),
            P(("row", "col"), None, None),
        ),
        out_specs=(P(None, ("row", "col")), P(None, ("row", "col")), P(None, ("row", "col"))),
        check_vma=False,
    )
```
